512 devices in a mesh: sec: 4 (over y_lo, core), row: 128 (over z, x, y_hi).
Axes of the slice: x: 4, y: 8 (y_hi: 4, y_lo: 2; y = y_hi * 2 + y_lo), z: 8, core: 2. Of those that a mesh axis runs over, the one named last changes fastest.
Arguments:
- images: bfloat16 [4, 8192, 1088], P('sec', 'row'), may hold values from -12 to 12
- initial: float32 [4, 2, 128, 16], P('sec', None, 'row'), may hold values from -6 to 6
- offsets: int32 [4, 2, 128, 16], P('sec', None, 'row'), may hold values from -4 to 4
- stiffness: float32 [8, 2], replicated, may hold values from 0.1 to 0.8
- plan: int32 [3], replicated, may hold values from 0 to 7
Outputs:
- flow_field: float32 [4, 2, 128, 16], P('sec', None, 'row')
- moving: float32 [4, 2, 128, 16], P('sec', None, 'row')
The draws below stay inside these ranges and needn't reach their ends.
All inputs are finite; a program needn't handle non-finite values.
Results may differ from the reference program's by a relative error of at most 0.0003.
Values may be sent and summed in bfloat16 or wider, within the bound.
No kernel may reach another device: no remote copies, remote signals or barrier semaphores. Data moves between devices by JAX's collectives and lax.ppermute only.
A program may use at most 64 MiB of HBM per device.

```python
import math
import jax
import jax.numpy as jnp
from jax import lax

PATCH = 128
STRIDE = 64
NR = 1
NC = 16
SWEEPS = 3
LEVELS = 8
SECTIONS = 4
NRT = 128
ROWS_IMG = 8192
WIDTH = 1088
N_ROW = 128


def pair_shifts(key):
    return jax.random.randint(jax.random.fold_in(key, 101), (SECTIONS - 1, 2), -3, 4, dtype=jnp.int32)


def draw_offsets(key, part):
    shifts = pair_shifts(key)
    key = jax.random.fold_in(key, 7)
    key_jitter, key_last = jax.random.split(key)
    jitter = jax.random.randint(key_jitter, (SECTIONS - 1, 2, NRT, NC), -1, 2, dtype=jnp.int32)
    last_rows = jax.random.randint(key_last, (1, 2, NRT, NC), -4, 5, dtype=jnp.int32)
    return jnp.concatenate([shifts[:, :, None, None] + jitter, last_rows], axis=0)


def draw_images(key, part):
    shifts = pair_shifts(key)
    key = jax.random.fold_in(key, 3)
    key_coarse, key_detail, key_noise, key_level = jax.random.split(key, 4)
    margin = 3 * SECTIONS
    tall = ROWS_IMG + 2 * margin
    broad = WIDTH + 2 * margin
    coarse = jax.random.truncated_normal(key_coarse, -4.0, 4.0, (tall + 3, broad + 3), jnp.float32)
    detail = jax.random.truncated_normal(key_detail, -4.0, 4.0, (tall, broad), jnp.float32)
    noise = jax.random.truncated_normal(key_noise, -4.0, 4.0, (SECTIONS, ROWS_IMG, WIDTH), jnp.float32)
    across_sum = coarse[:, 0:-3] + coarse[:, 1:-2] + coarse[:, 2:-1] + coarse[:, 3:]
    smooth = across_sum[0:-3] + across_sum[1:-2] + across_sum[2:-1] + across_sum[3:]
    volume = 0.25 * smooth + 0.5 * detail
    cumulative = jnp.concatenate([jnp.zeros((1, 2), jnp.int32), jnp.cumsum(shifts, axis=0).astype(jnp.int32)], axis=0)
    layers = []
    for section in range(SECTIONS):
        start_row = (margin - cumulative[section, 0]).astype(jnp.int32)
        start_col = (margin - cumulative[section, 1]).astype(jnp.int32)
        layers.append(lax.dynamic_slice(volume, (start_row, start_col), (ROWS_IMG, WIDTH)))
    clean = jnp.stack(layers)
    level_draw = jax.random.uniform(key_level, (SECTIONS, ROWS_IMG // STRIDE, 1, WIDTH // STRIDE, 1), jnp.float32, math.log(0.15), math.log(1.5))
    noise_gain = jnp.broadcast_to(jnp.exp(level_draw), (SECTIONS, ROWS_IMG // STRIDE, STRIDE, WIDTH // STRIDE, STRIDE)).reshape(SECTIONS, ROWS_IMG, WIDTH)
    return jnp.clip(clean + noise_gain * noise, -12.0, 12.0).astype(jnp.bfloat16)


def block_scale(stream_key, shape, shards, smallest, high):
    def one(axis_at, parts):
        draws = jax.random.uniform(jax.random.fold_in(jax.random.fold_in(stream_key, 6), axis_at), (parts,), jnp.float32, smallest / len(shards), high / len(shards))
        return jnp.repeat(jnp.exp(draws), shape[axis_at] // parts).reshape((-1,) + (1,) * (len(shape) - axis_at - 1))

    loudness = one(*shards[0])
    for cut in shards[1:]:
        loudness = loudness * one(*cut)
    return loudness


def bell_draw(stream_key, shape, width, reach, shards=(), kind=jnp.bfloat16):
    entries = jax.random.normal(stream_key, shape, jnp.float32) * width
    if len(shards) > 0:
        entries = block_scale(stream_key, shape, shards, -0.22, 0.18) * entries
    return jnp.clip(entries, min=-reach, max=reach).astype(kind)


def setup_inputs(seed: int = 0) -> dict:
    splits = jax.random.split(jax.random.key(seed), 6)
    images = draw_images(jax.random.fold_in(splits[5], 71), 0)
    initial = bell_draw(splits[1], (SECTIONS, 2, NRT, NC), 1.0, 6.0, ((0, 4), (2, 128)), jnp.float32)
    offsets = draw_offsets(jax.random.fold_in(splits[5], 71), 0)
    stiffness = jnp.clip(jnp.exp(jax.random.uniform(splits[3], (LEVELS, 2), jnp.float32, math.log(0.1), math.log(0.8))), 0.1, 0.8)
    plan = jax.random.randint(splits[4], (SWEEPS,), 0, LEVELS).astype(jnp.int32)
    return {"images": images, "initial": initial, "offsets": offsets, "stiffness": stiffness, "plan": plan}


step_size = 0.2
floor_ratio = 0.2

def dft_tables(length):
    freq = jnp.arange(length, dtype=jnp.int32)
    phase = freq[:, None] * freq[None, :] % length
    folded = jnp.minimum(phase, length - phase)
    angle = folded.astype(jnp.float32) * (2.0 * math.pi / length)
    upper = (phase * 2 > length).astype(jnp.float32)
    middle = (folded * 2 == length).astype(jnp.float32)
    sine = jnp.sin(angle) * (1.0 - 2.0 * upper) * (1.0 - middle)
    return jnp.concatenate([jnp.cos(angle), -sine], axis=0).astype(jnp.bfloat16)

def cut_patches(extended, height, across, stride, length):
    blocks_per = length // stride
    tiling = extended.reshape(height + blocks_per - 1, stride, across + blocks_per - 1, stride)
    pieces = [tiling[i:i + height, :, j:j + across, :] for i in range(blocks_per) for j in range(blocks_per)]
    stacked = jnp.stack(pieces).reshape(blocks_per, blocks_per, height, stride, across, stride)
    return stacked.transpose(2, 4, 0, 3, 1, 5).reshape(height * across, length, length)

def spectra(patches, tables):
    length = patches.shape[-1]
    number = patches.shape[0]
    segmented = jnp.dot(patches.reshape(number * length, length), tables.T, preferred_element_type=jnp.float32)
    segmented = segmented.reshape(number, length, 2 * length).astype(jnp.bfloat16)
    product = jnp.einsum('ky,nyl->nkl', tables.astype(jnp.float32), segmented.astype(jnp.float32))
    real_part = product[:, :length, :length] - product[:, length:, length:]
    imag_part = product[:, :length, length:] + product[:, length:, :length]
    return jnp.concatenate([real_part, imag_part], axis=-1).astype(jnp.bfloat16)

def spectrum_norms(spec):
    length = spec.shape[1]
    energy = lax.optimization_barrier(jnp.sum(jnp.square(spec.astype(jnp.float32)), axis=(1, 2)))
    return jnp.sqrt(energy / (length * length) + 1e-06)

def correlate(spec_lower, spec_upper, norm_lower, norm_upper, shift_y, shift_x):
    length = spec_lower.shape[1]
    lower_f = spec_lower.astype(jnp.float32)
    upper_f = spec_upper.astype(jnp.float32)
    low_re = lower_f[..., :length]
    low_im = lower_f[..., length:]
    up_re = upper_f[..., :length]
    up_im = upper_f[..., length:]
    cross_re = low_re * up_re + low_im * up_im
    cross_im = low_re * up_im - low_im * up_re
    modulus = jnp.sqrt(cross_re * cross_re + cross_im * cross_im)
    divisor = modulus + (floor_ratio * norm_lower * norm_upper)[:, None, None]
    white_re = cross_re / divisor
    white_im = cross_im / divisor
    freq = jnp.arange(length, dtype=jnp.int32)
    beside_all = jnp.arange(3, dtype=jnp.int32) - 1

    def twiddle(shift):
        lagged = shift[:, None] + beside_all[None, :]
        phase = freq[None, :, None] * lagged[:, None, :] % length
        angle = phase.astype(jnp.float32) * (2.0 * math.pi / length)
        return (jnp.cos(angle), jnp.sin(angle))
    cos_x, sin_x = twiddle(shift_x)
    cos_y, sin_y = twiddle(shift_y)
    highest = lax.Precision.HIGHEST
    part_re = jnp.einsum('nkl,nli->nki', white_re, cos_x, precision=highest) - jnp.einsum('nkl,nli->nki', white_im, sin_x, precision=highest)
    part_im = jnp.einsum('nkl,nli->nki', white_re, sin_x, precision=highest) + jnp.einsum('nkl,nli->nki', white_im, cos_x, precision=highest)
    values = jnp.einsum('nkj,nki->nji', cos_y, part_re, precision=highest) - jnp.einsum('nkj,nki->nji', sin_y, part_im, precision=highest)
    values = values / (length * length)
    grad_y = 0.5 * (values[:, 2, 1] - values[:, 0, 1])
    curve_y = 2.0 * values[:, 1, 1] - values[:, 0, 1] - values[:, 2, 1]
    grad_x = 0.5 * (values[:, 1, 2] - values[:, 1, 0])
    curve_x = 2.0 * values[:, 1, 1] - values[:, 1, 0] - values[:, 1, 2]
    flow_y = shift_y.astype(jnp.float32) + grad_y / (1.0 + jnp.abs(curve_y))
    flow_x = shift_x.astype(jnp.float32) + grad_x / (1.0 + jnp.abs(curve_x))
    return (flow_y, flow_x)

def reference(images, initial, offsets, stiffness, plan):
    tail = PATCH - STRIDE
    padded = jnp.pad(images, ((0, 0), (0, tail), (0, 0)))
    tables = dft_tables(PATCH)
    per_block = NR * NC

    def block(block_no):
        begin = block_no.astype(jnp.int32) * (NR * STRIDE)
        extended = lax.dynamic_slice(padded, (jnp.int32(0), begin, jnp.int32(0)), (SECTIONS, NR * STRIDE + tail, WIDTH))
        block_offsets = lax.dynamic_slice_in_dim(offsets, block_no.astype(jnp.int32) * NR, NR, 2)
        patches = jnp.concatenate([cut_patches(extended[s], NR, NC, STRIDE, PATCH) for s in range(SECTIONS)], axis=0)
        spec_flat = spectra(patches, tables)
        norms = spectrum_norms(spec_flat).reshape(SECTIONS, per_block)
        spec = spec_flat.reshape(SECTIONS, per_block, PATCH, 2 * PATCH)
        pairs = (SECTIONS - 1) * per_block
        flow_y, flow_x = correlate(spec[:-1].reshape(pairs, PATCH, 2 * PATCH), spec[1:].reshape(pairs, PATCH, 2 * PATCH), norms[:-1].reshape(pairs), norms[1:].reshape(pairs), block_offsets[:-1, 0].reshape(pairs), block_offsets[:-1, 1].reshape(pairs))
        flow_pairs = jnp.stack([flow_y.reshape(SECTIONS - 1, NR, NC), flow_x.reshape(SECTIONS - 1, NR, NC)], axis=1)
        return jnp.concatenate([flow_pairs, jnp.zeros((1, 2, NR, NC), jnp.float32)], axis=0)
    blocks = lax.map(block, jnp.arange(N_ROW, dtype=jnp.int32))
    flow_field = blocks.transpose(1, 2, 0, 3, 4).reshape(SECTIONS, 2, NRT, NC)
    row_ids = jnp.arange(NRT, dtype=jnp.int32)
    col_ids = jnp.arange(NC, dtype=jnp.int32)
    has_up = (row_ids > 0).astype(jnp.float32)[:, None]
    has_down = (row_ids < NRT - 1).astype(jnp.float32)[:, None]
    has_left = (col_ids > 0).astype(jnp.float32)[None, :]
    has_right = (col_ids < NC - 1).astype(jnp.float32)[None, :]
    sec_ids = jnp.arange(SECTIONS, dtype=jnp.int32)
    valid_up = (sec_ids < SECTIONS - 1).astype(jnp.float32)[:, None, None, None]
    moving = initial
    for sweep_no in range(SWEEPS):
        picked = plan[sweep_no]
        spring = stiffness[picked, 0]
        tether = stiffness[picked, 1]
        row_above = jnp.pad(moving[:, :, :-1], ((0, 0), (0, 0), (1, 0), (0, 0)))
        row_below = jnp.pad(moving[:, :, 1:], ((0, 0), (0, 0), (0, 1), (0, 0)))
        col_left = jnp.pad(moving[..., :-1], ((0, 0), (0, 0), (0, 0), (1, 0)))
        col_right = jnp.pad(moving[..., 1:], ((0, 0), (0, 0), (0, 0), (0, 1)))
        laplace = (row_above - moving) * has_up + (row_below - moving) * has_down + (col_left - moving) * has_left + (col_right - moving) * has_right
        above_sec = jnp.pad(moving[1:], ((0, 1), (0, 0), (0, 0), (0, 0)))
        residual = (above_sec - moving - flow_field) * valid_up
        below_res = jnp.pad(residual[:-1], ((1, 0), (0, 0), (0, 0), (0, 0)))
        moving = moving + step_size * (spring * laplace + tether * (residual - below_res))
    return (flow_field, moving)
```

```python
import math

import numpy as np
import jax
import jax.numpy as jnp
from jax import lax
from jax.experimental import pallas as pl
from jax.experimental.pallas import tpu as pltpu
from jax.sharding import PartitionSpec as P
import ml_dtypes

PATCH = 128
STRIDE = 64
HALF = 64
SWEEPS = 3
COLS = 16
PAIRS = 8
SECS = 4
RING = 4
SHIFTS = 16
REACH = 5
WIDTH = 1088
PADDED = 1152

step_size = 0.2
floor_ratio = 0.2

f32 = jnp.float32
bf16 = jnp.bfloat16


def dft_halves():
    freq = np.arange(PATCH)
    phase = freq[:, None] * freq[None, :] % PATCH
    folded = np.minimum(phase, PATCH - phase)
    angle = folded * (2.0 * math.pi / PATCH)
    sine = np.sin(angle) * np.where(2 * phase > PATCH, -1.0, 1.0)
    sine = np.where(2 * folded == PATCH, 0.0, sine)
    cosine = np.cos(angle)
    cosine = np.where(4 * folded == PATCH, np.cos(np.float32(math.pi / 2)), cosine)
    return cosine.astype(ml_dtypes.bfloat16), (-sine).astype(ml_dtypes.bfloat16)


def two_parts(table):
    high = table.astype(ml_dtypes.bfloat16)
    low = (table - high.astype(np.float64)).astype(ml_dtypes.bfloat16)
    return high, low


def constant_tables():
    cos_t, sin_t = dft_halves()
    cos_f = cos_t.astype(np.float32)
    sin_f = sin_t.astype(np.float32)
    rows = np.zeros((2 * PATCH, 2 * PATCH), np.float32)
    rows[0:PATCH, 0:HALF] = cos_f[:HALF].T
    rows[0:PATCH, PATCH : PATCH + HALF] = sin_f[:HALF].T
    rows[HALF : HALF + PATCH, HALF:PATCH] = cos_f[:HALF].T
    rows[HALF : HALF + PATCH, PATCH + HALF :] = sin_f[:HALF].T
    nyquist = np.zeros((PADDED, PATCH), np.float32)
    for c in range(COLS):
        nyquist[c * STRIDE : c * STRIDE + PATCH, c] = cos_f[HALF]
    columns = np.block([[cos_f, -sin_f], [sin_f, cos_f]])
    lags = np.arange(SHIFTS) - REACH
    used = (np.arange(SHIFTS) <= 2 * REACH).astype(np.float64)
    freq = np.arange(PATCH)
    turn = (freq[None, :] * lags[:, None] % PATCH) * (2.0 * math.pi / PATCH)
    cos_y = np.cos(turn) * used[:, None]
    sin_y = np.sin(turn) * used[:, None]
    high, low = two_parts(np.block([[cos_y, -sin_y], [sin_y, cos_y]]))
    lag_y = np.concatenate([high, low], axis=0)
    weight = np.where(freq[:HALF] == 0, 1.0, 2.0)
    across = np.zeros((3 * PATCH, PATCH))
    for p in range(2):
        cols = slice(p * HALF, p * HALF + SHIFTS)
        block = slice(p * HALF, (p + 1) * HALF)
        across[:PATCH][block, cols] = (cos_y[:, :HALF] * weight).T
        across[PATCH : 2 * PATCH][block, cols] = (-sin_y[:, :HALF] * weight).T
        for c in range(p, COLS, 2):
            across[2 * PATCH + c, cols] = np.where(lags % 2 == 0, 1.0, -1.0) * used
    high, low = two_parts(across)
    lag_x = np.concatenate([high, low], axis=1)
    lane = np.arange(PATCH)
    patch = (lane % COLS % 2)[None, :] == (lane // HALF)[:, None]
    gather = (patch & (lane < 2 * COLS)[None, :]).astype(np.float32)
    single = (patch & (lane < COLS)[None, :]).astype(np.float32)
    same = ((lane // HALF)[:, None] == (lane // HALF)[None, :]).astype(np.float32)
    blank = np.zeros((PATCH, PATCH), np.float32)
    spread = np.block([[same, gather], [single.T, blank]])
    as_bf16 = lambda t: np.asarray(t).astype(ml_dtypes.bfloat16)
    return [as_bf16(t) for t in (rows, nyquist, columns, lag_y, lag_x, spread)]


def three_parts(x):
    high = x.astype(bf16)
    rest = x - high.astype(f32)
    mid = rest.astype(bf16)
    low = (rest - mid.astype(f32)).astype(bf16)
    return jnp.concatenate([high, mid, low], axis=0)


def dot(a, b):
    return jnp.dot(a, b, preferred_element_type=f32)


def flow_kernel(
    own, below, near, near_below, record, rows_t, nyq_t, cols_t, lag_y, lag_x, spread_t, out, image, spec, lagged
):
    for i, ref in enumerate((own, below, near, near_below)):
        image[pl.ds(i * HALF, HALF), pl.ds(0, WIDTH)] = ref[0]
    image[:, pl.ds(WIDTH, PADDED - WIDTH)] = jnp.zeros((4 * HALF, PADDED - WIDTH), bf16)

    def finish_spectrum(m, stacked, table):
        product = dot(table, stacked).astype(bf16)
        spec[m] = product
        wide = product.astype(f32)
        return jnp.sum(wide * wide, axis=0, keepdims=True)

    energies = []
    for m in range(PAIRS):
        seg = dot(image[:, pl.ds(m * PATCH, 2 * PATCH)], rows_t[...]).astype(bf16)
        stacked = jnp.concatenate(
            [
                jnp.concatenate([seg[:PATCH, :PATCH], seg[PATCH:, :PATCH]], axis=1),
                jnp.concatenate([seg[:PATCH, PATCH:], seg[PATCH:, PATCH:]], axis=1),
            ],
            axis=0,
        )
        energies.append(finish_spectrum(m, stacked, cols_t[...]))
    seg = dot(image[...], nyq_t[...]).astype(bf16)
    stacked = jnp.concatenate([seg[:PATCH], seg[PATCH:]], axis=1)
    energy_64 = finish_spectrum(PAIRS, stacked, cols_t[:, pl.ds(0, PATCH)])

    lane = lax.broadcasted_iota(jnp.int32, (PAIRS, PATCH), 1)
    pair = lax.broadcasted_iota(jnp.int32, (PAIRS, PATCH), 0)
    own_pair = (lane % COLS) // 2 == pair
    first_16 = own_pair & (lane < COLS)
    weight = jnp.where(lane % HALF == 0, 1.0, 2.0)
    energy = jnp.concatenate(energies, axis=0)

    def halves(x):
        return x[:, :PATCH], x[:, PATCH:]

    def totals(main, extra):
        left = jnp.concatenate([main * weight, jnp.where(first_16, extra, 0.0)], axis=1)
        found = dot(three_parts(left), spread_t[...])
        found = found[:PAIRS] + found[PAIRS : 2 * PAIRS] + found[2 * PAIRS :]
        by_pair, by_patch = halves(found)
        by_patch = jnp.sum(jnp.where(first_16, by_patch, 0.0), axis=0, keepdims=True) + extra
        scale = 1.0 / (PATCH * PATCH)
        return jnp.sqrt(by_pair * scale + 1e-06), jnp.sqrt(by_patch * scale + 1e-06)

    low_e, up_e = halves(energy)
    low_x, up_x = halves(energy_64)
    low_pair, low_patch = totals(low_e, low_x)
    up_pair, up_patch = totals(up_e, up_x)
    floor_pair = floor_ratio * low_pair * up_pair
    floor_patch = floor_ratio * low_patch * up_patch

    for m in range(PAIRS + 1):
        floor = floor_pair[m : m + 1] if m < PAIRS else floor_patch
        low_re = spec[m, pl.ds(0, PATCH), pl.ds(0, PATCH)].astype(f32)
        low_im = spec[m, pl.ds(PATCH, PATCH), pl.ds(0, PATCH)].astype(f32)
        up_re = spec[m, pl.ds(0, PATCH), pl.ds(PATCH, PATCH)].astype(f32)
        up_im = spec[m, pl.ds(PATCH, PATCH), pl.ds(PATCH, PATCH)].astype(f32)
        cross_re = low_re * up_re + low_im * up_im
        cross_im = low_re * up_im - low_im * up_re
        square = cross_re * cross_re + cross_im * cross_im
        modulus = square * lax.rsqrt(jnp.maximum(square, 1e-36))
        inverse = 1.0 / (modulus + floor)
        white = jnp.concatenate([cross_re * inverse, cross_im * inverse], axis=0)
        high = white.astype(bf16)
        low = (white - high.astype(f32)).astype(bf16)
        found = dot(lag_y[...], jnp.concatenate([high, low], axis=1))
        part = found[: 2 * SHIFTS, :PATCH] + found[: 2 * SHIFTS, PATCH:] + found[2 * SHIFTS :, :PATCH]
        lagged[pl.ds(m * SHIFTS, SHIFTS), pl.ds(0, PATCH)] = part[:SHIFTS]
        lagged[pl.ds(m * SHIFTS, SHIFTS), pl.ds(PATCH, PATCH)] = part[SHIFTS:]

    extra = lagged[pl.ds(PAIRS * SHIFTS, SHIFTS), pl.ds(0, PATCH)]
    extra = jnp.where(first_16[:, None, :], extra[None], 0.0).reshape(PAIRS * SHIFTS, PATCH)
    left = jnp.concatenate([lagged[pl.ds(0, PAIRS * SHIFTS), :], extra], axis=1)
    high = left.astype(bf16)
    low = (left - high.astype(f32)).astype(bf16)
    rows_all = PAIRS * SHIFTS
    found = dot(jnp.concatenate([high, low], axis=0), lag_x[...])
    surface = found[:rows_all, :PATCH] + found[:rows_all, PATCH:] + found[rows_all:, :PATCH]
    surface = surface.reshape(PAIRS, SHIFTS, PATCH)

    rec = record[...]
    at_y = jnp.where(first_16, rec, 0.0)
    at_x = jnp.where(own_pair & (lane >= COLS) & (lane < 2 * COLS), rec, 0.0)
    gather = spread_t[pl.ds(0, PATCH), pl.ds(PATCH, PATCH)]
    shifts = lax.dot_general(
        jnp.concatenate([at_y, at_x], axis=0).astype(bf16),
        gather,
        (((1,), (1,)), ((), ())),
        preferred_element_type=f32,
    )
    lag_row = lax.broadcasted_iota(jnp.int32, (PAIRS, SHIFTS, PATCH), 1).astype(f32) - REACH
    lag_col = (lax.broadcasted_iota(jnp.int32, (PAIRS, SHIFTS, PATCH), 2) % HALF).astype(f32) - REACH
    dy = lag_row - shifts[:PAIRS][:, None, :]
    dx = lag_col - shifts[PAIRS:][:, None, :]
    mid_y, up_y, down_y = ((dy == k).astype(f32) for k in (0.0, 1.0, -1.0))
    mid_x, up_x, down_x = ((dx == k).astype(f32) for k in (0.0, 1.0, -1.0))
    at_mid_x = surface * mid_x
    at_mid_y = surface * mid_y
    picks = [
        jnp.sum(at_mid_x * (up_y - down_y), axis=1),
        jnp.sum(at_mid_x * (2.0 * mid_y - up_y - down_y), axis=1),
        jnp.sum(at_mid_y * (up_x - down_x), axis=1),
        jnp.sum(at_mid_y * (2.0 * mid_x - up_x - down_x), axis=1),
    ]
    found = dot(three_parts(jnp.concatenate(picks, axis=0)), gather)
    found = found[: 4 * PAIRS] + found[4 * PAIRS : 8 * PAIRS] + found[8 * PAIRS :]
    found = found.reshape(4, PAIRS, PATCH)
    found = jnp.sum(jnp.where(own_pair[None], found, 0.0), axis=1) * (1.0 / (PATCH * PATCH))
    lane_1 = lax.broadcasted_iota(jnp.int32, (1, PATCH), 1)
    slope = jnp.where(lane_1 < COLS, found[0:1], found[2:3])
    bend = jnp.where(lane_1 < COLS, found[1:2], found[3:4])
    flow = rec + 0.5 * slope / (1.0 + jnp.abs(bend))
    result = jnp.where(lane_1 < 2 * COLS, flow, rec)
    out[...] = jnp.broadcast_to(result[None], out.shape)


def vmem_spec():
    return pl.BlockSpec(memory_space=pltpu.VMEM)


def pair_flow(own, below, near, near_below, record, copies):
    tables = [jnp.asarray(t) for t in constant_tables()]
    return pl.pallas_call(
        flow_kernel,
        out_shape=jax.ShapeDtypeStruct((copies, 1, PATCH), f32),
        in_specs=[vmem_spec()] * (5 + len(tables)),
        out_specs=vmem_spec(),
        scratch_shapes=[
            pltpu.VMEM((4 * HALF, PADDED), bf16),
            pltpu.VMEM((PAIRS + 1, 2 * PATCH, 2 * PATCH), bf16),
            pltpu.VMEM(((PAIRS + 1) * SHIFTS, 2 * PATCH), f32),
        ],
        compiler_params=pltpu.CompilerParams(vmem_limit_bytes=32 * 1024 * 1024),
    )(own, below, near, near_below, record, *tables)


def relax_kernel(place, stiffness, plan, mid, before, after, flow_out, moving_out):
    sec = place[0]
    row = place[1]
    base = row - lax.rem(row, RING)
    count = SECS * RING
    node = lax.broadcasted_iota(jnp.int32, (count, PATCH), 0)
    lane = lax.broadcasted_iota(jnp.int32, (count, PATCH), 1)
    in_ring = node % RING
    section = node // RING
    blocks = [ref[...].reshape(count, PATCH) for ref in (before, mid, after)]
    valid = (section < SECS - 1) & (lane < 2 * COLS)
    flows = [jnp.where(valid, b, 0.0) for b in blocks]
    moving = [pltpu.roll(b, PATCH - 2 * COLS, 1) for b in blocks]
    valid_up = valid.astype(f32)
    has_left = (lane % COLS > 0).astype(f32)
    has_right = (lane % COLS < COLS - 1).astype(f32)
    rows = [base + in_ring + RING * (k - 1) for k in range(3)]
    has_up = [(r > 0).astype(f32) for r in rows]
    has_down = [(r < 127).astype(f32) for r in rows]

    def moved(x, by):
        by = by % count
        return jnp.concatenate([x[by:], x[:by]], axis=0) if by else x

    for sweep in range(SWEEPS):
        level = plan[sweep]
        spring = stiffness[level, 0]
        tether = stiffness[level, 1]
        fresh = []
        for k in range(3):
            x = moving[k]
            above = moving[k - 1] if k > 0 else x
            below = moving[k + 1] if k < 2 else x
            row_above = jnp.where(in_ring == 0, moved(above, RING - 1), moved(x, -1))
            row_below = jnp.where(in_ring == RING - 1, moved(below, 1 - RING), moved(x, 1))
            col_left = pltpu.roll(x, 1, 1)
            col_right = pltpu.roll(x, PATCH - 1, 1)
            laplace = (
                (row_above - x) * has_up[k]
                + (row_below - x) * has_down[k]
                + (col_left - x) * has_left
                + (col_right - x) * has_right
            )
            residual = (moved(x, RING) - x - flows[k]) * valid_up
            below_res = jnp.where(section == 0, 0.0, moved(residual, -RING))
            fresh.append(x + step_size * (spring * laplace + tether * (residual - below_res)))
        moving = fresh

    mine = (section == sec) & (in_ring == lax.rem(row, RING))
    for x, ref in ((flows[1], flow_out), (moving[1], moving_out)):
        line = jnp.sum(jnp.where(mine, x, 0.0), axis=0, keepdims=True)
        ref[0, 0] = line[:, :COLS]
        ref[0, 1] = line[:, COLS : 2 * COLS]


def relax(place, stiffness, plan, mid, before, after, shape):
    smem = pl.BlockSpec(memory_space=pltpu.SMEM)
    return pl.pallas_call(
        relax_kernel,
        out_shape=[jax.ShapeDtypeStruct(shape, f32)] * 2,
        in_specs=[smem] * 3 + [vmem_spec()] * 3,
        out_specs=[vmem_spec()] * 2,
    )(place, stiffness, plan, mid, before, after)


def shifted(block, axis, distance):
    devices = range(lax.axis_size(axis))
    route = [(i - distance, i) for i in devices if i - distance in devices]
    return lax.ppermute(block, axis, route)


def per_device(images, initial, offsets, stiffness, plan):
    rows = lax.axis_size("row")
    near = shifted(images, "sec", -1)
    below = shifted(images, "row", -1)
    near_below = shifted(below, "sec", -1)
    record = jnp.concatenate(
        [offsets.astype(f32).reshape(1, 2 * COLS), initial.reshape(1, 2 * COLS), jnp.zeros((1, 64), f32)], axis=1
    )
    mine = pair_flow(images, below, near, near_below, record, SECS * RING)
    groups = [
        [s * rows + RING * g + j for s in range(SECS) for j in range(RING)] for g in range(rows // RING)
    ]
    ring = lax.all_to_all(mine, ("sec", "row"), 0, 0, axis_index_groups=groups)
    before = shifted(ring, "row", RING)
    after = shifted(ring, "row", -RING)
    place = jnp.stack([lax.axis_index("sec"), lax.axis_index("row")]).astype(jnp.int32)
    return tuple(relax(place, stiffness, plan, ring, before, after, initial.shape))


def solution(mesh):
    return jax.shard_map(
        per_device,
        mesh=mesh,
        in_specs=(
            P("sec", "row", None),
            P("sec", None, "row", None),
            P("sec", None, "row", None),
            P(),
            P(),
        ),
        out_specs=(P("sec", None, "row", None), P("sec", None, "row", None)),
        check_vma=False,
    )
```

```python
import math

import numpy as np
import jax
import jax.numpy as jnp
from jax import lax
from jax.experimental import pallas as pl
from jax.experimental.pallas import tpu as pltpu
from jax.sharding import PartitionSpec as P
import ml_dtypes

PATCH = 128
STRIDE = 64
HALF = 64
SWEEPS = 3
COLS = 16
PAIRS = 8
SECS = 4
RING = 4
SHIFTS = 16
REACH = 5
WIDTH = 1088
VMEM_LIMIT = 48 * 1024 * 1024

step_size = 0.2
floor_ratio = 0.2

f32 = jnp.float32
bf16 = jnp.bfloat16


def dft_halves():
    freq = np.arange(PATCH)
    phase = freq[:, None] * freq[None, :] % PATCH
    folded = np.minimum(phase, PATCH - phase)
    angle = folded * (2.0 * math.pi / PATCH)
    sine = np.sin(angle) * np.where(2 * phase > PATCH, -1.0, 1.0)
    sine = np.where(2 * folded == PATCH, 0.0, sine)
    cosine = np.cos(angle)
    cosine = np.where(4 * folded == PATCH, np.cos(np.float32(math.pi / 2)), cosine)
    return cosine.astype(ml_dtypes.bfloat16), (-sine).astype(ml_dtypes.bfloat16)


def two_parts(table):
    high = table.astype(ml_dtypes.bfloat16)
    low = (table - high.astype(np.float64)).astype(ml_dtypes.bfloat16)
    return high, low


def constant_tables():
    cos_t, sin_t = dft_halves()
    cos_f = cos_t.astype(np.float32)
    sin_f = sin_t.astype(np.float32)
    rows = np.zeros((2 * PATCH, 2 * PATCH), np.float32)
    rows[0:PATCH, 0:HALF] = cos_f[:HALF].T
    rows[0:PATCH, PATCH : PATCH + HALF] = sin_f[:HALF].T
    rows[HALF : HALF + PATCH, HALF:PATCH] = cos_f[:HALF].T
    rows[HALF : HALF + PATCH, PATCH + HALF :] = sin_f[:HALF].T
    nyquist = np.zeros((2 * PATCH, PATCH), np.float32)
    nyquist[0:PATCH, 0::2] = cos_f[HALF][:, None]
    nyquist[HALF : HALF + PATCH, 1::2] = cos_f[HALF][:, None]
    rows = np.concatenate([rows, nyquist], axis=1)
    columns = np.block([[cos_f, -sin_f], [sin_f, cos_f]])
    lags = np.arange(SHIFTS) - REACH
    used = (np.arange(SHIFTS) <= 2 * REACH).astype(np.float64)
    freq = np.arange(PATCH)
    turn = (freq[None, :] * lags[:, None] % PATCH) * (2.0 * math.pi / PATCH)
    cos_y = np.cos(turn) * used[:, None]
    sin_y = np.sin(turn) * used[:, None]
    high, low = two_parts(np.block([[cos_y, -sin_y], [sin_y, cos_y]]))
    lag_y = np.concatenate([high, low], axis=0)
    weight = np.where(freq[:HALF] == 0, 1.0, 2.0)
    across = np.zeros((3 * PATCH, PATCH))
    for p in range(2):
        cols = slice(p * HALF, p * HALF + SHIFTS)
        block = slice(p * HALF, (p + 1) * HALF)
        across[:PATCH][block, cols] = (cos_y[:, :HALF] * weight).T
        across[PATCH : 2 * PATCH][block, cols] = (-sin_y[:, :HALF] * weight).T
        for c in range(p, COLS, 2):
            across[2 * PATCH + c, cols] = np.where(lags % 2 == 0, 1.0, -1.0) * used
    high, low = two_parts(across)
    lag_x = np.concatenate([high, low], axis=1)
    lane = np.arange(PATCH)
    patch = (lane % COLS % 2)[None, :] == (lane // HALF)[:, None]
    gather = (patch & (lane < 2 * COLS)[None, :]).astype(np.float32)
    single = (patch & (lane < COLS)[None, :]).astype(np.float32)
    same = ((lane // HALF)[:, None] == (lane // HALF)[None, :]).astype(np.float32)
    blank = np.zeros((PATCH, PATCH), np.float32)
    spread = np.block([[same, gather], [single.T, blank]])
    as_bf16 = lambda t: np.asarray(t).astype(ml_dtypes.bfloat16)
    return [as_bf16(t) for t in (rows, columns, lag_y, lag_x, spread)]


def three_parts(x):
    high = x.astype(bf16)
    rest = x - high.astype(f32)
    mid = rest.astype(bf16)
    low = (rest - mid.astype(f32)).astype(bf16)
    return jnp.concatenate([high, mid, low], axis=0)


def dot(a, b):
    return jnp.dot(a, b, preferred_element_type=f32)


def flow_kernel(
    own,
    below,
    near,
    near_below,
    offsets,
    initial,
    remote_initial,
    rows_h,
    cols_h,
    lag_y_h,
    lag_x_h,
    spread_h,
    out,
    image,
    rows_t,
    cols_t,
    lag_y,
    lag_x,
    spread_t,
    shift_in,
    node_in,
    record,
    spec,
    lagged,
    sems,
):
    moves = [(ref.at[0], image.at[pl.ds(i * HALF, HALF)]) for i, ref in enumerate((own, below, near, near_below))]
    moves += [(rows_h, rows_t), (cols_h, cols_t)]
    moves += [(offsets.at[0], shift_in), (initial.at[0], node_in.at[0]), (remote_initial.at[0], node_in.at[1])]
    moves += [(spread_h, spread_t), (lag_y_h, lag_y), (lag_x_h, lag_x)]
    copies = [pltpu.make_async_copy(src, dst, sems.at[i]) for i, (src, dst) in enumerate(moves)]
    for copy in copies:
        copy.start()
    for copy in copies[:6]:
        copy.wait()

    def finish_spectrum(m, stacked, table):
        product = dot(table, stacked).astype(bf16)
        spec[m] = product
        wide = product.astype(f32)
        return jnp.sum(wide * wide, axis=0, keepdims=True)

    energies = []
    lane_4 = lax.broadcasted_iota(jnp.int32, (4 * HALF, PATCH), 1)
    nyquist = jnp.zeros((4 * HALF, PATCH), f32)
    for m in range(PAIRS):
        span = 2 * PATCH if m < PAIRS - 1 else WIDTH - m * PATCH
        seg = dot(image[:, pl.ds(m * PATCH, span)], rows_t[pl.ds(0, span), :])
        nyquist = jnp.where(lane_4 // 2 == m, seg[:, 2 * PATCH :], nyquist)
        seg = seg[:, : 2 * PATCH].astype(bf16)
        stacked = jnp.concatenate(
            [
                jnp.concatenate([seg[:PATCH, :PATCH], seg[PATCH:, :PATCH]], axis=1),
                jnp.concatenate([seg[:PATCH, PATCH:], seg[PATCH:, PATCH:]], axis=1),
            ],
            axis=0,
        )
        energies.append(finish_spectrum(m, stacked, cols_t[...]))
    seg = nyquist.astype(bf16)
    stacked = jnp.concatenate([seg[:PATCH], seg[PATCH:]], axis=1)
    energy_64 = finish_spectrum(PAIRS, stacked, cols_t[:, pl.ds(0, PATCH)])
    for copy in copies[6:]:
        copy.wait()

    lane = lax.broadcasted_iota(jnp.int32, (PAIRS, PATCH), 1)
    pair = lax.broadcasted_iota(jnp.int32, (PAIRS, PATCH), 0)
    own_pair = (lane % COLS) // 2 == pair
    first_16 = own_pair & (lane < COLS)
    weight = jnp.where(lane % HALF == 0, 1.0, 2.0)
    energy = jnp.concatenate(energies, axis=0)

    def halves(x):
        return x[:, :PATCH], x[:, PATCH:]

    def totals(main, extra):
        left = jnp.concatenate([main * weight, jnp.where(first_16, extra, 0.0)], axis=1)
        found = dot(three_parts(left), spread_t[...])
        found = found[:PAIRS] + found[PAIRS : 2 * PAIRS] + found[2 * PAIRS :]
        by_pair, by_patch = halves(found)
        by_patch = jnp.sum(jnp.where(first_16, by_patch, 0.0), axis=0, keepdims=True) + extra
        scale = 1.0 / (PATCH * PATCH)
        return jnp.sqrt(by_pair * scale + 1e-06), jnp.sqrt(by_patch * scale + 1e-06)

    low_e, up_e = halves(energy)
    low_x, up_x = halves(energy_64)
    low_pair, low_patch = totals(low_e, low_x)
    up_pair, up_patch = totals(up_e, up_x)
    floor_pair = floor_ratio * low_pair * up_pair
    floor_patch = floor_ratio * low_patch * up_patch

    for m in range(PAIRS + 1):
        floor = floor_pair[m : m + 1] if m < PAIRS else floor_patch
        low_re = spec[m, pl.ds(0, PATCH), pl.ds(0, PATCH)].astype(f32)
        low_im = spec[m, pl.ds(PATCH, PATCH), pl.ds(0, PATCH)].astype(f32)
        up_re = spec[m, pl.ds(0, PATCH), pl.ds(PATCH, PATCH)].astype(f32)
        up_im = spec[m, pl.ds(PATCH, PATCH), pl.ds(PATCH, PATCH)].astype(f32)
        cross_re = low_re * up_re + low_im * up_im
        cross_im = low_re * up_im - low_im * up_re
        square = cross_re * cross_re + cross_im * cross_im
        modulus = square * lax.rsqrt(jnp.maximum(square, 1e-36))
        inverse = 1.0 / (modulus + floor)
        white = jnp.concatenate([cross_re * inverse, cross_im * inverse], axis=0)
        high = white.astype(bf16)
        low = (white - high.astype(f32)).astype(bf16)
        found = dot(lag_y[...], jnp.concatenate([high, low], axis=1))
        part = found[: 2 * SHIFTS, :PATCH] + found[: 2 * SHIFTS, PATCH:] + found[2 * SHIFTS :, :PATCH]
        lagged[pl.ds(m * SHIFTS, SHIFTS), pl.ds(0, PATCH)] = part[:SHIFTS]
        lagged[pl.ds(m * SHIFTS, SHIFTS), pl.ds(PATCH, PATCH)] = part[SHIFTS:]

    extra = lagged[pl.ds(PAIRS * SHIFTS, SHIFTS), pl.ds(0, PATCH)]
    extra = jnp.where(first_16[:, None, :], extra[None], 0.0).reshape(PAIRS * SHIFTS, PATCH)
    left = jnp.concatenate([lagged[pl.ds(0, PAIRS * SHIFTS), :], extra], axis=1)
    high = left.astype(bf16)
    low = (left - high.astype(f32)).astype(bf16)
    rows_all = PAIRS * SHIFTS
    found = dot(jnp.concatenate([high, low], axis=0), lag_x[...])
    surface = found[:rows_all, :PATCH] + found[:rows_all, PATCH:] + found[rows_all:, :PATCH]
    surface = surface.reshape(PAIRS, SHIFTS, PATCH)

    record[...] = jnp.zeros((1, PATCH), f32)
    for i in range(2):
        record[:, pl.ds(i * COLS, COLS)] = shift_in[i].astype(f32)
        record[:, pl.ds((2 + i) * COLS, COLS)] = node_in[0, i]
        record[:, pl.ds((4 + i) * COLS, COLS)] = node_in[1, i]
    rec = record[...]
    at_y = jnp.where(first_16, rec, 0.0)
    at_x = jnp.where(own_pair & (lane >= COLS) & (lane < 2 * COLS), rec, 0.0)
    gather = spread_t[pl.ds(0, PATCH), pl.ds(PATCH, PATCH)]
    shifts = lax.dot_general(
        jnp.concatenate([at_y, at_x], axis=0).astype(bf16),
        gather,
        (((1,), (1,)), ((), ())),
        preferred_element_type=f32,
    )
    lag_row = lax.broadcasted_iota(jnp.int32, (PAIRS, SHIFTS, PATCH), 1).astype(f32) - REACH
    lag_col = (lax.broadcasted_iota(jnp.int32, (PAIRS, SHIFTS, PATCH), 2) % HALF).astype(f32) - REACH
    dy = lag_row - shifts[:PAIRS][:, None, :]
    dx = lag_col - shifts[PAIRS:][:, None, :]
    mid_y, up_y, down_y = ((dy == k).astype(f32) for k in (0.0, 1.0, -1.0))
    mid_x, up_x, down_x = ((dx == k).astype(f32) for k in (0.0, 1.0, -1.0))
    at_mid_x = surface * mid_x
    at_mid_y = surface * mid_y
    picks = [
        jnp.sum(at_mid_x * (up_y - down_y), axis=1),
        jnp.sum(at_mid_x * (2.0 * mid_y - up_y - down_y), axis=1),
        jnp.sum(at_mid_y * (up_x - down_x), axis=1),
        jnp.sum(at_mid_y * (2.0 * mid_x - up_x - down_x), axis=1),
    ]
    found = dot(three_parts(jnp.concatenate(picks, axis=0)), gather)
    found = found[: 4 * PAIRS] + found[4 * PAIRS : 8 * PAIRS] + found[8 * PAIRS :]
    found = found.reshape(4, PAIRS, PATCH)
    found = jnp.sum(jnp.where(own_pair[None], found, 0.0), axis=1) * (1.0 / (PATCH * PATCH))
    lane_1 = lax.broadcasted_iota(jnp.int32, (1, PATCH), 1)
    slope = jnp.where(lane_1 < COLS, found[0:1], found[2:3])
    bend = jnp.where(lane_1 < COLS, found[1:2], found[3:4])
    flow = rec + 0.5 * slope / (1.0 + jnp.abs(bend))
    result = jnp.where(lane_1 < 2 * COLS, flow, rec)
    out[...] = jnp.broadcast_to(result, out.shape)


def pair_flow(own, below, near, near_below, offsets, initial, remote_initial, copies):
    tables = [jnp.asarray(t) for t in constant_tables()]
    operands = (own, below, near, near_below, offsets, initial, remote_initial, *tables)
    return pl.pallas_call(
        flow_kernel,
        out_shape=jax.ShapeDtypeStruct((copies, PATCH), f32),
        in_specs=[pl.BlockSpec(memory_space=pl.ANY)] * len(operands),
        out_specs=pl.BlockSpec(memory_space=pltpu.VMEM),
        scratch_shapes=[
            pltpu.VMEM((4 * HALF, WIDTH), bf16),
            *[pltpu.VMEM(t.shape, bf16) for t in tables],
            pltpu.VMEM(offsets.shape[1:], jnp.int32),
            pltpu.VMEM((2,) + initial.shape[1:], f32),
            pltpu.VMEM((1, PATCH), f32),
            pltpu.VMEM((PAIRS + 1, 2 * PATCH, 2 * PATCH), bf16),
            pltpu.VMEM(((PAIRS + 1) * SHIFTS, 2 * PATCH), f32),
            pltpu.SemaphoreType.DMA((len(operands),)),
        ],
        compiler_params=pltpu.CompilerParams(vmem_limit_bytes=VMEM_LIMIT),
    )(*operands)


def relax_kernel(plan, stiffness_h, ring_h, other_h, flow_out, moving_out, stiffness, ring, other, sems):
    moves = ((stiffness_h, stiffness), (ring_h, ring), (other_h, other))
    copies = [pltpu.make_async_copy(src, dst, sems.at[i]) for i, (src, dst) in enumerate(moves)]
    for copy in copies:
        copy.start()
    sec = lax.axis_index("sec")
    row = lax.axis_index("row")
    last_row = lax.axis_size("row") - 1
    place = lax.rem(row, RING)
    base = row - place
    count = SECS * RING
    node = lax.broadcasted_iota(jnp.int32, (count, PATCH), 0)
    lane = lax.broadcasted_iota(jnp.int32, (count, PATCH), 1)
    in_ring = node % RING
    section = node // RING
    other_first = jnp.broadcast_to(place, (count, PATCH)) < RING // 2
    valid = (section < SECS - 1) & (lane < 2 * COLS)
    valid_up = valid.astype(f32)
    has_left = (lane % COLS > 0).astype(f32)
    has_right = (lane % COLS < COLS - 1).astype(f32)
    row_here = base + in_ring
    row_other = row_here + jnp.where(other_first, -RING, RING)
    at_rows = (row_here, row_other)
    has_up = [(r > 0).astype(f32) for r in at_rows]
    has_down = [(r < last_row).astype(f32) for r in at_rows]
    first = in_ring == 0
    final = in_ring == RING - 1
    for copy in copies:
        copy.wait()
    level_id = lax.broadcasted_iota(jnp.int32, stiffness.shape, 0)
    here = ring[...]
    beyond = other[...]
    flows = [jnp.where(valid, b, 0.0) for b in (here, beyond)]
    moving = [pltpu.roll(b, PATCH - 2 * COLS, 1) for b in (here, beyond)]
    third = pltpu.roll(here, PATCH - 4 * COLS, 1)

    def moved(x, by):
        by = by % count
        return jnp.concatenate([x[by:], x[:by]], axis=0)

    for sweep in range(SWEEPS):
        picked = jnp.sum(jnp.where(level_id == plan[sweep], stiffness[...], 0.0), axis=0, keepdims=True)
        spring = picked[:, 0:1]
        tether = picked[:, 1:2]
        near_x, far_x = moving
        edge_above = jnp.where(other_first, moved(far_x, RING - 1), moved(third, RING - 1))
        edge_below = jnp.where(other_first, moved(third, 1 - RING), moved(far_x, 1 - RING))
        above = (jnp.where(first, edge_above, moved(near_x, -1)), jnp.where(first, moved(near_x, RING - 1), moved(far_x, -1)))
        below = (jnp.where(final, edge_below, moved(near_x, 1)), jnp.where(final, moved(near_x, 1 - RING), moved(far_x, 1)))
        fresh = []
        for k, x in enumerate(moving):
            col_left = pltpu.roll(x, 1, 1)
            col_right = pltpu.roll(x, PATCH - 1, 1)
            laplace = (
                (above[k] - x) * has_up[k]
                + (below[k] - x) * has_down[k]
                + (col_left - x) * has_left
                + (col_right - x) * has_right
            )
            residual = (moved(x, RING) - x - flows[k]) * valid_up
            below_res = jnp.where(section == 0, 0.0, moved(residual, -RING))
            fresh.append(x + step_size * (spring * laplace + tether * (residual - below_res)))
        moving = fresh

    mine = (section == sec) & (in_ring == place)
    for x, ref in ((flows[0], flow_out), (moving[0], moving_out)):
        line = jnp.sum(jnp.where(mine, x, 0.0), axis=0, keepdims=True)
        ref[0, 0] = line[:, :COLS]
        ref[0, 1] = line[:, COLS : 2 * COLS]


def relax(plan, stiffness, ring, other, shape):
    anywhere = pl.BlockSpec(memory_space=pl.ANY)
    return pl.pallas_call(
        relax_kernel,
        out_shape=[jax.ShapeDtypeStruct(shape, f32)] * 2,
        in_specs=[pl.BlockSpec(memory_space=pltpu.SMEM)] + [anywhere] * 3,
        out_specs=[pl.BlockSpec(memory_space=pltpu.VMEM)] * 2,
        scratch_shapes=[
            pltpu.VMEM(stiffness.shape, f32),
            pltpu.VMEM(ring.shape, f32),
            pltpu.VMEM(ring.shape, f32),
            pltpu.SemaphoreType.DMA((3,)),
        ],
        compiler_params=pltpu.CompilerParams(vmem_limit_bytes=VMEM_LIMIT),
    )(plan, stiffness, ring, other)


def shifted(block, axis, distance):
    devices = range(lax.axis_size(axis))
    route = [(i - distance, i) for i in devices if i - distance in devices]
    return lax.ppermute(block, axis, route)


def ring_route(rows, outward):
    route = []
    for r in range(rows):
        step = RING if (r % RING < RING // 2) == outward else -RING
        if 0 <= r - step < rows:
            route.append((r - step, r))
    return route


def per_device(images, initial, offsets, stiffness, plan):
    rows = lax.axis_size("row")
    near = shifted(images, "sec", -1)
    below = shifted(images, "row", -1)
    remote_initial = lax.ppermute(initial, "row", ring_route(rows, False))
    near_below = shifted(below, "sec", -1)
    count = SECS * RING
    mine = pair_flow(images, below, near, near_below, offsets, initial, remote_initial, count)
    groups = [
        [s * rows + RING * g + j for s in range(SECS) for j in range(RING)] for g in range(rows // RING)
    ]
    ring = lax.all_to_all(mine.reshape(count, 1, PATCH), ("sec", "row"), 0, 0, axis_index_groups=groups)
    other = lax.ppermute(ring, "row", ring_route(rows, True))
    return tuple(
        relax(plan, stiffness, ring.reshape(count, PATCH), other.reshape(count, PATCH), initial.shape)
    )


def solution(mesh):
    return jax.shard_map(
        per_device,
        mesh=mesh,
        in_specs=(
            P("sec", "row", None),
            P("sec", None, "row", None),
            P("sec", None, "row", None),
            P(),
            P(),
        ),
        out_specs=(P("sec", None, "row", None), P("sec", None, "row", None)),
        check_vma=False,
    )
```

```python
import math

import numpy as np
import jax
import jax.numpy as jnp
from jax import lax
from jax.experimental import pallas as pl
from jax.experimental.pallas import tpu as pltpu
from jax.sharding import PartitionSpec as P
import ml_dtypes

PATCH = 128
STRIDE = 64
HALF = 64
SWEEPS = 3
COLS = 16
PAIRS = 8
SECS = 4
RING = 4
SHIFTS = 16
REACH = 5
WIDTH = 1088

step_size = 0.2
floor_ratio = 0.2

VMEM_LIMIT = 24 * 1024 * 1024

f32 = jnp.float32
bf16 = jnp.bfloat16


def dft_halves():
    freq = np.arange(PATCH)
    phase = freq[:, None] * freq[None, :] % PATCH
    folded = np.minimum(phase, PATCH - phase)
    angle = folded * (2.0 * math.pi / PATCH)
    sine = np.sin(angle) * np.where(2 * phase > PATCH, -1.0, 1.0)
    sine = np.where(2 * folded == PATCH, 0.0, sine)
    cosine = np.cos(angle)
    cosine = np.where(4 * folded == PATCH, np.cos(np.float32(math.pi / 2)), cosine)
    return cosine.astype(ml_dtypes.bfloat16), (-sine).astype(ml_dtypes.bfloat16)


def two_parts(table):
    high = table.astype(ml_dtypes.bfloat16)
    low = (table - high.astype(np.float64)).astype(ml_dtypes.bfloat16)
    return high, low


def constant_tables():
    cos_t, sin_t = dft_halves()
    cos_f = cos_t.astype(np.float32)
    sin_f = sin_t.astype(np.float32)
    rows = np.zeros((2 * PATCH, 2 * PATCH), np.float32)
    rows[0:PATCH, 0:HALF] = cos_f[:HALF].T
    rows[0:PATCH, PATCH : PATCH + HALF] = sin_f[:HALF].T
    rows[HALF : HALF + PATCH, HALF:PATCH] = cos_f[:HALF].T
    rows[HALF : HALF + PATCH, PATCH + HALF :] = sin_f[:HALF].T
    nyquist = np.zeros((2 * PATCH, PATCH), np.float32)
    nyquist[0:PATCH, 0::2] = cos_f[HALF][:, None]
    nyquist[HALF : HALF + PATCH, 1::2] = cos_f[HALF][:, None]
    columns = np.block([[cos_f, -sin_f], [sin_f, cos_f]])
    lags = np.arange(SHIFTS) - REACH
    used = (np.arange(SHIFTS) <= 2 * REACH).astype(np.float64)
    freq = np.arange(PATCH)
    turn = (freq[None, :] * lags[:, None] % PATCH) * (2.0 * math.pi / PATCH)
    cos_y = np.cos(turn) * used[:, None]
    sin_y = np.sin(turn) * used[:, None]
    high, low = two_parts(np.block([[cos_y, -sin_y], [sin_y, cos_y]]))
    lag_y = np.concatenate([high, low], axis=0)
    weight = np.where(freq[:HALF] == 0, 1.0, 2.0)
    across = np.zeros((3 * PATCH, PATCH))
    for p in range(2):
        cols = slice(p * HALF, p * HALF + SHIFTS)
        block = slice(p * HALF, (p + 1) * HALF)
        across[:PATCH][block, cols] = (cos_y[:, :HALF] * weight).T
        across[PATCH : 2 * PATCH][block, cols] = (-sin_y[:, :HALF] * weight).T
        for c in range(p, COLS, 2):
            across[2 * PATCH + c, cols] = np.where(lags % 2 == 0, 1.0, -1.0) * used
    high, low = two_parts(across)
    lag_x = np.concatenate([high, low], axis=1)
    lane = np.arange(PATCH)
    patch = (lane % COLS % 2)[None, :] == (lane // HALF)[:, None]
    gather = (patch & (lane < 2 * COLS)[None, :]).astype(np.float32)
    single = (patch & (lane < COLS)[None, :]).astype(np.float32)
    same = ((lane // HALF)[:, None] == (lane // HALF)[None, :]).astype(np.float32)
    blank = np.zeros((PATCH, PATCH), np.float32)
    spread = np.block([[same, gather], [single.T, blank]])
    packed = [rows, np.concatenate([nyquist[:PATCH], nyquist[PATCH:]], axis=1), columns, spread, lag_y, lag_x]
    return np.concatenate([np.asarray(t).astype(ml_dtypes.bfloat16) for t in packed], axis=0)


TABLE_ROWS = {"rows": (0, 256), "nyquist": (256, 128), "columns": (384, 256), "spread": (640, 256)}
TABLE_ROWS |= {"lag_y": (896, 64), "lag_x": (960, 384)}


def table(ref, name):
    start, length = TABLE_ROWS[name]
    return ref[pl.ds(start, length), :]


def three_parts(x):
    high = x.astype(bf16)
    rest = x - high.astype(f32)
    mid = rest.astype(bf16)
    low = (rest - mid.astype(f32)).astype(bf16)
    return jnp.concatenate([high, mid, low], axis=0)


def dot(a, b):
    return jnp.dot(a, b, preferred_element_type=f32)


def prepare_kernel(plan, images, tables, offsets, initial, stiffness, own_out, tables_out, record, springs, sems):
    moves = ((images.at[0], own_out), (tables, tables_out))
    copies = [pltpu.make_async_copy(src, dst, sems.at[i]) for i, (src, dst) in enumerate(moves)]
    for copy in copies:
        copy.start()
    record[...] = jnp.zeros((1, PATCH), f32)
    for i in range(2):
        record[:, pl.ds(i * COLS, COLS)] = offsets[0, i].astype(f32)
        record[:, pl.ds((2 + i) * COLS, COLS)] = initial[0, i]
    level_id = lax.broadcasted_iota(jnp.int32, stiffness.shape, 0)
    for sweep in range(SWEEPS):
        picked = jnp.sum(jnp.where(level_id == plan[sweep], stiffness[...], 0.0), axis=0, keepdims=True)
        for i in range(2):
            springs[pl.ds(2 * sweep + i, 1), :] = jnp.broadcast_to(picked[:, i : i + 1], (1, PATCH))
    for copy in copies:
        copy.wait()


def prepare(plan, images, offsets, initial, stiffness):
    tables = jnp.asarray(constant_tables())
    in_vmem = pl.BlockSpec(memory_space=pltpu.VMEM)
    anywhere = pl.BlockSpec(memory_space=pl.ANY)
    return pl.pallas_call(
        prepare_kernel,
        out_shape=[
            jax.ShapeDtypeStruct(images.shape[1:], bf16),
            jax.ShapeDtypeStruct(tables.shape, bf16),
            jax.ShapeDtypeStruct((1, PATCH), f32),
            jax.ShapeDtypeStruct((8, PATCH), f32),
        ],
        in_specs=[pl.BlockSpec(memory_space=pltpu.SMEM), anywhere, anywhere, in_vmem, in_vmem, in_vmem],
        out_specs=[in_vmem] * 4,
        scratch_shapes=[pltpu.SemaphoreType.DMA((2,))],
        compiler_params=pltpu.CompilerParams(vmem_limit_bytes=VMEM_LIMIT),
    )(plan, images, tables, offsets, initial, stiffness)


def flow_kernel(own, below, near, near_below, record, remote, tables, out, spec, lagged):
    columns = table(tables, "columns")
    spread = table(tables, "spread")
    nyq_t = table(tables, "nyquist")
    rows_t = jnp.concatenate([table(tables, "rows"), jnp.concatenate([nyq_t[:, :PATCH], nyq_t[:, PATCH:]], axis=0)], axis=1)

    def finish_spectrum(m, stacked, table):
        product = dot(table, stacked).astype(bf16)
        spec[m] = product
        wide = product.astype(f32)
        return jnp.sum(wide * wide, axis=0, keepdims=True)

    energies = []
    lane_4 = lax.broadcasted_iota(jnp.int32, (4 * HALF, PATCH), 1)
    nyquist = jnp.zeros((4 * HALF, PATCH), f32)
    for m in range(PAIRS):
        span = 2 * PATCH if m < PAIRS - 1 else WIDTH - m * PATCH
        tiles = [ref[0, :, pl.ds(m * PATCH, span)] for ref in (below, near, near_below)]
        tiles.insert(0, own[:, pl.ds(m * PATCH, span)])
        seg = dot(jnp.concatenate(tiles, axis=0), rows_t[:span])
        nyquist = jnp.where(lane_4 // 2 == m, seg[:, 2 * PATCH :], nyquist)
        seg = seg[:, : 2 * PATCH].astype(bf16)
        stacked = jnp.concatenate(
            [
                jnp.concatenate([seg[:PATCH, :PATCH], seg[PATCH:, :PATCH]], axis=1),
                jnp.concatenate([seg[:PATCH, PATCH:], seg[PATCH:, PATCH:]], axis=1),
            ],
            axis=0,
        )
        energies.append(finish_spectrum(m, stacked, columns))
    seg = nyquist.astype(bf16)
    stacked = jnp.concatenate([seg[:PATCH], seg[PATCH:]], axis=1)
    energy_64 = finish_spectrum(PAIRS, stacked, columns[:, :PATCH])

    lane = lax.broadcasted_iota(jnp.int32, (PAIRS, PATCH), 1)
    pair = lax.broadcasted_iota(jnp.int32, (PAIRS, PATCH), 0)
    own_pair = (lane % COLS) // 2 == pair
    first_16 = own_pair & (lane < COLS)
    weight = jnp.where(lane % HALF == 0, 1.0, 2.0)
    energy = jnp.concatenate(energies, axis=0)

    def halves(x):
        return x[:, :PATCH], x[:, PATCH:]

    def totals(main, extra):
        left = jnp.concatenate([main * weight, jnp.where(first_16, extra, 0.0)], axis=1)
        found = dot(three_parts(left), spread)
        found = found[:PAIRS] + found[PAIRS : 2 * PAIRS] + found[2 * PAIRS :]
        by_pair, by_patch = halves(found)
        by_patch = jnp.sum(jnp.where(first_16, by_patch, 0.0), axis=0, keepdims=True) + extra
        scale = 1.0 / (PATCH * PATCH)
        return jnp.sqrt(by_pair * scale + 1e-06), jnp.sqrt(by_patch * scale + 1e-06)

    low_e, up_e = halves(energy)
    low_x, up_x = halves(energy_64)
    low_pair, low_patch = totals(low_e, low_x)
    up_pair, up_patch = totals(up_e, up_x)
    floor_pair = floor_ratio * low_pair * up_pair
    floor_patch = floor_ratio * low_patch * up_patch

    for m in range(PAIRS + 1):
        floor = floor_pair[m : m + 1] if m < PAIRS else floor_patch
        low_re = spec[m, pl.ds(0, PATCH), pl.ds(0, PATCH)].astype(f32)
        low_im = spec[m, pl.ds(PATCH, PATCH), pl.ds(0, PATCH)].astype(f32)
        up_re = spec[m, pl.ds(0, PATCH), pl.ds(PATCH, PATCH)].astype(f32)
        up_im = spec[m, pl.ds(PATCH, PATCH), pl.ds(PATCH, PATCH)].astype(f32)
        cross_re = low_re * up_re + low_im * up_im
        cross_im = low_re * up_im - low_im * up_re
        square = cross_re * cross_re + cross_im * cross_im
        modulus = square * lax.rsqrt(jnp.maximum(square, 1e-36))
        inverse = 1.0 / (modulus + floor)
        white = jnp.concatenate([cross_re * inverse, cross_im * inverse], axis=0)
        high = white.astype(bf16)
        low = (white - high.astype(f32)).astype(bf16)
        found = dot(table(tables, "lag_y"), jnp.concatenate([high, low], axis=1))
        part = found[: 2 * SHIFTS, :PATCH] + found[: 2 * SHIFTS, PATCH:] + found[2 * SHIFTS :, :PATCH]
        lagged[pl.ds(m * SHIFTS, SHIFTS), pl.ds(0, PATCH)] = part[:SHIFTS]
        lagged[pl.ds(m * SHIFTS, SHIFTS), pl.ds(PATCH, PATCH)] = part[SHIFTS:]

    extra = lagged[pl.ds(PAIRS * SHIFTS, SHIFTS), pl.ds(0, PATCH)]
    extra = jnp.where(first_16[:, None, :], extra[None], 0.0).reshape(PAIRS * SHIFTS, PATCH)
    left = jnp.concatenate([lagged[pl.ds(0, PAIRS * SHIFTS), :], extra], axis=1)
    high = left.astype(bf16)
    low = (left - high.astype(f32)).astype(bf16)
    rows_all = PAIRS * SHIFTS
    found = dot(jnp.concatenate([high, low], axis=0), table(tables, "lag_x"))
    surface = found[:rows_all, :PATCH] + found[:rows_all, PATCH:] + found[rows_all:, :PATCH]
    surface = surface.reshape(PAIRS, SHIFTS, PATCH)

    rec = record[...]
    at_y = jnp.where(first_16, rec, 0.0)
    at_x = jnp.where(own_pair & (lane >= COLS) & (lane < 2 * COLS), rec, 0.0)
    gather = spread[:PATCH, PATCH:]
    shifts = lax.dot_general(
        jnp.concatenate([at_y, at_x], axis=0).astype(bf16),
        gather,
        (((1,), (1,)), ((), ())),
        preferred_element_type=f32,
    )
    lag_row = lax.broadcasted_iota(jnp.int32, (PAIRS, SHIFTS, PATCH), 1).astype(f32) - REACH
    lag_col = (lax.broadcasted_iota(jnp.int32, (PAIRS, SHIFTS, PATCH), 2) % HALF).astype(f32) - REACH
    dy = lag_row - shifts[:PAIRS][:, None, :]
    dx = lag_col - shifts[PAIRS:][:, None, :]
    mid_y, up_y, down_y = ((dy == k).astype(f32) for k in (0.0, 1.0, -1.0))
    mid_x, up_x, down_x = ((dx == k).astype(f32) for k in (0.0, 1.0, -1.0))
    at_mid_x = surface * mid_x
    at_mid_y = surface * mid_y
    picks = [
        jnp.sum(at_mid_x * (up_y - down_y), axis=1),
        jnp.sum(at_mid_x * (2.0 * mid_y - up_y - down_y), axis=1),
        jnp.sum(at_mid_y * (up_x - down_x), axis=1),
        jnp.sum(at_mid_y * (2.0 * mid_x - up_x - down_x), axis=1),
    ]
    found = dot(three_parts(jnp.concatenate(picks, axis=0)), gather)
    found = found[: 4 * PAIRS] + found[4 * PAIRS : 8 * PAIRS] + found[8 * PAIRS :]
    found = found.reshape(4, PAIRS, PATCH)
    found = jnp.sum(jnp.where(own_pair[None], found, 0.0), axis=1) * (1.0 / (PATCH * PATCH))
    lane_1 = lax.broadcasted_iota(jnp.int32, (1, PATCH), 1)
    slope = jnp.where(lane_1 < COLS, found[0:1], found[2:3])
    bend = jnp.where(lane_1 < COLS, found[1:2], found[3:4])
    flow = rec + 0.5 * slope / (1.0 + jnp.abs(bend))
    result = jnp.where(lane_1 < 2 * COLS, flow, rec)
    out[...] = jnp.broadcast_to(result, out.shape)
    for i in range(2):
        out[:, pl.ds((4 + i) * COLS, COLS)] = jnp.broadcast_to(remote[0, i], (out.shape[0], COLS))


def pair_flow(own, below, near, near_below, record, remote_initial, tables, copies):
    operands = (own, below, near, near_below, record, remote_initial, tables)
    return pl.pallas_call(
        flow_kernel,
        out_shape=jax.ShapeDtypeStruct((copies, PATCH), f32),
        in_specs=[pl.BlockSpec(memory_space=pltpu.VMEM)] * len(operands),
        out_specs=pl.BlockSpec(memory_space=pltpu.VMEM),
        scratch_shapes=[
            pltpu.VMEM((PAIRS + 1, 2 * PATCH, 2 * PATCH), bf16),
            pltpu.VMEM(((PAIRS + 1) * SHIFTS, 2 * PATCH), f32),
        ],
        compiler_params=pltpu.CompilerParams(vmem_limit_bytes=VMEM_LIMIT),
    )(*operands)


def relax_kernel(springs, ring, other, flow_out, moving_out):
    sec = lax.axis_index("sec")
    row = lax.axis_index("row")
    last_row = lax.axis_size("row") - 1
    place = lax.rem(row, RING)
    base = row - place
    count = SECS * RING
    node = lax.broadcasted_iota(jnp.int32, (count, PATCH), 0)
    lane = lax.broadcasted_iota(jnp.int32, (count, PATCH), 1)
    in_ring = node % RING
    section = node // RING
    other_first = jnp.broadcast_to(place, (count, PATCH)) < RING // 2
    valid = (section < SECS - 1) & (lane < 2 * COLS)
    valid_up = valid.astype(f32)
    has_left = (lane % COLS > 0).astype(f32)
    has_right = (lane % COLS < COLS - 1).astype(f32)
    row_here = base + in_ring
    row_other = row_here + jnp.where(other_first, -RING, RING)
    at_rows = (row_here, row_other)
    has_up = [(r > 0).astype(f32) for r in at_rows]
    has_down = [(r < last_row).astype(f32) for r in at_rows]
    first = in_ring == 0
    final = in_ring == RING - 1
    here = ring[...]
    beyond = other[...]
    flows = [jnp.where(valid, b, 0.0) for b in (here, beyond)]
    moving = [pltpu.roll(b, PATCH - 2 * COLS, 1) for b in (here, beyond)]
    third = pltpu.roll(here, PATCH - 4 * COLS, 1)

    def moved(x, by):
        by = by % count
        return jnp.concatenate([x[by:], x[:by]], axis=0)

    for sweep in range(SWEEPS):
        spring = springs[pl.ds(2 * sweep, 1), :]
        tether = springs[pl.ds(2 * sweep + 1, 1), :]
        near_x, far_x = moving
        edge_above = jnp.where(other_first, moved(far_x, RING - 1), moved(third, RING - 1))
        edge_below = jnp.where(other_first, moved(third, 1 - RING), moved(far_x, 1 - RING))
        above = (jnp.where(first, edge_above, moved(near_x, -1)), jnp.where(first, moved(near_x, RING - 1), moved(far_x, -1)))
        below = (jnp.where(final, edge_below, moved(near_x, 1)), jnp.where(final, moved(near_x, 1 - RING), moved(far_x, 1)))
        fresh = []
        for k, x in enumerate(moving):
            col_left = pltpu.roll(x, 1, 1)
            col_right = pltpu.roll(x, PATCH - 1, 1)
            laplace = (
                (above[k] - x) * has_up[k]
                + (below[k] - x) * has_down[k]
                + (col_left - x) * has_left
                + (col_right - x) * has_right
            )
            residual = (moved(x, RING) - x - flows[k]) * valid_up
            below_res = jnp.where(section == 0, 0.0, moved(residual, -RING))
            fresh.append(x + step_size * (spring * laplace + tether * (residual - below_res)))
        moving = fresh

    mine = (section == sec) & (in_ring == place)
    for x, ref in ((flows[0], flow_out), (moving[0], moving_out)):
        line = jnp.sum(jnp.where(mine, x, 0.0), axis=0, keepdims=True)
        ref[0, 0] = line[:, :COLS]
        ref[0, 1] = line[:, COLS : 2 * COLS]


def relax(springs, ring, other, shape):
    in_vmem = pl.BlockSpec(memory_space=pltpu.VMEM)
    return pl.pallas_call(
        relax_kernel,
        out_shape=[jax.ShapeDtypeStruct(shape, f32)] * 2,
        in_specs=[in_vmem] * 3,
        out_specs=[in_vmem] * 2,
        compiler_params=pltpu.CompilerParams(vmem_limit_bytes=VMEM_LIMIT),
    )(springs, ring, other)


def shifted(block, axis, distance):
    devices = range(lax.axis_size(axis))
    route = [(i - distance, i) for i in devices if i - distance in devices]
    return lax.ppermute(block, axis, route)


def ring_route(rows, outward):
    route = []
    for r in range(rows):
        step = RING if (r % RING < RING // 2) == outward else -RING
        if 0 <= r - step < rows:
            route.append((r - step, r))
    return route


def per_device(images, initial, offsets, stiffness, plan):
    rows = lax.axis_size("row")
    below = shifted(images, "row", -1)
    remote_initial = lax.ppermute(initial, "row", ring_route(rows, False))
    near = shifted(images, "sec", -1)
    own, tables, record, springs = prepare(plan, images, offsets, initial, stiffness)
    below, remote_initial, own, tables, record, springs = lax.optimization_barrier(
        (below, remote_initial, own, tables, record, springs)
    )
    near_below = shifted(below, "sec", -1)
    count = SECS * RING
    mine = pair_flow(own, below, near, near_below, record, remote_initial, tables, count)
    groups = [
        [s * rows + RING * g + j for s in range(SECS) for j in range(RING)] for g in range(rows // RING)
    ]
    ring = lax.all_to_all(mine.reshape(count, 1, PATCH), ("sec", "row"), 0, 0, axis_index_groups=groups)
    other = lax.ppermute(ring, "row", ring_route(rows, True))
    return tuple(
        relax(springs, ring.reshape(count, PATCH), other.reshape(count, PATCH), initial.shape)
    )


def solution(mesh):
    return jax.shard_map(
        per_device,
        mesh=mesh,
        in_specs=(
            P("sec", "row", None),
            P("sec", None, "row", None),
            P("sec", None, "row", None),
            P(),
            P(),
        ),
        out_specs=(P("sec", None, "row", None), P("sec", None, "row", None)),
        check_vma=False,
    )
```

```python
import math

import numpy as np
import jax
import jax.numpy as jnp
from jax import lax
from jax.experimental import pallas as pl
from jax.experimental.pallas import tpu as pltpu
from jax.sharding import PartitionSpec as P
import ml_dtypes

PATCH = 128
STRIDE = 64
HALF = 64
SWEEPS = 3
COLS = 16
PAIRS = 8
SECS = 4
RING = 4
SHIFTS = 16
REACH = 5
WINDOW = 8
REACH_ROWS = 3
WIDTH = 1088

step_size = 0.2
floor_ratio = 0.2

VMEM_LIMIT = 24 * 1024 * 1024

f32 = jnp.float32
bf16 = jnp.bfloat16


def dft_halves():
    freq = np.arange(PATCH)
    phase = freq[:, None] * freq[None, :] % PATCH
    folded = np.minimum(phase, PATCH - phase)
    angle = folded * (2.0 * math.pi / PATCH)
    sine = np.sin(angle) * np.where(2 * phase > PATCH, -1.0, 1.0)
    sine = np.where(2 * folded == PATCH, 0.0, sine)
    cosine = np.cos(angle)
    cosine = np.where(4 * folded == PATCH, np.cos(np.float32(math.pi / 2)), cosine)
    return cosine.astype(ml_dtypes.bfloat16), (-sine).astype(ml_dtypes.bfloat16)


def two_parts(table):
    high = table.astype(ml_dtypes.bfloat16)
    low = (table - high.astype(np.float64)).astype(ml_dtypes.bfloat16)
    return high, low


def constant_tables():
    cos_t, sin_t = dft_halves()
    cos_f = cos_t.astype(np.float32)
    sin_f = sin_t.astype(np.float32)
    rows = np.zeros((2 * PATCH, 2 * PATCH), np.float32)
    rows[0:PATCH, 0:HALF] = cos_f[:HALF].T
    rows[0:PATCH, PATCH : PATCH + HALF] = sin_f[:HALF].T
    rows[HALF : HALF + PATCH, HALF:PATCH] = cos_f[:HALF].T
    rows[HALF : HALF + PATCH, PATCH + HALF :] = sin_f[:HALF].T
    nyquist = np.zeros((2 * PATCH, PATCH), np.float32)
    nyquist[0:PATCH, 0::2] = cos_f[HALF][:, None]
    nyquist[HALF : HALF + PATCH, 1::2] = cos_f[HALF][:, None]
    columns = np.block([[cos_f, -sin_f], [sin_f, cos_f]])
    lags = np.arange(SHIFTS) - REACH
    used = (np.arange(SHIFTS) <= 2 * REACH).astype(np.float64)
    freq = np.arange(PATCH)
    turn = (freq[None, :] * lags[:, None] % PATCH) * (2.0 * math.pi / PATCH)
    cos_y = np.cos(turn) * used[:, None]
    sin_y = np.sin(turn) * used[:, None]
    high, low = two_parts(np.block([[cos_y, -sin_y], [sin_y, cos_y]]))
    lag_y = np.concatenate([high, low], axis=0)
    weight = np.where(freq[:HALF] == 0, 1.0, 2.0)
    across = np.zeros((3 * PATCH, PATCH))
    for p in range(2):
        cols = slice(p * HALF, p * HALF + SHIFTS)
        block = slice(p * HALF, (p + 1) * HALF)
        across[:PATCH][block, cols] = (cos_y[:, :HALF] * weight).T
        across[PATCH : 2 * PATCH][block, cols] = (-sin_y[:, :HALF] * weight).T
        for c in range(p, COLS, 2):
            across[2 * PATCH + c, cols] = np.where(lags % 2 == 0, 1.0, -1.0) * used
    high, low = two_parts(across)
    lag_x = np.concatenate([high, low], axis=1)
    lane = np.arange(PATCH)
    patch = (lane % COLS % 2)[None, :] == (lane // HALF)[:, None]
    gather = (patch & (lane < 2 * COLS)[None, :]).astype(np.float32)
    single = (patch & (lane < COLS)[None, :]).astype(np.float32)
    same = ((lane // HALF)[:, None] == (lane // HALF)[None, :]).astype(np.float32)
    blank = np.zeros((PATCH, PATCH), np.float32)
    spread = np.block([[same, gather], [single.T, blank]])
    turned = np.roll(columns.reshape(2 * PATCH, 2, PATCH), HALF, axis=2).reshape(2 * PATCH, 2 * PATCH)
    packed = [rows, np.concatenate([nyquist[:PATCH], nyquist[PATCH:]], axis=1), spread, lag_y, lag_x, columns, turned]
    return np.concatenate([np.asarray(t).astype(ml_dtypes.bfloat16) for t in packed], axis=0)


TABLE_ROWS = {"rows": (0, 256), "nyquist": (256, 128), "spread": (384, 256)}
TABLE_ROWS |= {"lag_y": (640, 64), "lag_x": (704, 384), "columns": (1088, 256)}
FIXED_ROWS = 1088


def table(ref, name):
    start, length = TABLE_ROWS[name]
    return ref[pl.ds(start, length), :]


def three_parts(x):
    high = x.astype(bf16)
    rest = x - high.astype(f32)
    mid = rest.astype(bf16)
    low = (rest - mid.astype(f32)).astype(bf16)
    return jnp.concatenate([high, mid, low], axis=0)


def dot(a, b):
    return jnp.dot(a, b, preferred_element_type=f32)


def takes_row_above(sec):
    return sec < 2


def prepare_kernel(plan, images, tables, offsets, initial, stiffness, own_out, tables_out, record, springs, sems):
    downward = takes_row_above(lax.axis_index("sec"))
    columns, length = TABLE_ROWS["columns"]
    chosen = pl.multiple_of(columns + length * downward.astype(jnp.int32), length // 2)
    moves = (
        (tables.at[pl.ds(0, FIXED_ROWS)], tables_out.at[pl.ds(0, FIXED_ROWS)]),
        (tables.at[pl.ds(chosen, length)], tables_out.at[pl.ds(columns, length)]),
    )
    copies = [pltpu.make_async_copy(src, dst, sems.at[i]) for i, (src, dst) in enumerate(moves)]
    for copy in copies:
        copy.start()
    past = downward & (lax.axis_index("row") == 0)
    own = images[0]
    own_out[...] = jnp.where(jnp.broadcast_to(past, own.shape), jnp.zeros_like(own), own)
    record[...] = jnp.zeros((1, PATCH), f32)
    for i in range(2):
        record[:, pl.ds(i * COLS, COLS)] = offsets[0, i].astype(f32)
        record[:, pl.ds((2 + i) * COLS, COLS)] = initial[0, i]
    level_id = lax.broadcasted_iota(jnp.int32, stiffness.shape, 0)
    for sweep in range(SWEEPS):
        picked = jnp.sum(jnp.where(level_id == plan[sweep], stiffness[...], 0.0), axis=0, keepdims=True)
        for i in range(2):
            springs[pl.ds(2 * sweep + i, 1), :] = jnp.broadcast_to(picked[:, i : i + 1], (1, PATCH))
    for copy in copies:
        copy.wait()


def prepare(plan, images, offsets, initial, stiffness):
    tables = jnp.asarray(constant_tables())
    columns, length = TABLE_ROWS["columns"]
    in_vmem = pl.BlockSpec(memory_space=pltpu.VMEM)
    anywhere = pl.BlockSpec(memory_space=pl.ANY)
    return pl.pallas_call(
        prepare_kernel,
        out_shape=[
            jax.ShapeDtypeStruct(images.shape[1:], bf16),
            jax.ShapeDtypeStruct((columns + length, 2 * PATCH), bf16),
            jax.ShapeDtypeStruct((1, PATCH), f32),
            jax.ShapeDtypeStruct((8, PATCH), f32),
        ],
        in_specs=[pl.BlockSpec(memory_space=pltpu.SMEM), in_vmem, anywhere, in_vmem, in_vmem, in_vmem],
        out_specs=[in_vmem] * 4,
        scratch_shapes=[pltpu.SemaphoreType.DMA((2,))],
        compiler_params=pltpu.CompilerParams(vmem_limit_bytes=VMEM_LIMIT),
    )(plan, images, tables, offsets, initial, stiffness)


def flow_kernel(own, across, near, near_across, record, far_offsets, tables, out, spec, lagged, shift_row):
    columns = table(tables, "columns")
    spread = table(tables, "spread")
    nyq_t = table(tables, "nyquist")
    rows_t = jnp.concatenate([table(tables, "rows"), jnp.concatenate([nyq_t[:, :PATCH], nyq_t[:, PATCH:]], axis=0)], axis=1)

    def finish_spectrum(m, stacked, table):
        product = dot(table, stacked).astype(bf16)
        spec[m] = product
        wide = product.astype(f32)
        return jnp.sum(wide * wide, axis=0, keepdims=True)

    energies = []
    lane_4 = lax.broadcasted_iota(jnp.int32, (4 * HALF, PATCH), 1)
    nyquist = jnp.zeros((4 * HALF, PATCH), f32)
    for m in range(PAIRS):
        span = 2 * PATCH if m < PAIRS - 1 else WIDTH - m * PATCH
        tiles = [ref[0, :, pl.ds(m * PATCH, span)] for ref in (across, near, near_across)]
        tiles.insert(0, own[:, pl.ds(m * PATCH, span)])
        seg = dot(jnp.concatenate(tiles, axis=0), rows_t[:span])
        nyquist = jnp.where(lane_4 // 2 == m, seg[:, 2 * PATCH :], nyquist)
        seg = seg[:, : 2 * PATCH].astype(bf16)
        stacked = jnp.concatenate(
            [
                jnp.concatenate([seg[:PATCH, :PATCH], seg[PATCH:, :PATCH]], axis=1),
                jnp.concatenate([seg[:PATCH, PATCH:], seg[PATCH:, PATCH:]], axis=1),
            ],
            axis=0,
        )
        energies.append(finish_spectrum(m, stacked, columns))
    seg = nyquist.astype(bf16)
    stacked = jnp.concatenate([seg[:PATCH], seg[PATCH:]], axis=1)
    energy_64 = finish_spectrum(PAIRS, stacked, columns[:, :PATCH])

    lane = lax.broadcasted_iota(jnp.int32, (PAIRS, PATCH), 1)
    pair = lax.broadcasted_iota(jnp.int32, (PAIRS, PATCH), 0)
    own_pair = (lane % COLS) // 2 == pair
    first_16 = own_pair & (lane < COLS)
    weight = jnp.where(lane % HALF == 0, 1.0, 2.0)
    energy = jnp.concatenate(energies, axis=0)

    def halves(x):
        return x[:, :PATCH], x[:, PATCH:]

    def totals(main, extra):
        left = jnp.concatenate([main * weight, jnp.where(first_16, extra, 0.0)], axis=1)
        found = dot(three_parts(left), spread)
        found = found[:PAIRS] + found[PAIRS : 2 * PAIRS] + found[2 * PAIRS :]
        by_pair, by_patch = halves(found)
        by_patch = jnp.sum(jnp.where(first_16, by_patch, 0.0), axis=0, keepdims=True) + extra
        scale = 1.0 / (PATCH * PATCH)
        return jnp.sqrt(by_pair * scale + 1e-06), jnp.sqrt(by_patch * scale + 1e-06)

    low_e, up_e = halves(energy)
    low_x, up_x = halves(energy_64)
    low_pair, low_patch = totals(low_e, low_x)
    up_pair, up_patch = totals(up_e, up_x)
    floor_pair = floor_ratio * low_pair * up_pair
    floor_patch = floor_ratio * low_patch * up_patch

    for m in range(PAIRS + 1):
        floor = floor_pair[m : m + 1] if m < PAIRS else floor_patch
        low_re = spec[m, pl.ds(0, PATCH), pl.ds(0, PATCH)].astype(f32)
        low_im = spec[m, pl.ds(PATCH, PATCH), pl.ds(0, PATCH)].astype(f32)
        up_re = spec[m, pl.ds(0, PATCH), pl.ds(PATCH, PATCH)].astype(f32)
        up_im = spec[m, pl.ds(PATCH, PATCH), pl.ds(PATCH, PATCH)].astype(f32)
        cross_re = low_re * up_re + low_im * up_im
        cross_im = low_re * up_im - low_im * up_re
        square = cross_re * cross_re + cross_im * cross_im
        modulus = square * lax.rsqrt(jnp.maximum(square, 1e-36))
        inverse = 1.0 / (modulus + floor)
        white = jnp.concatenate([cross_re * inverse, cross_im * inverse], axis=0)
        high = white.astype(bf16)
        low = (white - high.astype(f32)).astype(bf16)
        found = dot(table(tables, "lag_y"), jnp.concatenate([high, low], axis=1))
        part = found[: 2 * SHIFTS, :PATCH] + found[: 2 * SHIFTS, PATCH:] + found[2 * SHIFTS :, :PATCH]
        lagged[pl.ds(m * SHIFTS, SHIFTS), pl.ds(0, PATCH)] = part[:SHIFTS]
        lagged[pl.ds(m * SHIFTS, SHIFTS), pl.ds(PATCH, PATCH)] = part[SHIFTS:]

    extra = lagged[pl.ds(PAIRS * SHIFTS, SHIFTS), pl.ds(0, PATCH)]
    extra = jnp.where(first_16[:, None, :], extra[None], 0.0).reshape(PAIRS * SHIFTS, PATCH)
    left = jnp.concatenate([lagged[pl.ds(0, PAIRS * SHIFTS), :], extra], axis=1)
    high = left.astype(bf16)
    low = (left - high.astype(f32)).astype(bf16)
    rows_all = PAIRS * SHIFTS
    found = dot(jnp.concatenate([high, low], axis=0), table(tables, "lag_x"))
    surface = found[:rows_all, :PATCH] + found[:rows_all, PATCH:] + found[rows_all:, :PATCH]
    surface = surface.reshape(PAIRS, SHIFTS, PATCH)

    for i in range(2):
        shift_row[:, pl.ds(i * COLS, COLS)] = far_offsets[0, i].astype(f32)
    rec = record[...]
    lane_1 = lax.broadcasted_iota(jnp.int32, (1, PATCH), 1)
    downward = jnp.broadcast_to(takes_row_above(lax.axis_index("sec")), (1, PATCH))
    rec = jnp.where(downward & (lane_1 < 2 * COLS), shift_row[...], rec)
    at_y = jnp.where(first_16, rec, 0.0)
    at_x = jnp.where(own_pair & (lane >= COLS) & (lane < 2 * COLS), rec, 0.0)
    gather = spread[:PATCH, PATCH:]
    shifts = lax.dot_general(
        jnp.concatenate([at_y, at_x], axis=0).astype(bf16),
        gather,
        (((1,), (1,)), ((), ())),
        preferred_element_type=f32,
    )
    lag_row = lax.broadcasted_iota(jnp.int32, (PAIRS, SHIFTS, PATCH), 1).astype(f32) - REACH
    lag_col = (lax.broadcasted_iota(jnp.int32, (PAIRS, SHIFTS, PATCH), 2) % HALF).astype(f32) - REACH
    dy = lag_row - shifts[:PAIRS][:, None, :]
    dx = lag_col - shifts[PAIRS:][:, None, :]
    mid_y, up_y, down_y = ((dy == k).astype(f32) for k in (0.0, 1.0, -1.0))
    mid_x, up_x, down_x = ((dx == k).astype(f32) for k in (0.0, 1.0, -1.0))
    at_mid_x = surface * mid_x
    at_mid_y = surface * mid_y
    picks = [
        jnp.sum(at_mid_x * (up_y - down_y), axis=1),
        jnp.sum(at_mid_x * (2.0 * mid_y - up_y - down_y), axis=1),
        jnp.sum(at_mid_y * (up_x - down_x), axis=1),
        jnp.sum(at_mid_y * (2.0 * mid_x - up_x - down_x), axis=1),
    ]
    found = dot(three_parts(jnp.concatenate(picks, axis=0)), gather)
    found = found[: 4 * PAIRS] + found[4 * PAIRS : 8 * PAIRS] + found[8 * PAIRS :]
    found = found.reshape(4, PAIRS, PATCH)
    found = jnp.sum(jnp.where(own_pair[None], found, 0.0), axis=1) * (1.0 / (PATCH * PATCH))
    slope = jnp.where(lane_1 < COLS, found[0:1], found[2:3])
    bend = jnp.where(lane_1 < COLS, found[1:2], found[3:4])
    flow = rec + 0.5 * slope / (1.0 + jnp.abs(bend))
    result = jnp.where(lane_1 < 2 * COLS, flow, rec)
    out[...] = jnp.broadcast_to(result, out.shape)


def pair_flow(own, across, near, near_across, record, far_offsets, tables, copies):
    operands = (own, across, near, near_across, record, far_offsets, tables)
    return pl.pallas_call(
        flow_kernel,
        out_shape=jax.ShapeDtypeStruct((copies, PATCH), f32),
        in_specs=[pl.BlockSpec(memory_space=pltpu.VMEM)] * len(operands),
        out_specs=pl.BlockSpec(memory_space=pltpu.VMEM),
        scratch_shapes=[
            pltpu.VMEM((PAIRS + 1, 2 * PATCH, 2 * PATCH), bf16),
            pltpu.VMEM(((PAIRS + 1) * SHIFTS, 2 * PATCH), f32),
            pltpu.VMEM((1, PATCH), f32),
        ],
        compiler_params=pltpu.CompilerParams(vmem_limit_bytes=VMEM_LIMIT),
    )(*operands)


def relax_kernel(springs, before, mid, after, flow_out, moving_out, nodes):
    sec = lax.axis_index("sec")
    row = lax.axis_index("row")
    last_row = lax.axis_size("row") - 1
    place = lax.rem(row, RING)
    for s in range(SECS):
        for k, ref in enumerate((before, mid, after)):
            nodes[s, pl.ds(k * RING, RING), :] = ref[pl.ds(s * RING, RING), :]
        nodes[s, pl.ds(3 * RING, RING), :] = jnp.zeros((RING, PATCH), f32)
    window = (WINDOW, PATCH)
    lane = lax.broadcasted_iota(jnp.int32, window, 1)
    here = lax.broadcasted_iota(jnp.int32, window, 0) + (row - REACH_ROWS)
    used = lane < 2 * COLS
    has_up = here > 0
    has_down = here < last_row
    has_left = lane % COLS > 0
    has_right = lane % COLS < COLS - 1
    start = place + RING - REACH_ROWS
    moving = []
    flows = []
    for s in range(SECS):
        records = nodes[s, pl.ds(start, WINDOW), :]
        moving.append(pltpu.roll(records, PATCH - 2 * COLS, 1))
        if s < SECS - 1:
            found = nodes[s, pl.ds(start + 1, WINDOW), :] if takes_row_above(s) else records
            flows.append(jnp.where(used, found, 0.0))

    for sweep in range(SWEEPS):
        spring = springs[pl.ds(2 * sweep, 1), :]
        tether = springs[pl.ds(2 * sweep + 1, 1), :]
        residuals = [moving[s + 1] - moving[s] - flows[s] for s in range(SECS - 1)]
        fresh = []
        for s, x in enumerate(moving):
            laplace = (
                jnp.where(has_up, pltpu.roll(x, 1, 0) - x, 0.0)
                + jnp.where(has_down, pltpu.roll(x, WINDOW - 1, 0) - x, 0.0)
                + jnp.where(has_left, pltpu.roll(x, 1, 1) - x, 0.0)
                + jnp.where(has_right, pltpu.roll(x, PATCH - 1, 1) - x, 0.0)
            )
            if s == 0:
                pull = residuals[0]
            elif s == SECS - 1:
                pull = -residuals[s - 1]
            else:
                pull = residuals[s] - residuals[s - 1]
            fresh.append(x + step_size * (spring * laplace + tether * pull))
        moving = fresh

    flows.append(jnp.zeros(window, f32))
    for parts, ref in ((flows, flow_out), (moving, moving_out)):
        line = parts[0][REACH_ROWS : REACH_ROWS + 1]
        for s in range(1, SECS):
            line = jnp.where(jnp.broadcast_to(sec == s, line.shape), parts[s][REACH_ROWS : REACH_ROWS + 1], line)
        ref[0, 0] = line[:, :COLS]
        ref[0, 1] = line[:, COLS : 2 * COLS]


def relax(springs, before, mid, after, shape):
    in_vmem = pl.BlockSpec(memory_space=pltpu.VMEM)
    return pl.pallas_call(
        relax_kernel,
        out_shape=[jax.ShapeDtypeStruct(shape, f32)] * 2,
        in_specs=[in_vmem] * 4,
        out_specs=[in_vmem] * 2,
        scratch_shapes=[pltpu.VMEM((SECS, 4 * RING, PATCH), f32)],
        compiler_params=pltpu.CompilerParams(vmem_limit_bytes=VMEM_LIMIT),
    )(springs, before, mid, after)


def image_routes(rows):
    at = lambda s, r: s * rows + r % rows
    across, near, near_across, shifts = [], [], [], []
    for r in range(rows):
        for s in range(SECS - 1):
            if takes_row_above(s):
                across.append((at(s, r - 1), at(s, r)))
                shifts.append((at(s, r - 1), at(s, r)))
                near_across.append((at(s + 1, r - 1), at(s, r)))
                if r > 0:
                    near.append((at(s + 1, r), at(s, r)))
            else:
                near.append((at(s + 1, r), at(s, r)))
                if r < rows - 1:
                    across.append((at(s, r + 1), at(s, r)))
                    near_across.append((at(s + 1, r + 1), at(s, r)))
    return across, near, near_across, shifts


def per_device(images, initial, offsets, stiffness, plan):
    rows = lax.axis_size("row")
    both = ("sec", "row")
    across_route, near_route, near_across_route, shift_route = image_routes(rows)
    across = lax.ppermute(images, both, across_route)
    near_across = lax.ppermute(images, both, near_across_route)
    near = lax.ppermute(images, both, near_route)
    far_offsets = lax.ppermute(offsets, both, shift_route)
    own, tables, record, springs = prepare(plan, images, offsets, initial, stiffness)
    count = SECS * RING
    mine = pair_flow(own, across, near, near_across, record, far_offsets, tables, count)
    groups = [
        [s * rows + RING * g + j for s in range(SECS) for j in range(RING)] for g in range(rows // RING)
    ]
    ring = lax.all_to_all(mine.reshape(count, 1, PATCH), both, 0, 0, axis_index_groups=groups)
    before = lax.ppermute(ring, "row", [(r, (r + RING) % rows) for r in range(rows)])
    after = lax.ppermute(ring, "row", [((r + RING) % rows, r) for r in range(rows)])
    blocks = [block.reshape(count, PATCH) for block in (before, ring, after)]
    return tuple(relax(springs, *blocks, initial.shape))


def solution(mesh):
    return jax.shard_map(
        per_device,
        mesh=mesh,
        in_specs=(
            P("sec", "row", None),
            P("sec", None, "row", None),
            P("sec", None, "row", None),
            P(),
            P(),
        ),
        out_specs=(P("sec", None, "row", None), P("sec", None, "row", None)),
        check_vma=False,
    )
```

```python
import math

import numpy as np
import jax
import jax.numpy as jnp
from jax import lax
from jax.experimental import pallas as pl
from jax.experimental.pallas import tpu as pltpu
from jax.sharding import PartitionSpec as P
import ml_dtypes

PATCH = 128
STRIDE = 64
HALF = 64
SWEEPS = 3
COLS = 16
PAIRS = 8
SECS = 4
RING = 4
SHIFTS = 16
REACH = 5
WIDTH = 1088

step_size = 0.2
floor_ratio = 0.2

VMEM_LIMIT = 24 * 1024 * 1024

f32 = jnp.float32
bf16 = jnp.bfloat16


def dft_halves():
    freq = np.arange(PATCH)
    phase = freq[:, None] * freq[None, :] % PATCH
    folded = np.minimum(phase, PATCH - phase)
    angle = folded * (2.0 * math.pi / PATCH)
    sine = np.sin(angle) * np.where(2 * phase > PATCH, -1.0, 1.0)
    sine = np.where(2 * folded == PATCH, 0.0, sine)
    cosine = np.cos(angle)
    cosine = np.where(4 * folded == PATCH, np.cos(np.float32(math.pi / 2)), cosine)
    return cosine.astype(ml_dtypes.bfloat16), (-sine).astype(ml_dtypes.bfloat16)


def two_parts(table):
    high = table.astype(ml_dtypes.bfloat16)
    low = (table - high.astype(np.float64)).astype(ml_dtypes.bfloat16)
    return high, low


def constant_tables():
    cos_t, sin_t = dft_halves()
    cos_f = cos_t.astype(np.float32)
    sin_f = sin_t.astype(np.float32)
    rows = np.zeros((2 * PATCH, 2 * PATCH), np.float32)
    rows[0:PATCH, 0:HALF] = cos_f[:HALF].T
    rows[0:PATCH, PATCH : PATCH + HALF] = sin_f[:HALF].T
    rows[HALF : HALF + PATCH, HALF:PATCH] = cos_f[:HALF].T
    rows[HALF : HALF + PATCH, PATCH + HALF :] = sin_f[:HALF].T
    nyquist = np.zeros((2 * PATCH, PATCH), np.float32)
    nyquist[0:PATCH, 0::2] = cos_f[HALF][:, None]
    nyquist[HALF : HALF + PATCH, 1::2] = cos_f[HALF][:, None]
    columns = np.block([[cos_f, -sin_f], [sin_f, cos_f]])
    lags = np.arange(SHIFTS) - REACH
    used = (np.arange(SHIFTS) <= 2 * REACH).astype(np.float64)
    freq = np.arange(PATCH)
    turn = (freq[None, :] * lags[:, None] % PATCH) * (2.0 * math.pi / PATCH)
    cos_y = np.cos(turn) * used[:, None]
    sin_y = np.sin(turn) * used[:, None]
    high, low = two_parts(np.block([[cos_y, -sin_y], [sin_y, cos_y]]))
    lag_y = np.concatenate([high, low], axis=0)
    weight = np.where(freq[:HALF] == 0, 1.0, 2.0)
    across = np.zeros((3 * PATCH, PATCH))
    for p in range(2):
        cols = slice(p * HALF, p * HALF + SHIFTS)
        block = slice(p * HALF, (p + 1) * HALF)
        across[:PATCH][block, cols] = (cos_y[:, :HALF] * weight).T
        across[PATCH : 2 * PATCH][block, cols] = (-sin_y[:, :HALF] * weight).T
        for c in range(p, COLS, 2):
            across[2 * PATCH + c, cols] = np.where(lags % 2 == 0, 1.0, -1.0) * used
    high, low = two_parts(across)
    lag_x = np.concatenate([high, low], axis=1)
    lane = np.arange(PATCH)
    patch = (lane % COLS % 2)[None, :] == (lane // HALF)[:, None]
    gather = (patch & (lane < 2 * COLS)[None, :]).astype(np.float32)
    single = (patch & (lane < COLS)[None, :]).astype(np.float32)
    same = ((lane // HALF)[:, None] == (lane // HALF)[None, :]).astype(np.float32)
    blank = np.zeros((PATCH, PATCH), np.float32)
    spread = np.block([[same, gather], [single.T, blank]])
    packed = [rows, np.concatenate([nyquist[:PATCH], nyquist[PATCH:]], axis=1), columns, spread, lag_y, lag_x]
    return np.concatenate([np.asarray(t).astype(ml_dtypes.bfloat16) for t in packed], axis=0)


TABLE_ROWS = {"rows": (0, 256), "nyquist": (256, 128), "columns": (384, 256), "spread": (640, 256)}
TABLE_ROWS |= {"lag_y": (896, 64), "lag_x": (960, 384)}


def table(ref, name):
    start, length = TABLE_ROWS[name]
    return ref[pl.ds(start, length), :]


def three_parts(x):
    high = x.astype(bf16)
    rest = x - high.astype(f32)
    mid = rest.astype(bf16)
    low = (rest - mid.astype(f32)).astype(bf16)
    return jnp.concatenate([high, mid, low], axis=0)


def dot(a, b):
    return jnp.dot(a, b, preferred_element_type=f32)


def prepare_kernel(plan, tables, offsets, initial, stiffness, tables_out, record, springs, sem):
    copy = pltpu.make_async_copy(tables, tables_out, sem)
    copy.start()
    record[...] = jnp.zeros((1, PATCH), f32)
    for i in range(2):
        record[:, pl.ds(i * COLS, COLS)] = offsets[0, i].astype(f32)
        record[:, pl.ds((2 + i) * COLS, COLS)] = initial[0, i]
    level_id = lax.broadcasted_iota(jnp.int32, stiffness.shape, 1)
    for sweep in range(SWEEPS):
        picked = jnp.sum(jnp.where(level_id == plan[sweep], stiffness[...], 0.0), axis=1, keepdims=True)
        springs[pl.ds(2 * sweep, 2), :] = jnp.broadcast_to(picked, (2, PATCH))
    copy.wait()


def prepare(plan, offsets, initial, stiffness):
    tables = jnp.asarray(constant_tables())
    in_vmem = pl.BlockSpec(memory_space=pltpu.VMEM)
    anywhere = pl.BlockSpec(memory_space=pl.ANY)
    return pl.pallas_call(
        prepare_kernel,
        out_shape=[
            jax.ShapeDtypeStruct(tables.shape, bf16),
            jax.ShapeDtypeStruct((1, PATCH), f32),
            jax.ShapeDtypeStruct((8, PATCH), f32),
        ],
        in_specs=[pl.BlockSpec(memory_space=pltpu.SMEM), anywhere, in_vmem, in_vmem, in_vmem],
        out_specs=[in_vmem] * 3,
        scratch_shapes=[pltpu.SemaphoreType.DMA],
        compiler_params=pltpu.CompilerParams(vmem_limit_bytes=VMEM_LIMIT),
    )(plan, tables, offsets, initial, stiffness.T)


def section_spectra(upper, lower, tables):
    nyq_t = table(tables, "nyquist")
    nyq_t = jnp.concatenate([nyq_t[:, :PATCH], nyq_t[:, PATCH:]], axis=0)
    rows_t = jnp.concatenate([table(tables, "rows"), nyq_t], axis=1)
    columns = table(tables, "columns")
    lane = lax.broadcasted_iota(jnp.int32, (PATCH, PATCH), 1)
    nyquist = jnp.zeros((PATCH, PATCH), f32)
    stacked = []
    for m in range(PAIRS):
        span = 2 * PATCH if m < PAIRS - 1 else WIDTH - m * PATCH
        tile = jnp.concatenate([upper(m * PATCH, span), lower(m * PATCH, span)], axis=0)
        seg = dot(tile, rows_t[:span])
        nyquist = jnp.where(lane // 2 == m, seg[:, 2 * PATCH :], nyquist)
        seg = seg[:, : 2 * PATCH].astype(bf16)
        stacked.append(jnp.concatenate([seg[:, :PATCH], seg[:, PATCH:]], axis=0))
    spectra = []
    for m in range(0, PAIRS, 2):
        product = dot(columns, jnp.concatenate(stacked[m : m + 2], axis=1)).astype(bf16)
        spectra += [product[:, :PATCH], product[:, PATCH:]]
    spectra.append(dot(columns[:, :PATCH], nyquist.astype(bf16)).astype(bf16))
    return spectra


def energy(spectrum):
    wide = spectrum.astype(f32)
    return jnp.sum(wide * wide, axis=0, keepdims=True)


def block_tile(ref):
    return lambda start, span: ref[0, :, pl.ds(start, span)]


def own_kernel(own, below, tables, spec, energies):
    for m, spectrum in enumerate(section_spectra(block_tile(own), block_tile(below), tables)):
        spec[m] = spectrum
        energies[pl.ds(m, 1), :] = energy(spectrum)


def own_spectra(own, below, tables):
    in_vmem = pl.BlockSpec(memory_space=pltpu.VMEM)
    return pl.pallas_call(
        own_kernel,
        out_shape=[
            jax.ShapeDtypeStruct((PAIRS + 1, 2 * PATCH, PATCH), bf16),
            jax.ShapeDtypeStruct((2 * PAIRS, PATCH), f32),
        ],
        in_specs=[in_vmem] * 3,
        out_specs=[in_vmem] * 2,
        compiler_params=pltpu.CompilerParams(vmem_limit_bytes=VMEM_LIMIT),
        cost_estimate=pl.CostEstimate(flops=600_000_000, bytes_accessed=2_000_000, transcendentals=0),
    )(own, below, tables)


def flow_kernel(own_spec, own_energies, near, near_below, record, remote, tables, out, spec, lagged):
    spread = table(tables, "spread")
    energies = []
    for m, spectrum in enumerate(section_spectra(block_tile(near), block_tile(near_below), tables)):
        spec[m] = spectrum
        energies.append(energy(spectrum))

    lane = lax.broadcasted_iota(jnp.int32, (PAIRS, PATCH), 1)
    pair = lax.broadcasted_iota(jnp.int32, (PAIRS, PATCH), 0)
    own_pair = (lane % COLS) // 2 == pair
    first_16 = own_pair & (lane < COLS)
    weight = jnp.where(lane % HALF == 0, 1.0, 2.0)

    def halves(x):
        return x[:, :PATCH], x[:, PATCH:]

    def totals(main, extra):
        left = jnp.concatenate([main * weight, jnp.where(first_16, extra, 0.0)], axis=1)
        found = dot(three_parts(left), spread)
        found = found[:PAIRS] + found[PAIRS : 2 * PAIRS] + found[2 * PAIRS :]
        by_pair, by_patch = halves(found)
        by_patch = jnp.sum(jnp.where(first_16, by_patch, 0.0), axis=0, keepdims=True) + extra
        scale = 1.0 / (PATCH * PATCH)
        return jnp.sqrt(by_pair * scale + 1e-06), jnp.sqrt(by_patch * scale + 1e-06)

    low_pair, low_patch = totals(own_energies[pl.ds(0, PAIRS), :], own_energies[pl.ds(PAIRS, 1), :])
    up_pair, up_patch = totals(jnp.concatenate(energies[:PAIRS], axis=0), energies[PAIRS])
    floor_pair = floor_ratio * low_pair * up_pair
    floor_patch = floor_ratio * low_patch * up_patch

    for m in range(PAIRS + 1):
        floor = floor_pair[m : m + 1] if m < PAIRS else floor_patch
        low_re = own_spec[m, pl.ds(0, PATCH)].astype(f32)
        low_im = own_spec[m, pl.ds(PATCH, PATCH)].astype(f32)
        up_re = spec[m, pl.ds(0, PATCH)].astype(f32)
        up_im = spec[m, pl.ds(PATCH, PATCH)].astype(f32)
        cross_re = low_re * up_re + low_im * up_im
        cross_im = low_re * up_im - low_im * up_re
        square = cross_re * cross_re + cross_im * cross_im
        modulus = square * lax.rsqrt(jnp.maximum(square, 1e-36))
        inverse = 1.0 / (modulus + floor)
        white = jnp.concatenate([cross_re * inverse, cross_im * inverse], axis=0)
        high = white.astype(bf16)
        low = (white - high.astype(f32)).astype(bf16)
        found = dot(table(tables, "lag_y"), jnp.concatenate([high, low], axis=1))
        part = found[: 2 * SHIFTS, :PATCH] + found[: 2 * SHIFTS, PATCH:] + found[2 * SHIFTS :, :PATCH]
        lagged[pl.ds(m * SHIFTS, SHIFTS), pl.ds(0, PATCH)] = part[:SHIFTS]
        lagged[pl.ds(m * SHIFTS, SHIFTS), pl.ds(PATCH, PATCH)] = part[SHIFTS:]

    extra = lagged[pl.ds(PAIRS * SHIFTS, SHIFTS), pl.ds(0, PATCH)]
    extra = jnp.where(first_16[:, None, :], extra[None], 0.0).reshape(PAIRS * SHIFTS, PATCH)
    left = jnp.concatenate([lagged[pl.ds(0, PAIRS * SHIFTS), :], extra], axis=1)
    high = left.astype(bf16)
    low = (left - high.astype(f32)).astype(bf16)
    rows_all = PAIRS * SHIFTS
    found = dot(jnp.concatenate([high, low], axis=0), table(tables, "lag_x"))
    surface = found[:rows_all, :PATCH] + found[:rows_all, PATCH:] + found[rows_all:, :PATCH]
    surface = surface.reshape(PAIRS, SHIFTS, PATCH)

    rec = record[...]
    at_y = jnp.where(first_16, rec, 0.0)
    at_x = jnp.where(own_pair & (lane >= COLS) & (lane < 2 * COLS), rec, 0.0)
    gather = spread[:PATCH, PATCH:]
    shifts = lax.dot_general(
        jnp.concatenate([at_y, at_x], axis=0).astype(bf16),
        gather,
        (((1,), (1,)), ((), ())),
        preferred_element_type=f32,
    )
    lag_row = lax.broadcasted_iota(jnp.int32, (PAIRS, SHIFTS, PATCH), 1).astype(f32) - REACH
    lag_col = (lax.broadcasted_iota(jnp.int32, (PAIRS, SHIFTS, PATCH), 2) % HALF).astype(f32) - REACH
    dy = lag_row - shifts[:PAIRS][:, None, :]
    dx = lag_col - shifts[PAIRS:][:, None, :]
    mid_y, up_y, down_y = ((dy == k).astype(f32) for k in (0.0, 1.0, -1.0))
    mid_x, up_x, down_x = ((dx == k).astype(f32) for k in (0.0, 1.0, -1.0))
    at_mid_x = surface * mid_x
    at_mid_y = surface * mid_y
    picks = [
        jnp.sum(at_mid_x * (up_y - down_y), axis=1),
        jnp.sum(at_mid_x * (2.0 * mid_y - up_y - down_y), axis=1),
        jnp.sum(at_mid_y * (up_x - down_x), axis=1),
        jnp.sum(at_mid_y * (2.0 * mid_x - up_x - down_x), axis=1),
    ]
    found = dot(three_parts(jnp.concatenate(picks, axis=0)), gather)
    found = found[: 4 * PAIRS] + found[4 * PAIRS : 8 * PAIRS] + found[8 * PAIRS :]
    found = found.reshape(4, PAIRS, PATCH)
    found = jnp.sum(jnp.where(own_pair[None], found, 0.0), axis=1) * (1.0 / (PATCH * PATCH))
    lane_1 = lax.broadcasted_iota(jnp.int32, (1, PATCH), 1)
    slope = jnp.where(lane_1 < COLS, found[0:1], found[2:3])
    bend = jnp.where(lane_1 < COLS, found[1:2], found[3:4])
    flow = rec + 0.5 * slope / (1.0 + jnp.abs(bend))
    result = jnp.where(lane_1 < 2 * COLS, flow, rec)
    out[...] = jnp.broadcast_to(result, out.shape)
    for i in range(2):
        out[:, pl.ds((4 + i) * COLS, COLS)] = jnp.broadcast_to(remote[0, i], (out.shape[0], COLS))


def pair_flow(own_parts, near, near_below, record, remote_initial, tables, copies):
    operands = (*own_parts, near, near_below, record, remote_initial, tables)
    return pl.pallas_call(
        flow_kernel,
        out_shape=jax.ShapeDtypeStruct((copies, PATCH), f32),
        in_specs=[pl.BlockSpec(memory_space=pltpu.VMEM)] * len(operands),
        out_specs=pl.BlockSpec(memory_space=pltpu.VMEM),
        scratch_shapes=[
            pltpu.VMEM((PAIRS + 1, 2 * PATCH, PATCH), bf16),
            pltpu.VMEM(((PAIRS + 1) * SHIFTS, 2 * PATCH), f32),
        ],
        compiler_params=pltpu.CompilerParams(vmem_limit_bytes=VMEM_LIMIT),
    )(*operands)


def relax_kernel(springs, ring, other, flow_out, moving_out):
    sec = lax.axis_index("sec")
    row = lax.axis_index("row")
    last_row = lax.axis_size("row") - 1
    place = lax.rem(row, RING)
    base = row - place
    count = SECS * RING
    node = lax.broadcasted_iota(jnp.int32, (count, PATCH), 0)
    lane = lax.broadcasted_iota(jnp.int32, (count, PATCH), 1)
    in_ring = node % RING
    section = node // RING
    other_first = jnp.broadcast_to(place, (count, PATCH)) < RING // 2
    valid = (section < SECS - 1) & (lane < 2 * COLS)
    valid_up = valid.astype(f32)
    has_left = (lane % COLS > 0).astype(f32)
    has_right = (lane % COLS < COLS - 1).astype(f32)
    row_here = base + in_ring
    row_other = row_here + jnp.where(other_first, -RING, RING)
    at_rows = (row_here, row_other)
    has_up = [(r > 0).astype(f32) for r in at_rows]
    has_down = [(r < last_row).astype(f32) for r in at_rows]
    first = in_ring == 0
    final = in_ring == RING - 1
    here = ring[...]
    beyond = other[...]
    flows = [jnp.where(valid, b, 0.0) for b in (here, beyond)]
    moving = [pltpu.roll(b, PATCH - 2 * COLS, 1) for b in (here, beyond)]
    third = pltpu.roll(here, PATCH - 4 * COLS, 1)

    def moved(x, by):
        by = by % count
        return jnp.concatenate([x[by:], x[:by]], axis=0)

    for sweep in range(SWEEPS):
        spring = springs[pl.ds(2 * sweep, 1), :]
        tether = springs[pl.ds(2 * sweep + 1, 1), :]
        near_x, far_x = moving
        edge_above = jnp.where(other_first, moved(far_x, RING - 1), moved(third, RING - 1))
        edge_below = jnp.where(other_first, moved(third, 1 - RING), moved(far_x, 1 - RING))
        above = (jnp.where(first, edge_above, moved(near_x, -1)), jnp.where(first, moved(near_x, RING - 1), moved(far_x, -1)))
        below = (jnp.where(final, edge_below, moved(near_x, 1)), jnp.where(final, moved(near_x, 1 - RING), moved(far_x, 1)))
        fresh = []
        for k, x in enumerate(moving):
            col_left = pltpu.roll(x, 1, 1)
            col_right = pltpu.roll(x, PATCH - 1, 1)
            laplace = (
                (above[k] - x) * has_up[k]
                + (below[k] - x) * has_down[k]
                + (col_left - x) * has_left
                + (col_right - x) * has_right
            )
            residual = (moved(x, RING) - x - flows[k]) * valid_up
            below_res = jnp.where(section == 0, 0.0, moved(residual, -RING))
            fresh.append(x + step_size * (spring * laplace + tether * (residual - below_res)))
        moving = fresh

    mine = (section == sec) & (in_ring == place)
    for x, ref in ((flows[0], flow_out), (moving[0], moving_out)):
        line = jnp.sum(jnp.where(mine, x, 0.0), axis=0, keepdims=True)
        ref[0, 0] = line[:, :COLS]
        ref[0, 1] = line[:, COLS : 2 * COLS]


def relax(springs, ring, other, shape):
    in_vmem = pl.BlockSpec(memory_space=pltpu.VMEM)
    return pl.pallas_call(
        relax_kernel,
        out_shape=[jax.ShapeDtypeStruct(shape, f32)] * 2,
        in_specs=[in_vmem] * 3,
        out_specs=[in_vmem] * 2,
        compiler_params=pltpu.CompilerParams(vmem_limit_bytes=VMEM_LIMIT),
    )(springs, ring, other)


def shifted(block, axis, distance):
    devices = range(lax.axis_size(axis))
    route = [(i - distance, i) for i in devices if i - distance in devices]
    return lax.ppermute(block, axis, route)


def ring_route(rows, outward):
    route = []
    for r in range(rows):
        step = RING if (r % RING < RING // 2) == outward else -RING
        if 0 <= r - step < rows:
            route.append((r - step, r))
    return route


def per_device(images, initial, offsets, stiffness, plan):
    rows = lax.axis_size("row")
    below = shifted(images, "row", -1)
    remote_initial = lax.ppermute(initial, "row", ring_route(rows, False))
    near = shifted(images, "sec", -1)
    tables, record, springs = prepare(plan, offsets, initial, stiffness)
    below, remote_initial, tables, record, springs = lax.optimization_barrier(
        (below, remote_initial, tables, record, springs)
    )
    near_below = shifted(below, "sec", -1)
    count = SECS * RING
    own_parts = own_spectra(images, below, tables)
    mine = pair_flow(own_parts, near, near_below, record, remote_initial, tables, count)
    groups = [
        [s * rows + RING * g + j for s in range(SECS) for j in range(RING)] for g in range(rows // RING)
    ]
    ring = lax.all_to_all(mine.reshape(count, 1, PATCH), ("sec", "row"), 0, 0, axis_index_groups=groups)
    other = lax.ppermute(ring, "row", ring_route(rows, True))
    return tuple(
        relax(springs, ring.reshape(count, PATCH), other.reshape(count, PATCH), initial.shape)
    )


def solution(mesh):
    return jax.shard_map(
        per_device,
        mesh=mesh,
        in_specs=(
            P("sec", "row", None),
            P("sec", None, "row", None),
            P("sec", None, "row", None),
            P(),
            P(),
        ),
        out_specs=(P("sec", None, "row", None), P("sec", None, "row", None)),
        check_vma=False,
    )
```

```python
import math

import numpy as np
import jax
import jax.numpy as jnp
from jax import lax
from jax.experimental import pallas as pl
from jax.experimental.pallas import tpu as pltpu
from jax.sharding import PartitionSpec as P
import ml_dtypes

PATCH = 128
STRIDE = 64
HALF = 64
SWEEPS = 3
COLS = 16
PAIRS = 8
SECS = 4
RING = 4
SHIFTS = 16
REACH = 5
WIDTH = 1088

step_size = 0.2
floor_ratio = 0.2

VMEM_LIMIT = 24 * 1024 * 1024
PREPARE_FLOPS = 1_000_000_000

f32 = jnp.float32
bf16 = jnp.bfloat16


def dft_halves():
    freq = np.arange(PATCH)
    phase = freq[:, None] * freq[None, :] % PATCH
    folded = np.minimum(phase, PATCH - phase)
    angle = folded * (2.0 * math.pi / PATCH)
    sine = np.sin(angle) * np.where(2 * phase > PATCH, -1.0, 1.0)
    sine = np.where(2 * folded == PATCH, 0.0, sine)
    cosine = np.cos(angle)
    cosine = np.where(4 * folded == PATCH, np.cos(np.float32(math.pi / 2)), cosine)
    return cosine.astype(ml_dtypes.bfloat16), (-sine).astype(ml_dtypes.bfloat16)


def two_parts(table):
    high = table.astype(ml_dtypes.bfloat16)
    low = (table - high.astype(np.float64)).astype(ml_dtypes.bfloat16)
    return high, low


def constant_tables():
    cos_t, sin_t = dft_halves()
    cos_f = cos_t.astype(np.float32)
    sin_f = sin_t.astype(np.float32)
    rows = np.zeros((2 * PATCH, 2 * PATCH), np.float32)
    rows[0:PATCH, 0:HALF] = cos_f[:HALF].T
    rows[0:PATCH, PATCH : PATCH + HALF] = sin_f[:HALF].T
    rows[HALF : HALF + PATCH, HALF:PATCH] = cos_f[:HALF].T
    rows[HALF : HALF + PATCH, PATCH + HALF :] = sin_f[:HALF].T
    nyquist = np.zeros((2 * PATCH, PATCH), np.float32)
    nyquist[0:PATCH, 0::2] = cos_f[HALF][:, None]
    nyquist[HALF : HALF + PATCH, 1::2] = cos_f[HALF][:, None]
    columns = np.block([[cos_f, -sin_f], [sin_f, cos_f]])
    lags = np.arange(SHIFTS) - REACH
    used = (np.arange(SHIFTS) <= 2 * REACH).astype(np.float64)
    freq = np.arange(PATCH)
    turn = (freq[None, :] * lags[:, None] % PATCH) * (2.0 * math.pi / PATCH)
    cos_y = np.cos(turn) * used[:, None]
    sin_y = np.sin(turn) * used[:, None]
    high, low = two_parts(np.block([[cos_y, -sin_y], [sin_y, cos_y]]))
    lag_y = np.concatenate([high, low], axis=0)
    weight = np.where(freq[:HALF] == 0, 1.0, 2.0)
    across = np.zeros((3 * PATCH, PATCH))
    for p in range(2):
        cols = slice(p * HALF, p * HALF + SHIFTS)
        block = slice(p * HALF, (p + 1) * HALF)
        across[:PATCH][block, cols] = (cos_y[:, :HALF] * weight).T
        across[PATCH : 2 * PATCH][block, cols] = (-sin_y[:, :HALF] * weight).T
        for c in range(p, COLS, 2):
            across[2 * PATCH + c, cols] = np.where(lags % 2 == 0, 1.0, -1.0) * used
    high, low = two_parts(across)
    lag_x = np.concatenate([high, low], axis=1)
    lane = np.arange(PATCH)
    patch = (lane % COLS % 2)[None, :] == (lane // HALF)[:, None]
    gather = (patch & (lane < 2 * COLS)[None, :]).astype(np.float32)
    single = (patch & (lane < COLS)[None, :]).astype(np.float32)
    same = ((lane // HALF)[:, None] == (lane // HALF)[None, :]).astype(np.float32)
    blank = np.zeros((PATCH, PATCH), np.float32)
    spread = np.block([[same, gather], [single.T, blank]])
    turned = np.roll(columns.reshape(2 * PATCH, 2, PATCH), HALF, axis=2).reshape(2 * PATCH, 2 * PATCH)
    packed = [rows, np.concatenate([nyquist[:PATCH], nyquist[PATCH:]], axis=1), spread, lag_y, lag_x, columns, turned]
    return np.concatenate([np.asarray(t).astype(ml_dtypes.bfloat16) for t in packed], axis=0)


TABLE_ROWS = {"rows": (0, 256), "nyquist": (256, 128), "spread": (384, 256)}
TABLE_ROWS |= {"lag_y": (640, 64), "lag_x": (704, 384), "columns": (1088, 256), "turned": (1344, 256)}


def table(ref, name):
    start, length = TABLE_ROWS[name]
    return ref[pl.ds(start, length), :]


def three_parts(x):
    high = x.astype(bf16)
    rest = x - high.astype(f32)
    mid = rest.astype(bf16)
    low = (rest - mid.astype(f32)).astype(bf16)
    return jnp.concatenate([high, mid, low], axis=0)


def dot(a, b):
    return jnp.dot(a, b, preferred_element_type=f32)


def takes_row_above(sec):
    return sec < 2


def is_ring_head(sec, row):
    return takes_row_above(sec) & (lax.rem(row, RING) == 0)


def prepare_kernel(plan, offsets, initial, stiffness, record, springs):
    record[...] = jnp.zeros((1, PATCH), f32)
    for i in range(2):
        record[:, pl.ds(i * COLS, COLS)] = offsets[0, i].astype(f32)
        record[:, pl.ds((2 + i) * COLS, COLS)] = initial[0, i]
    level_id = lax.broadcasted_iota(jnp.int32, stiffness.shape, 1)
    for sweep in range(SWEEPS):
        picked = jnp.sum(jnp.where(level_id == plan[sweep], stiffness[...], 0.0), axis=1, keepdims=True)
        springs[pl.ds(2 * sweep, 2), :] = jnp.broadcast_to(picked, (2, PATCH))


def prepare(plan, offsets, initial, stiffness):
    in_vmem = pl.BlockSpec(memory_space=pltpu.VMEM)
    return pl.pallas_call(
        prepare_kernel,
        out_shape=[jax.ShapeDtypeStruct((1, PATCH), f32), jax.ShapeDtypeStruct((8, PATCH), f32)],
        in_specs=[pl.BlockSpec(memory_space=pltpu.SMEM), in_vmem, in_vmem, in_vmem],
        out_specs=[in_vmem] * 2,
        compiler_params=pltpu.CompilerParams(vmem_limit_bytes=VMEM_LIMIT),
        cost_estimate=pl.CostEstimate(flops=PREPARE_FLOPS, bytes_accessed=10_000, transcendentals=0),
    )(plan, offsets, initial, stiffness.T)


def section_spectra(first, second, tables):
    nyq_t = table(tables, "nyquist")
    nyq_t = jnp.concatenate([nyq_t[:, :PATCH], nyq_t[:, PATCH:]], axis=0)
    rows_t = jnp.concatenate([table(tables, "rows"), nyq_t], axis=1)
    downward = takes_row_above(lax.axis_index("sec"))
    columns = jnp.where(
        jnp.broadcast_to(downward, (2 * PATCH, 2 * PATCH)), table(tables, "turned"), table(tables, "columns")
    )
    lane = lax.broadcasted_iota(jnp.int32, (PATCH, PATCH), 1)
    nyquist = jnp.zeros((PATCH, PATCH), f32)
    stacked = []
    for m in range(PAIRS):
        span = 2 * PATCH if m < PAIRS - 1 else WIDTH - m * PATCH
        tile = jnp.concatenate([first(m * PATCH, span), second(m * PATCH, span)], axis=0)
        seg = dot(tile, rows_t[:span])
        nyquist = jnp.where(lane // 2 == m, seg[:, 2 * PATCH :], nyquist)
        seg = seg[:, : 2 * PATCH].astype(bf16)
        stacked.append(jnp.concatenate([seg[:, :PATCH], seg[:, PATCH:]], axis=0))
    spectra = []
    for m in range(0, PAIRS, 2):
        product = dot(columns, jnp.concatenate(stacked[m : m + 2], axis=1)).astype(bf16)
        spectra += [product[:, :PATCH], product[:, PATCH:]]
    spectra.append(dot(columns[:, :PATCH], nyquist.astype(bf16)).astype(bf16))
    return spectra


def energy(spectrum):
    wide = spectrum.astype(f32)
    return jnp.sum(wide * wide, axis=0, keepdims=True)


def block_tile(ref):
    return lambda start, span: ref[0, :, pl.ds(start, span)]


def own_kernel(images, head, across, tables, spec, energies):
    at_head = is_ring_head(lax.axis_index("sec"), lax.axis_index("row"))

    def own(start, span):
        here = images[0, :, pl.ds(start, span)]
        return jnp.where(jnp.broadcast_to(at_head, here.shape), head[0, :, pl.ds(start, span)], here)

    for m, spectrum in enumerate(section_spectra(own, block_tile(across), tables)):
        spec[m] = spectrum
        energies[pl.ds(m, 1), :] = energy(spectrum)


def own_spectra(images, head, across, tables):
    in_vmem = pl.BlockSpec(memory_space=pltpu.VMEM)
    return pl.pallas_call(
        own_kernel,
        out_shape=[
            jax.ShapeDtypeStruct((PAIRS + 1, 2 * PATCH, PATCH), bf16),
            jax.ShapeDtypeStruct((2 * PAIRS, PATCH), f32),
        ],
        in_specs=[in_vmem] * 4,
        out_specs=[in_vmem] * 2,
        compiler_params=pltpu.CompilerParams(vmem_limit_bytes=VMEM_LIMIT),
        cost_estimate=pl.CostEstimate(flops=600_000_000, bytes_accessed=2_000_000, transcendentals=0),
    )(images, head, across, tables)


def flow_kernel(
    own_spec, own_energies, near, near_far, near_across, record, remote, far_offsets, tables, out, spec, lagged, shift_row
):
    spread = table(tables, "spread")
    energies = []

    def second(start, span):
        return near_far[0, :, pl.ds(start, span)] + near_across[0, :, pl.ds(start, span)]

    for m, spectrum in enumerate(section_spectra(block_tile(near), second, tables)):
        spec[m] = spectrum
        energies.append(energy(spectrum))

    lane = lax.broadcasted_iota(jnp.int32, (PAIRS, PATCH), 1)
    pair = lax.broadcasted_iota(jnp.int32, (PAIRS, PATCH), 0)
    own_pair = (lane % COLS) // 2 == pair
    first_16 = own_pair & (lane < COLS)
    weight = jnp.where(lane % HALF == 0, 1.0, 2.0)

    def halves(x):
        return x[:, :PATCH], x[:, PATCH:]

    def totals(main, extra):
        left = jnp.concatenate([main * weight, jnp.where(first_16, extra, 0.0)], axis=1)
        found = dot(three_parts(left), spread)
        found = found[:PAIRS] + found[PAIRS : 2 * PAIRS] + found[2 * PAIRS :]
        by_pair, by_patch = halves(found)
        by_patch = jnp.sum(jnp.where(first_16, by_patch, 0.0), axis=0, keepdims=True) + extra
        scale = 1.0 / (PATCH * PATCH)
        return jnp.sqrt(by_pair * scale + 1e-06), jnp.sqrt(by_patch * scale + 1e-06)

    low_pair, low_patch = totals(own_energies[pl.ds(0, PAIRS), :], own_energies[pl.ds(PAIRS, 1), :])
    up_pair, up_patch = totals(jnp.concatenate(energies[:PAIRS], axis=0), energies[PAIRS])
    floor_pair = floor_ratio * low_pair * up_pair
    floor_patch = floor_ratio * low_patch * up_patch

    for m in range(PAIRS + 1):
        floor = floor_pair[m : m + 1] if m < PAIRS else floor_patch
        low_re = own_spec[m, pl.ds(0, PATCH)].astype(f32)
        low_im = own_spec[m, pl.ds(PATCH, PATCH)].astype(f32)
        up_re = spec[m, pl.ds(0, PATCH)].astype(f32)
        up_im = spec[m, pl.ds(PATCH, PATCH)].astype(f32)
        cross_re = low_re * up_re + low_im * up_im
        cross_im = low_re * up_im - low_im * up_re
        square = cross_re * cross_re + cross_im * cross_im
        modulus = square * lax.rsqrt(jnp.maximum(square, 1e-36))
        inverse = 1.0 / (modulus + floor)
        white = jnp.concatenate([cross_re * inverse, cross_im * inverse], axis=0)
        high = white.astype(bf16)
        low = (white - high.astype(f32)).astype(bf16)
        found = dot(table(tables, "lag_y"), jnp.concatenate([high, low], axis=1))
        part = found[: 2 * SHIFTS, :PATCH] + found[: 2 * SHIFTS, PATCH:] + found[2 * SHIFTS :, :PATCH]
        lagged[pl.ds(m * SHIFTS, SHIFTS), pl.ds(0, PATCH)] = part[:SHIFTS]
        lagged[pl.ds(m * SHIFTS, SHIFTS), pl.ds(PATCH, PATCH)] = part[SHIFTS:]

    extra = lagged[pl.ds(PAIRS * SHIFTS, SHIFTS), pl.ds(0, PATCH)]
    extra = jnp.where(first_16[:, None, :], extra[None], 0.0).reshape(PAIRS * SHIFTS, PATCH)
    left = jnp.concatenate([lagged[pl.ds(0, PAIRS * SHIFTS), :], extra], axis=1)
    high = left.astype(bf16)
    low = (left - high.astype(f32)).astype(bf16)
    rows_all = PAIRS * SHIFTS
    found = dot(jnp.concatenate([high, low], axis=0), table(tables, "lag_x"))
    surface = found[:rows_all, :PATCH] + found[:rows_all, PATCH:] + found[rows_all:, :PATCH]
    surface = surface.reshape(PAIRS, SHIFTS, PATCH)

    for i in range(2):
        shift_row[:, pl.ds(i * COLS, COLS)] = far_offsets[0, i].astype(f32)
    rec = record[...]
    lane_1 = lax.broadcasted_iota(jnp.int32, (1, PATCH), 1)
    downward = jnp.broadcast_to(takes_row_above(lax.axis_index("sec")), (1, PATCH))
    rec = jnp.where(downward & (lane_1 < 2 * COLS), shift_row[...], rec)
    at_y = jnp.where(first_16, rec, 0.0)
    at_x = jnp.where(own_pair & (lane >= COLS) & (lane < 2 * COLS), rec, 0.0)
    gather = spread[:PATCH, PATCH:]
    shifts = lax.dot_general(
        jnp.concatenate([at_y, at_x], axis=0).astype(bf16),
        gather,
        (((1,), (1,)), ((), ())),
        preferred_element_type=f32,
    )
    lag_row = lax.broadcasted_iota(jnp.int32, (PAIRS, SHIFTS, PATCH), 1).astype(f32) - REACH
    lag_col = (lax.broadcasted_iota(jnp.int32, (PAIRS, SHIFTS, PATCH), 2) % HALF).astype(f32) - REACH
    dy = lag_row - shifts[:PAIRS][:, None, :]
    dx = lag_col - shifts[PAIRS:][:, None, :]
    mid_y, up_y, down_y = ((dy == k).astype(f32) for k in (0.0, 1.0, -1.0))
    mid_x, up_x, down_x = ((dx == k).astype(f32) for k in (0.0, 1.0, -1.0))
    at_mid_x = surface * mid_x
    at_mid_y = surface * mid_y
    picks = [
        jnp.sum(at_mid_x * (up_y - down_y), axis=1),
        jnp.sum(at_mid_x * (2.0 * mid_y - up_y - down_y), axis=1),
        jnp.sum(at_mid_y * (up_x - down_x), axis=1),
        jnp.sum(at_mid_y * (2.0 * mid_x - up_x - down_x), axis=1),
    ]
    found = dot(three_parts(jnp.concatenate(picks, axis=0)), gather)
    found = found[: 4 * PAIRS] + found[4 * PAIRS : 8 * PAIRS] + found[8 * PAIRS :]
    found = found.reshape(4, PAIRS, PATCH)
    found = jnp.sum(jnp.where(own_pair[None], found, 0.0), axis=1) * (1.0 / (PATCH * PATCH))
    slope = jnp.where(lane_1 < COLS, found[0:1], found[2:3])
    bend = jnp.where(lane_1 < COLS, found[1:2], found[3:4])
    flow = rec + 0.5 * slope / (1.0 + jnp.abs(bend))
    result = jnp.where(lane_1 < 2 * COLS, flow, rec)
    out[...] = jnp.broadcast_to(result, out.shape)
    for i in range(2):
        out[:, pl.ds((4 + i) * COLS, COLS)] = jnp.broadcast_to(remote[0, i], (out.shape[0], COLS))


def pair_flow(own_parts, blocks, record, remote_initial, far_offsets, tables, copies):
    operands = (*own_parts, *blocks, record, remote_initial, far_offsets, tables)
    return pl.pallas_call(
        flow_kernel,
        out_shape=jax.ShapeDtypeStruct((copies, PATCH), f32),
        in_specs=[pl.BlockSpec(memory_space=pltpu.VMEM)] * len(operands),
        out_specs=pl.BlockSpec(memory_space=pltpu.VMEM),
        scratch_shapes=[
            pltpu.VMEM((PAIRS + 1, 2 * PATCH, PATCH), bf16),
            pltpu.VMEM(((PAIRS + 1) * SHIFTS, 2 * PATCH), f32),
            pltpu.VMEM((1, PATCH), f32),
        ],
        compiler_params=pltpu.CompilerParams(vmem_limit_bytes=VMEM_LIMIT),
    )(*operands)


def relax_kernel(springs, ring, other, flow_out, moving_out):
    sec = lax.axis_index("sec")
    row = lax.axis_index("row")
    last_row = lax.axis_size("row") - 1
    place = lax.rem(row, RING)
    base = row - place
    count = SECS * RING
    node = lax.broadcasted_iota(jnp.int32, (count, PATCH), 0)
    lane = lax.broadcasted_iota(jnp.int32, (count, PATCH), 1)
    in_ring = node % RING
    section = node // RING
    other_first = jnp.broadcast_to(place, (count, PATCH)) < RING // 2
    valid = (section < SECS - 1) & (lane < 2 * COLS)
    valid_up = valid.astype(f32)
    has_left = (lane % COLS > 0).astype(f32)
    has_right = (lane % COLS < COLS - 1).astype(f32)
    row_here = base + in_ring
    row_other = row_here + jnp.where(other_first, -RING, RING)
    at_rows = (row_here, row_other)
    has_up = [(r > 0).astype(f32) for r in at_rows]
    has_down = [(r < last_row).astype(f32) for r in at_rows]
    first = in_ring == 0
    final = in_ring == RING - 1
    here = ring[...]
    beyond = other[...]
    moving = [pltpu.roll(b, PATCH - 2 * COLS, 1) for b in (here, beyond)]
    third = pltpu.roll(here, PATCH - 4 * COLS, 1)

    def moved(x, by):
        by = by % count
        return jnp.concatenate([x[by:], x[:by]], axis=0)

    flows = []
    for b in (here, beyond):
        found = jnp.where(takes_row_above(section), jnp.where(final, moved(b, 1 - RING), moved(b, 1)), b)
        flows.append(jnp.where(valid, found, 0.0))

    for sweep in range(SWEEPS):
        spring = springs[pl.ds(2 * sweep, 1), :]
        tether = springs[pl.ds(2 * sweep + 1, 1), :]
        near_x, far_x = moving
        edge_above = jnp.where(other_first, moved(far_x, RING - 1), moved(third, RING - 1))
        edge_below = jnp.where(other_first, moved(third, 1 - RING), moved(far_x, 1 - RING))
        above = (jnp.where(first, edge_above, moved(near_x, -1)), jnp.where(first, moved(near_x, RING - 1), moved(far_x, -1)))
        below = (jnp.where(final, edge_below, moved(near_x, 1)), jnp.where(final, moved(near_x, 1 - RING), moved(far_x, 1)))
        fresh = []
        for k, x in enumerate(moving):
            col_left = pltpu.roll(x, 1, 1)
            col_right = pltpu.roll(x, PATCH - 1, 1)
            laplace = (
                (above[k] - x) * has_up[k]
                + (below[k] - x) * has_down[k]
                + (col_left - x) * has_left
                + (col_right - x) * has_right
            )
            residual = (moved(x, RING) - x - flows[k]) * valid_up
            below_res = jnp.where(section == 0, 0.0, moved(residual, -RING))
            fresh.append(x + step_size * (spring * laplace + tether * (residual - below_res)))
        moving = fresh

    mine = (section == sec) & (in_ring == place)
    for x, ref in ((flows[0], flow_out), (moving[0], moving_out)):
        line = jnp.sum(jnp.where(mine, x, 0.0), axis=0, keepdims=True)
        ref[0, 0] = line[:, :COLS]
        ref[0, 1] = line[:, COLS : 2 * COLS]


def relax(springs, ring, other, shape):
    in_vmem = pl.BlockSpec(memory_space=pltpu.VMEM)
    return pl.pallas_call(
        relax_kernel,
        out_shape=[jax.ShapeDtypeStruct(shape, f32)] * 2,
        in_specs=[in_vmem] * 3,
        out_specs=[in_vmem] * 2,
        compiler_params=pltpu.CompilerParams(vmem_limit_bytes=VMEM_LIMIT),
    )(springs, ring, other)


def shifted(block, axis, distance):
    devices = range(lax.axis_size(axis))
    route = [(i - distance, i) for i in devices if i - distance in devices]
    return lax.ppermute(block, axis, route)


def ring_route(rows, outward):
    route = []
    for r in range(rows):
        step = RING if (r % RING < RING // 2) == outward else -RING
        if 0 <= r - step < rows:
            route.append((r - step, r))
    return route


def image_routes(rows):
    at = lambda s, r: s * rows + r
    across, near, far, head, shifts = [], [], [], [], []
    for r in range(rows):
        ring_head = r % RING == 0
        above = r + RING - 1 if ring_head else r - 1
        for s in range(SECS):
            if takes_row_above(s):
                across.append((at(s, above), at(s, r)))
                shifts.append((at(s, above), at(s, r)))
                beside = r + RING if ring_head else r
                if beside < rows:
                    near.append((at(s + 1, beside), at(s, r)))
                    if ring_head:
                        head.append((at(s, beside), at(s, r)))
                if s == 1:
                    far.append((at(2, above), at(1, r)))
            else:
                if r < rows - 1:
                    across.append((at(s, r + 1), at(s, r)))
                if s == 2:
                    near.append((at(3, r), at(2, r)))
    return across, near, far, head, shifts


def per_device(images, initial, offsets, stiffness, plan):
    rows = lax.axis_size("row")
    both = ("sec", "row")
    across_route, near_route, far_route, head_route, shift_route = image_routes(rows)
    across = lax.ppermute(images, both, across_route)
    near = lax.ppermute(images, both, near_route)
    near_far = lax.ppermute(images, both, far_route)
    head = lax.ppermute(images, both, head_route)
    far_offsets = lax.ppermute(offsets, both, shift_route)
    remote_initial = lax.ppermute(initial, "row", ring_route(rows, False))
    record, springs = prepare(plan, offsets, initial, stiffness)
    across, near_far, head, far_offsets, remote_initial, record, springs = lax.optimization_barrier(
        (across, near_far, head, far_offsets, remote_initial, record, springs)
    )
    near_across = lax.ppermute(across, "sec", [(1, 0), (3, 2)])
    count = SECS * RING
    tables = jnp.asarray(constant_tables())
    own_parts = own_spectra(images, head, across, tables)
    mine = pair_flow(
        own_parts, (near, near_far, near_across), record, remote_initial, far_offsets, tables, count
    )
    groups = [
        [s * rows + RING * g + j for s in range(SECS) for j in range(RING)] for g in range(rows // RING)
    ]
    ring = lax.all_to_all(mine.reshape(count, 1, PATCH), both, 0, 0, axis_index_groups=groups)
    other = lax.ppermute(ring, "row", ring_route(rows, True))
    return tuple(relax(springs, ring.reshape(count, PATCH), other.reshape(count, PATCH), initial.shape))


def solution(mesh):
    return jax.shard_map(
        per_device,
        mesh=mesh,
        in_specs=(
            P("sec", "row", None),
            P("sec", None, "row", None),
            P("sec", None, "row", None),
            P(),
            P(),
        ),
        out_specs=(P("sec", None, "row", None), P("sec", None, "row", None)),
        check_vma=False,
    )
```

```python
import math

import numpy as np
import jax
import jax.numpy as jnp
from jax import lax
from jax.experimental import pallas as pl
from jax.experimental.pallas import tpu as pltpu
from jax.sharding import PartitionSpec as P
import ml_dtypes

PATCH = 128
STRIDE = 64
HALF = 64
SWEEPS = 3
COLS = 16
PAIRS = 8
SECS = 4
RING = 4
SHIFTS = 16
REACH = 5
WIDTH = 1088

step_size = 0.2
floor_ratio = 0.2

VMEM_LIMIT = 24 * 1024 * 1024
PREPARE_FLOPS = 1_000_000_000

f32 = jnp.float32
bf16 = jnp.bfloat16


def dft_halves():
    freq = np.arange(PATCH)
    phase = freq[:, None] * freq[None, :] % PATCH
    folded = np.minimum(phase, PATCH - phase)
    angle = folded * (2.0 * math.pi / PATCH)
    sine = np.sin(angle) * np.where(2 * phase > PATCH, -1.0, 1.0)
    sine = np.where(2 * folded == PATCH, 0.0, sine)
    cosine = np.cos(angle)
    cosine = np.where(4 * folded == PATCH, np.cos(np.float32(math.pi / 2)), cosine)
    return cosine.astype(ml_dtypes.bfloat16), (-sine).astype(ml_dtypes.bfloat16)


def two_parts(table):
    high = table.astype(ml_dtypes.bfloat16)
    low = (table - high.astype(np.float64)).astype(ml_dtypes.bfloat16)
    return high, low


def constant_tables():
    cos_t, sin_t = dft_halves()
    cos_f = cos_t.astype(np.float32)
    sin_f = sin_t.astype(np.float32)
    rows = np.zeros((2 * PATCH, 2 * PATCH), np.float32)
    rows[0:PATCH, 0:HALF] = cos_f[:HALF].T
    rows[0:PATCH, PATCH : PATCH + HALF] = sin_f[:HALF].T
    rows[HALF : HALF + PATCH, HALF:PATCH] = cos_f[:HALF].T
    rows[HALF : HALF + PATCH, PATCH + HALF :] = sin_f[:HALF].T
    nyquist = np.zeros((2 * PATCH, PATCH), np.float32)
    nyquist[0:PATCH, 0::2] = cos_f[HALF][:, None]
    nyquist[HALF : HALF + PATCH, 1::2] = cos_f[HALF][:, None]
    columns = np.block([[cos_f, -sin_f], [sin_f, cos_f]])
    lags = np.arange(SHIFTS) - REACH
    used = (np.arange(SHIFTS) <= 2 * REACH).astype(np.float64)
    freq = np.arange(PATCH)
    turn = (freq[None, :] * lags[:, None] % PATCH) * (2.0 * math.pi / PATCH)
    cos_y = np.cos(turn) * used[:, None]
    sin_y = np.sin(turn) * used[:, None]
    high, low = two_parts(np.block([[cos_y, -sin_y], [sin_y, cos_y]]))
    lag_y = np.concatenate([high, low], axis=0)
    weight = np.where(freq[:HALF] == 0, 1.0, 2.0)
    across = np.zeros((3 * PATCH, PATCH))
    for p in range(2):
        cols = slice(p * HALF, p * HALF + SHIFTS)
        block = slice(p * HALF, (p + 1) * HALF)
        across[:PATCH][block, cols] = (cos_y[:, :HALF] * weight).T
        across[PATCH : 2 * PATCH][block, cols] = (-sin_y[:, :HALF] * weight).T
        for c in range(p, COLS, 2):
            across[2 * PATCH + c, cols] = np.where(lags % 2 == 0, 1.0, -1.0) * used
    high, low = two_parts(across)
    lag_x = np.concatenate([high, low], axis=1)
    lane = np.arange(PATCH)
    patch = (lane % COLS % 2)[None, :] == (lane // HALF)[:, None]
    gather = (patch & (lane < 2 * COLS)[None, :]).astype(np.float32)
    single = (patch & (lane < COLS)[None, :]).astype(np.float32)
    same = ((lane // HALF)[:, None] == (lane // HALF)[None, :]).astype(np.float32)
    blank = np.zeros((PATCH, PATCH), np.float32)
    spread = np.block([[same, gather], [single.T, blank]])
    packed = [rows, np.concatenate([nyquist[:PATCH], nyquist[PATCH:]], axis=1), columns, spread, lag_y, lag_x]
    return np.concatenate([np.asarray(t).astype(ml_dtypes.bfloat16) for t in packed], axis=0)


TABLE_ROWS = {"rows": (0, 256), "nyquist": (256, 128), "columns": (384, 256), "spread": (640, 256)}
TABLE_ROWS |= {"lag_y": (896, 64), "lag_x": (960, 384)}


def table(ref, name):
    start, length = TABLE_ROWS[name]
    return ref[pl.ds(start, length), :]


def three_parts(x):
    high = x.astype(bf16)
    rest = x - high.astype(f32)
    mid = rest.astype(bf16)
    low = (rest - mid.astype(f32)).astype(bf16)
    return jnp.concatenate([high, mid, low], axis=0)


def dot(a, b):
    return jnp.dot(a, b, preferred_element_type=f32)


def prepare_kernel(plan, initial, stiffness, record, springs):
    record[...] = jnp.zeros((1, PATCH), f32)
    for i in range(2):
        record[:, pl.ds((2 + i) * COLS, COLS)] = initial[0, i]
    level_id = lax.broadcasted_iota(jnp.int32, stiffness.shape, 1)
    for sweep in range(SWEEPS):
        picked = jnp.sum(jnp.where(level_id == plan[sweep], stiffness[...], 0.0), axis=1, keepdims=True)
        springs[pl.ds(2 * sweep, 2), :] = jnp.broadcast_to(picked, (2, PATCH))


def prepare(plan, initial, stiffness):
    in_vmem = pl.BlockSpec(memory_space=pltpu.VMEM)
    return pl.pallas_call(
        prepare_kernel,
        out_shape=[jax.ShapeDtypeStruct((1, PATCH), f32), jax.ShapeDtypeStruct((8, PATCH), f32)],
        in_specs=[pl.BlockSpec(memory_space=pltpu.SMEM), in_vmem, in_vmem],
        out_specs=[in_vmem] * 2,
        compiler_params=pltpu.CompilerParams(vmem_limit_bytes=VMEM_LIMIT),
        cost_estimate=pl.CostEstimate(flops=PREPARE_FLOPS, bytes_accessed=10_000, transcendentals=0),
    )(plan, initial, stiffness.T)


def section_spectra(upper, lower, tables):
    nyq_t = table(tables, "nyquist")
    nyq_t = jnp.concatenate([nyq_t[:, :PATCH], nyq_t[:, PATCH:]], axis=0)
    rows_t = jnp.concatenate([table(tables, "rows"), nyq_t], axis=1)
    columns = table(tables, "columns")
    lane = lax.broadcasted_iota(jnp.int32, (PATCH, PATCH), 1)
    nyquist = jnp.zeros((PATCH, PATCH), f32)
    stacked = []
    for m in range(PAIRS):
        span = 2 * PATCH if m < PAIRS - 1 else WIDTH - m * PATCH
        tile = jnp.concatenate([upper(m * PATCH, span), lower(m * PATCH, span)], axis=0)
        seg = dot(tile, rows_t[:span])
        nyquist = jnp.where(lane // 2 == m, seg[:, 2 * PATCH :], nyquist)
        seg = seg[:, : 2 * PATCH].astype(bf16)
        stacked.append(jnp.concatenate([seg[:, :PATCH], seg[:, PATCH:]], axis=0))
    spectra = []
    for m in range(0, PAIRS, 2):
        product = dot(columns, jnp.concatenate(stacked[m : m + 2], axis=1)).astype(bf16)
        spectra += [product[:, :PATCH], product[:, PATCH:]]
    spectra.append(dot(columns[:, :PATCH], nyquist.astype(bf16)).astype(bf16))
    return spectra


def energy(spectrum):
    wide = spectrum.astype(f32)
    return jnp.sum(wide * wide, axis=0, keepdims=True)


def block_tile(ref):
    return lambda start, span: ref[0, :, pl.ds(start, span)]


def own_kernel(own, below, tables, spec, energies):
    for m, spectrum in enumerate(section_spectra(block_tile(own), block_tile(below), tables)):
        spec[m] = spectrum
        energies[pl.ds(m, 1), :] = energy(spectrum)


def own_spectra(own, below, tables):
    in_vmem = pl.BlockSpec(memory_space=pltpu.VMEM)
    return pl.pallas_call(
        own_kernel,
        out_shape=[
            jax.ShapeDtypeStruct((PAIRS + 1, 2 * PATCH, PATCH), bf16),
            jax.ShapeDtypeStruct((2 * PAIRS, PATCH), f32),
        ],
        in_specs=[in_vmem] * 3,
        out_specs=[in_vmem] * 2,
        compiler_params=pltpu.CompilerParams(vmem_limit_bytes=VMEM_LIMIT),
        cost_estimate=pl.CostEstimate(flops=600_000_000, bytes_accessed=2_000_000, transcendentals=0),
    )(own, below, tables)


def flow_kernel(own_spec, own_energies, near, near_below, record, remote, shifts_in, tables, out, spec, lagged, shift_row):
    spread = table(tables, "spread")
    energies = []
    for m, spectrum in enumerate(section_spectra(block_tile(near), block_tile(near_below), tables)):
        spec[m] = spectrum
        energies.append(energy(spectrum))

    lane = lax.broadcasted_iota(jnp.int32, (PAIRS, PATCH), 1)
    pair = lax.broadcasted_iota(jnp.int32, (PAIRS, PATCH), 0)
    own_pair = (lane % COLS) // 2 == pair
    first_16 = own_pair & (lane < COLS)
    weight = jnp.where(lane % HALF == 0, 1.0, 2.0)

    def halves(x):
        return x[:, :PATCH], x[:, PATCH:]

    def totals(main, extra):
        left = jnp.concatenate([main * weight, jnp.where(first_16, extra, 0.0)], axis=1)
        found = dot(three_parts(left), spread)
        found = found[:PAIRS] + found[PAIRS : 2 * PAIRS] + found[2 * PAIRS :]
        by_pair, by_patch = halves(found)
        by_patch = jnp.sum(jnp.where(first_16, by_patch, 0.0), axis=0, keepdims=True) + extra
        scale = 1.0 / (PATCH * PATCH)
        return jnp.sqrt(by_pair * scale + 1e-06), jnp.sqrt(by_patch * scale + 1e-06)

    low_pair, low_patch = totals(jnp.concatenate(energies[:PAIRS], axis=0), energies[PAIRS])
    up_pair, up_patch = totals(own_energies[pl.ds(0, PAIRS), :], own_energies[pl.ds(PAIRS, 1), :])
    floor_pair = floor_ratio * low_pair * up_pair
    floor_patch = floor_ratio * low_patch * up_patch

    for m in range(PAIRS + 1):
        floor = floor_pair[m : m + 1] if m < PAIRS else floor_patch
        low_re = spec[m, pl.ds(0, PATCH)].astype(f32)
        low_im = spec[m, pl.ds(PATCH, PATCH)].astype(f32)
        up_re = own_spec[m, pl.ds(0, PATCH)].astype(f32)
        up_im = own_spec[m, pl.ds(PATCH, PATCH)].astype(f32)
        cross_re = low_re * up_re + low_im * up_im
        cross_im = low_re * up_im - low_im * up_re
        square = cross_re * cross_re + cross_im * cross_im
        modulus = square * lax.rsqrt(jnp.maximum(square, 1e-36))
        inverse = 1.0 / (modulus + floor)
        white = jnp.concatenate([cross_re * inverse, cross_im * inverse], axis=0)
        high = white.astype(bf16)
        low = (white - high.astype(f32)).astype(bf16)
        found = dot(table(tables, "lag_y"), jnp.concatenate([high, low], axis=1))
        part = found[: 2 * SHIFTS, :PATCH] + found[: 2 * SHIFTS, PATCH:] + found[2 * SHIFTS :, :PATCH]
        lagged[pl.ds(m * SHIFTS, SHIFTS), pl.ds(0, PATCH)] = part[:SHIFTS]
        lagged[pl.ds(m * SHIFTS, SHIFTS), pl.ds(PATCH, PATCH)] = part[SHIFTS:]

    extra = lagged[pl.ds(PAIRS * SHIFTS, SHIFTS), pl.ds(0, PATCH)]
    extra = jnp.where(first_16[:, None, :], extra[None], 0.0).reshape(PAIRS * SHIFTS, PATCH)
    left = jnp.concatenate([lagged[pl.ds(0, PAIRS * SHIFTS), :], extra], axis=1)
    high = left.astype(bf16)
    low = (left - high.astype(f32)).astype(bf16)
    rows_all = PAIRS * SHIFTS
    found = dot(jnp.concatenate([high, low], axis=0), table(tables, "lag_x"))
    surface = found[:rows_all, :PATCH] + found[:rows_all, PATCH:] + found[rows_all:, :PATCH]
    surface = surface.reshape(PAIRS, SHIFTS, PATCH)

    shift_row[...] = record[...]
    for i in range(2):
        shift_row[:, pl.ds(i * COLS, COLS)] = shifts_in[0, i].astype(f32)
    rec = shift_row[...]
    at_y = jnp.where(first_16, rec, 0.0)
    at_x = jnp.where(own_pair & (lane >= COLS) & (lane < 2 * COLS), rec, 0.0)
    gather = spread[:PATCH, PATCH:]
    shifts = lax.dot_general(
        jnp.concatenate([at_y, at_x], axis=0).astype(bf16),
        gather,
        (((1,), (1,)), ((), ())),
        preferred_element_type=f32,
    )
    lag_row = lax.broadcasted_iota(jnp.int32, (PAIRS, SHIFTS, PATCH), 1).astype(f32) - REACH
    lag_col = (lax.broadcasted_iota(jnp.int32, (PAIRS, SHIFTS, PATCH), 2) % HALF).astype(f32) - REACH
    dy = lag_row - shifts[:PAIRS][:, None, :]
    dx = lag_col - shifts[PAIRS:][:, None, :]
    mid_y, up_y, down_y = ((dy == k).astype(f32) for k in (0.0, 1.0, -1.0))
    mid_x, up_x, down_x = ((dx == k).astype(f32) for k in (0.0, 1.0, -1.0))
    at_mid_x = surface * mid_x
    at_mid_y = surface * mid_y
    picks = [
        jnp.sum(at_mid_x * (up_y - down_y), axis=1),
        jnp.sum(at_mid_x * (2.0 * mid_y - up_y - down_y), axis=1),
        jnp.sum(at_mid_y * (up_x - down_x), axis=1),
        jnp.sum(at_mid_y * (2.0 * mid_x - up_x - down_x), axis=1),
    ]
    found = dot(three_parts(jnp.concatenate(picks, axis=0)), gather)
    found = found[: 4 * PAIRS] + found[4 * PAIRS : 8 * PAIRS] + found[8 * PAIRS :]
    found = found.reshape(4, PAIRS, PATCH)
    found = jnp.sum(jnp.where(own_pair[None], found, 0.0), axis=1) * (1.0 / (PATCH * PATCH))
    lane_1 = lax.broadcasted_iota(jnp.int32, (1, PATCH), 1)
    slope = jnp.where(lane_1 < COLS, found[0:1], found[2:3])
    bend = jnp.where(lane_1 < COLS, found[1:2], found[3:4])
    flow = rec + 0.5 * slope / (1.0 + jnp.abs(bend))
    result = jnp.where(lane_1 < 2 * COLS, flow, rec)
    out[...] = jnp.broadcast_to(result, out.shape)
    for i in range(2):
        out[:, pl.ds((4 + i) * COLS, COLS)] = jnp.broadcast_to(remote[0, i], (out.shape[0], COLS))


def pair_flow(own_parts, near, near_below, record, remote_initial, offsets, tables, copies):
    operands = (*own_parts, near, near_below, record, remote_initial, offsets, tables)
    return pl.pallas_call(
        flow_kernel,
        out_shape=jax.ShapeDtypeStruct((copies, PATCH), f32),
        in_specs=[pl.BlockSpec(memory_space=pltpu.VMEM)] * len(operands),
        out_specs=pl.BlockSpec(memory_space=pltpu.VMEM),
        scratch_shapes=[
            pltpu.VMEM((PAIRS + 1, 2 * PATCH, PATCH), bf16),
            pltpu.VMEM(((PAIRS + 1) * SHIFTS, 2 * PATCH), f32),
            pltpu.VMEM((1, PATCH), f32),
        ],
        compiler_params=pltpu.CompilerParams(vmem_limit_bytes=VMEM_LIMIT),
    )(*operands)


def relax_kernel(springs, ring, other, flow_out, moving_out):
    sec = lax.axis_index("sec")
    row = lax.axis_index("row")
    last_row = lax.axis_size("row") - 1
    place = lax.rem(row, RING)
    base = row - place
    count = SECS * RING
    node = lax.broadcasted_iota(jnp.int32, (count, PATCH), 0)
    lane = lax.broadcasted_iota(jnp.int32, (count, PATCH), 1)
    in_ring = node % RING
    section = node // RING
    other_first = jnp.broadcast_to(place, (count, PATCH)) < RING // 2
    valid = (section < SECS - 1) & (lane < 2 * COLS)
    valid_up = valid.astype(f32)
    has_left = (lane % COLS > 0).astype(f32)
    has_right = (lane % COLS < COLS - 1).astype(f32)
    row_here = base + in_ring
    row_other = row_here + jnp.where(other_first, -RING, RING)
    at_rows = (row_here, row_other)
    has_up = [(r > 0).astype(f32) for r in at_rows]
    has_down = [(r < last_row).astype(f32) for r in at_rows]
    first = in_ring == 0
    final = in_ring == RING - 1
    here = ring[...]
    beyond = other[...]
    moving = [pltpu.roll(b, PATCH - 2 * COLS, 1) for b in (here, beyond)]
    third = pltpu.roll(here, PATCH - 4 * COLS, 1)

    def moved(x, by):
        by = by % count
        return jnp.concatenate([x[by:], x[:by]], axis=0)

    flows = [jnp.where(valid, moved(b, RING), 0.0) for b in (here, beyond)]

    for sweep in range(SWEEPS):
        spring = springs[pl.ds(2 * sweep, 1), :]
        tether = springs[pl.ds(2 * sweep + 1, 1), :]
        near_x, far_x = moving
        edge_above = jnp.where(other_first, moved(far_x, RING - 1), moved(third, RING - 1))
        edge_below = jnp.where(other_first, moved(third, 1 - RING), moved(far_x, 1 - RING))
        above = (jnp.where(first, edge_above, moved(near_x, -1)), jnp.where(first, moved(near_x, RING - 1), moved(far_x, -1)))
        below = (jnp.where(final, edge_below, moved(near_x, 1)), jnp.where(final, moved(near_x, 1 - RING), moved(far_x, 1)))
        fresh = []
        for k, x in enumerate(moving):
            col_left = pltpu.roll(x, 1, 1)
            col_right = pltpu.roll(x, PATCH - 1, 1)
            laplace = (
                (above[k] - x) * has_up[k]
                + (below[k] - x) * has_down[k]
                + (col_left - x) * has_left
                + (col_right - x) * has_right
            )
            residual = (moved(x, RING) - x - flows[k]) * valid_up
            below_res = jnp.where(section == 0, 0.0, moved(residual, -RING))
            fresh.append(x + step_size * (spring * laplace + tether * (residual - below_res)))
        moving = fresh

    mine = (section == sec) & (in_ring == place)
    for x, ref in ((flows[0], flow_out), (moving[0], moving_out)):
        line = jnp.sum(jnp.where(mine, x, 0.0), axis=0, keepdims=True)
        ref[0, 0] = line[:, :COLS]
        ref[0, 1] = line[:, COLS : 2 * COLS]


def relax(springs, ring, other, shape):
    in_vmem = pl.BlockSpec(memory_space=pltpu.VMEM)
    return pl.pallas_call(
        relax_kernel,
        out_shape=[jax.ShapeDtypeStruct(shape, f32)] * 2,
        in_specs=[in_vmem] * 3,
        out_specs=[in_vmem] * 2,
        compiler_params=pltpu.CompilerParams(vmem_limit_bytes=VMEM_LIMIT),
    )(springs, ring, other)


def shifted(block, axis, distance):
    devices = range(lax.axis_size(axis))
    route = [(i - distance, i) for i in devices if i - distance in devices]
    return lax.ppermute(block, axis, route)


def ring_route(rows, outward):
    route = []
    for r in range(rows):
        step = RING if (r % RING < RING // 2) == outward else -RING
        if 0 <= r - step < rows:
            route.append((r - step, r))
    return route


def per_device(images, initial, offsets, stiffness, plan):
    rows = lax.axis_size("row")
    below = shifted(images, "row", -1)
    near = shifted(images, "sec", 1)
    near_offsets = shifted(offsets, "sec", 1)
    remote_initial = lax.ppermute(initial, "row", ring_route(rows, False))
    record, springs = prepare(plan, initial, stiffness)
    below, near_offsets, remote_initial, record, springs = lax.optimization_barrier(
        (below, near_offsets, remote_initial, record, springs)
    )
    near_below = shifted(below, "sec", 1)
    count = SECS * RING
    tables = jnp.asarray(constant_tables())
    own_parts = own_spectra(images, below, tables)
    mine = pair_flow(own_parts, near, near_below, record, remote_initial, near_offsets, tables, count)
    groups = [
        [s * rows + RING * g + j for s in range(SECS) for j in range(RING)] for g in range(rows // RING)
    ]
    ring = lax.all_to_all(mine.reshape(count, 1, PATCH), ("sec", "row"), 0, 0, axis_index_groups=groups)
    other = lax.ppermute(ring, "row", ring_route(rows, True))
    return tuple(
        relax(springs, ring.reshape(count, PATCH), other.reshape(count, PATCH), initial.shape)
    )


def solution(mesh):
    return jax.shard_map(
        per_device,
        mesh=mesh,
        in_specs=(
            P("sec", "row", None),
            P("sec", None, "row", None),
            P("sec", None, "row", None),
            P(),
            P(),
        ),
        out_specs=(P("sec", None, "row", None), P("sec", None, "row", None)),
        check_vma=False,
    )
```

```python
import math

import numpy as np
import jax
import jax.numpy as jnp
from jax import lax
from jax.experimental import pallas as pl
from jax.experimental.pallas import tpu as pltpu
from jax.sharding import PartitionSpec as P
import ml_dtypes

PATCH = 128
STRIDE = 64
HALF = 64
SWEEPS = 3
COLS = 16
PAIRS = 8
SECS = 4
RING = 4
SHIFTS = 16
REACH = 5
WIDTH = 1088
EXTRA = 16

step_size = 0.2
floor_ratio = 0.2

VMEM_LIMIT = 24 * 1024 * 1024
PREPARE_FLOPS = 1_000_000_000

f32 = jnp.float32
bf16 = jnp.bfloat16


def dft_halves():
    freq = np.arange(PATCH)
    phase = freq[:, None] * freq[None, :] % PATCH
    folded = np.minimum(phase, PATCH - phase)
    angle = folded * (2.0 * math.pi / PATCH)
    sine = np.sin(angle) * np.where(2 * phase > PATCH, -1.0, 1.0)
    sine = np.where(2 * folded == PATCH, 0.0, sine)
    cosine = np.cos(angle)
    cosine = np.where(4 * folded == PATCH, np.cos(np.float32(math.pi / 2)), cosine)
    return cosine.astype(ml_dtypes.bfloat16), (-sine).astype(ml_dtypes.bfloat16)


def two_parts(table):
    high = table.astype(ml_dtypes.bfloat16)
    low = (table - high.astype(np.float64)).astype(ml_dtypes.bfloat16)
    return high, low


def constant_tables():
    cos_t, sin_t = dft_halves()
    cos_f = cos_t.astype(np.float32)
    sin_f = sin_t.astype(np.float32)
    rows = np.zeros((2 * PATCH, 2 * PATCH), np.float32)
    rows[0:PATCH, 0:HALF] = cos_f[:HALF].T
    rows[0:PATCH, PATCH : PATCH + HALF] = sin_f[:HALF].T
    rows[HALF : HALF + PATCH, HALF:PATCH] = cos_f[:HALF].T
    rows[HALF : HALF + PATCH, PATCH + HALF :] = sin_f[:HALF].T
    nyquist = np.zeros((2 * PATCH, PATCH), np.float32)
    nyquist[0:PATCH, 0::2] = cos_f[HALF][:, None]
    nyquist[HALF : HALF + PATCH, 1::2] = cos_f[HALF][:, None]
    columns = np.block([[cos_f, -sin_f], [sin_f, cos_f]])
    lags = np.arange(SHIFTS) - REACH
    used = (np.arange(SHIFTS) <= 2 * REACH).astype(np.float64)
    freq = np.arange(PATCH)
    turn = (freq[None, :] * lags[:, None] % PATCH) * (2.0 * math.pi / PATCH)
    cos_y = np.cos(turn) * used[:, None]
    sin_y = np.sin(turn) * used[:, None]
    high, low = two_parts(np.block([[cos_y, -sin_y], [sin_y, cos_y]]))
    lag_y = np.concatenate([high, low], axis=0)
    weight = np.where(freq[:HALF] == 0, 1.0, 2.0)
    across = np.zeros((3 * PATCH, PATCH))
    for p in range(2):
        cols = slice(p * HALF, p * HALF + SHIFTS)
        block = slice(p * HALF, (p + 1) * HALF)
        across[:PATCH][block, cols] = (cos_y[:, :HALF] * weight).T
        across[PATCH : 2 * PATCH][block, cols] = (-sin_y[:, :HALF] * weight).T
        for c in range(p, COLS, 2):
            across[2 * PATCH + c, cols] = np.where(lags % 2 == 0, 1.0, -1.0) * used
    high, low = two_parts(across)
    lag_x = np.concatenate([high, low], axis=1)
    lane = np.arange(PATCH)
    patch = (lane % COLS % 2)[None, :] == (lane // HALF)[:, None]
    gather = (patch & (lane < 2 * COLS)[None, :]).astype(np.float32)
    single = (patch & (lane < COLS)[None, :]).astype(np.float32)
    same = ((lane // HALF)[:, None] == (lane // HALF)[None, :]).astype(np.float32)
    blank = np.zeros((PATCH, PATCH), np.float32)
    spread = np.block([[same, gather], [single.T, blank]])
    packed = [rows, np.concatenate([nyquist[:PATCH], nyquist[PATCH:]], axis=1), columns, spread, lag_y, lag_x]
    return np.concatenate([np.asarray(t).astype(ml_dtypes.bfloat16) for t in packed], axis=0)


TABLE_ROWS = {"rows": (0, 256), "nyquist": (256, 128), "columns": (384, 256), "spread": (640, 256)}
TABLE_ROWS |= {"lag_y": (896, 64), "lag_x": (960, 384)}


def table(ref, name):
    start, length = TABLE_ROWS[name]
    return ref[pl.ds(start, length), :]


def three_parts(x):
    high = x.astype(bf16)
    rest = x - high.astype(f32)
    mid = rest.astype(bf16)
    low = (rest - mid.astype(f32)).astype(bf16)
    return jnp.concatenate([high, mid, low], axis=0)


def dot(a, b):
    return jnp.dot(a, b, preferred_element_type=f32)


def prepare_kernel(plan, images, offsets, initial, stiffness, remote, sent, record, springs, shifts):
    sent[0, pl.ds(0, HALF), :] = images[0]
    sent[0, pl.ds(HALF, EXTRA), :] = jnp.zeros((EXTRA, WIDTH), bf16)
    shifts[...] = jnp.zeros((EXTRA, PATCH), f32)
    record[...] = jnp.zeros((1, PATCH), f32)
    for i in range(2):
        record[:, pl.ds((2 + i) * COLS, COLS)] = initial[0, i]
        record[:, pl.ds((4 + i) * COLS, COLS)] = remote[0, i]
        shifts[pl.ds(0, 1), pl.ds(i * COLS, COLS)] = offsets[0, i].astype(f32)
    sent[0, pl.ds(HALF, EXTRA), pl.ds(0, PATCH)] = shifts[...].astype(bf16)
    level_id = lax.broadcasted_iota(jnp.int32, stiffness.shape, 1)
    for sweep in range(SWEEPS):
        picked = jnp.sum(jnp.where(level_id == plan[sweep], stiffness[...], 0.0), axis=1, keepdims=True)
        springs[pl.ds(2 * sweep, 2), :] = jnp.broadcast_to(picked, (2, PATCH))


def prepare(plan, images, offsets, initial, stiffness, remote_initial):
    in_vmem = pl.BlockSpec(memory_space=pltpu.VMEM)
    return pl.pallas_call(
        prepare_kernel,
        out_shape=[
            jax.ShapeDtypeStruct((1, HALF + EXTRA, WIDTH), bf16),
            jax.ShapeDtypeStruct((1, PATCH), f32),
            jax.ShapeDtypeStruct((8, PATCH), f32),
        ],
        in_specs=[pl.BlockSpec(memory_space=pltpu.SMEM)] + [in_vmem] * 5,
        out_specs=[in_vmem] * 3,
        scratch_shapes=[pltpu.VMEM((EXTRA, PATCH), f32)],
        compiler_params=pltpu.CompilerParams(vmem_limit_bytes=VMEM_LIMIT),
        cost_estimate=pl.CostEstimate(flops=PREPARE_FLOPS, bytes_accessed=10_000, transcendentals=0),
    )(plan, images, offsets, initial, stiffness.T, remote_initial)


def section_spectra(upper, lower, tables):
    nyq_t = table(tables, "nyquist")
    nyq_t = jnp.concatenate([nyq_t[:, :PATCH], nyq_t[:, PATCH:]], axis=0)
    rows_t = jnp.concatenate([table(tables, "rows"), nyq_t], axis=1)
    columns = table(tables, "columns")
    lane = lax.broadcasted_iota(jnp.int32, (PATCH, PATCH), 1)
    nyquist = jnp.zeros((PATCH, PATCH), f32)
    stacked = []
    for m in range(PAIRS):
        span = 2 * PATCH if m < PAIRS - 1 else WIDTH - m * PATCH
        tile = jnp.concatenate([upper(m * PATCH, span), lower(m * PATCH, span)], axis=0)
        seg = dot(tile, rows_t[:span])
        nyquist = jnp.where(lane // 2 == m, seg[:, 2 * PATCH :], nyquist)
        seg = seg[:, : 2 * PATCH].astype(bf16)
        stacked.append(jnp.concatenate([seg[:, :PATCH], seg[:, PATCH:]], axis=0))
    spectra = []
    for m in range(0, PAIRS, 2):
        product = dot(columns, jnp.concatenate(stacked[m : m + 2], axis=1)).astype(bf16)
        spectra += [product[:, :PATCH], product[:, PATCH:]]
    spectra.append(dot(columns[:, :PATCH], nyquist.astype(bf16)).astype(bf16))
    return spectra


def energy(spectrum):
    wide = spectrum.astype(f32)
    return jnp.sum(wide * wide, axis=0, keepdims=True)


def block_tile(ref):
    return lambda start, span: ref[0, pl.ds(0, HALF), pl.ds(start, span)]


def own_kernel(own, below, tables, spec, energies):
    for m, spectrum in enumerate(section_spectra(block_tile(own), block_tile(below), tables)):
        spec[m] = spectrum
        energies[pl.ds(m, 1), :] = energy(spectrum)


def own_spectra(own, below, tables):
    in_vmem = pl.BlockSpec(memory_space=pltpu.VMEM)
    return pl.pallas_call(
        own_kernel,
        out_shape=[
            jax.ShapeDtypeStruct((PAIRS + 1, 2 * PATCH, PATCH), bf16),
            jax.ShapeDtypeStruct((2 * PAIRS, PATCH), f32),
        ],
        in_specs=[in_vmem] * 3,
        out_specs=[in_vmem] * 2,
        compiler_params=pltpu.CompilerParams(vmem_limit_bytes=VMEM_LIMIT),
        cost_estimate=pl.CostEstimate(flops=600_000_000, bytes_accessed=2_000_000, transcendentals=0),
    )(own, below, tables)


def flow_kernel(own_spec, own_energies, near, near_below, record, tables, out, spec, lagged):
    spread = table(tables, "spread")
    energies = []
    for m, spectrum in enumerate(section_spectra(block_tile(near), block_tile(near_below), tables)):
        spec[m] = spectrum
        energies.append(energy(spectrum))

    lane = lax.broadcasted_iota(jnp.int32, (PAIRS, PATCH), 1)
    pair = lax.broadcasted_iota(jnp.int32, (PAIRS, PATCH), 0)
    own_pair = (lane % COLS) // 2 == pair
    first_16 = own_pair & (lane < COLS)
    weight = jnp.where(lane % HALF == 0, 1.0, 2.0)

    def halves(x):
        return x[:, :PATCH], x[:, PATCH:]

    def totals(main, extra):
        left = jnp.concatenate([main * weight, jnp.where(first_16, extra, 0.0)], axis=1)
        found = dot(three_parts(left), spread)
        found = found[:PAIRS] + found[PAIRS : 2 * PAIRS] + found[2 * PAIRS :]
        by_pair, by_patch = halves(found)
        by_patch = jnp.sum(jnp.where(first_16, by_patch, 0.0), axis=0, keepdims=True) + extra
        scale = 1.0 / (PATCH * PATCH)
        return jnp.sqrt(by_pair * scale + 1e-06), jnp.sqrt(by_patch * scale + 1e-06)

    low_pair, low_patch = totals(jnp.concatenate(energies[:PAIRS], axis=0), energies[PAIRS])
    up_pair, up_patch = totals(own_energies[pl.ds(0, PAIRS), :], own_energies[pl.ds(PAIRS, 1), :])
    floor_pair = floor_ratio * low_pair * up_pair
    floor_patch = floor_ratio * low_patch * up_patch

    for m in range(PAIRS + 1):
        floor = floor_pair[m : m + 1] if m < PAIRS else floor_patch
        low_re = spec[m, pl.ds(0, PATCH)].astype(f32)
        low_im = spec[m, pl.ds(PATCH, PATCH)].astype(f32)
        up_re = own_spec[m, pl.ds(0, PATCH)].astype(f32)
        up_im = own_spec[m, pl.ds(PATCH, PATCH)].astype(f32)
        cross_re = low_re * up_re + low_im * up_im
        cross_im = low_re * up_im - low_im * up_re
        square = cross_re * cross_re + cross_im * cross_im
        modulus = square * lax.rsqrt(jnp.maximum(square, 1e-36))
        inverse = 1.0 / (modulus + floor)
        white = jnp.concatenate([cross_re * inverse, cross_im * inverse], axis=0)
        high = white.astype(bf16)
        low = (white - high.astype(f32)).astype(bf16)
        found = dot(table(tables, "lag_y"), jnp.concatenate([high, low], axis=1))
        part = found[: 2 * SHIFTS, :PATCH] + found[: 2 * SHIFTS, PATCH:] + found[2 * SHIFTS :, :PATCH]
        lagged[pl.ds(m * SHIFTS, SHIFTS), pl.ds(0, PATCH)] = part[:SHIFTS]
        lagged[pl.ds(m * SHIFTS, SHIFTS), pl.ds(PATCH, PATCH)] = part[SHIFTS:]

    extra = lagged[pl.ds(PAIRS * SHIFTS, SHIFTS), pl.ds(0, PATCH)]
    extra = jnp.where(first_16[:, None, :], extra[None], 0.0).reshape(PAIRS * SHIFTS, PATCH)
    left = jnp.concatenate([lagged[pl.ds(0, PAIRS * SHIFTS), :], extra], axis=1)
    high = left.astype(bf16)
    low = (left - high.astype(f32)).astype(bf16)
    rows_all = PAIRS * SHIFTS
    found = dot(jnp.concatenate([high, low], axis=0), table(tables, "lag_x"))
    surface = found[:rows_all, :PATCH] + found[:rows_all, PATCH:] + found[rows_all:, :PATCH]
    surface = surface.reshape(PAIRS, SHIFTS, PATCH)

    rec = near[0, pl.ds(HALF, EXTRA), pl.ds(0, PATCH)].astype(f32)[0:1]
    at_y = jnp.where(first_16, rec, 0.0)
    at_x = jnp.where(own_pair & (lane >= COLS) & (lane < 2 * COLS), rec, 0.0)
    gather = spread[:PATCH, PATCH:]
    shifts = lax.dot_general(
        jnp.concatenate([at_y, at_x], axis=0).astype(bf16),
        gather,
        (((1,), (1,)), ((), ())),
        preferred_element_type=f32,
    )
    lag_row = lax.broadcasted_iota(jnp.int32, (PAIRS, SHIFTS, PATCH), 1).astype(f32) - REACH
    lag_col = (lax.broadcasted_iota(jnp.int32, (PAIRS, SHIFTS, PATCH), 2) % HALF).astype(f32) - REACH
    dy = lag_row - shifts[:PAIRS][:, None, :]
    dx = lag_col - shifts[PAIRS:][:, None, :]
    mid_y, up_y, down_y = ((dy == k).astype(f32) for k in (0.0, 1.0, -1.0))
    mid_x, up_x, down_x = ((dx == k).astype(f32) for k in (0.0, 1.0, -1.0))
    at_mid_x = surface * mid_x
    at_mid_y = surface * mid_y
    picks = [
        jnp.sum(at_mid_x * (up_y - down_y), axis=1),
        jnp.sum(at_mid_x * (2.0 * mid_y - up_y - down_y), axis=1),
        jnp.sum(at_mid_y * (up_x - down_x), axis=1),
        jnp.sum(at_mid_y * (2.0 * mid_x - up_x - down_x), axis=1),
    ]
    found = dot(three_parts(jnp.concatenate(picks, axis=0)), gather)
    found = found[: 4 * PAIRS] + found[4 * PAIRS : 8 * PAIRS] + found[8 * PAIRS :]
    found = found.reshape(4, PAIRS, PATCH)
    found = jnp.sum(jnp.where(own_pair[None], found, 0.0), axis=1) * (1.0 / (PATCH * PATCH))
    lane_1 = lax.broadcasted_iota(jnp.int32, (1, PATCH), 1)
    slope = jnp.where(lane_1 < COLS, found[0:1], found[2:3])
    bend = jnp.where(lane_1 < COLS, found[1:2], found[3:4])
    flow = rec + 0.5 * slope / (1.0 + jnp.abs(bend))
    out[...] = jnp.broadcast_to(jnp.where(lane_1 < 2 * COLS, flow, record[...]), out.shape)


def pair_flow(own_parts, near, near_below, record, tables, copies):
    operands = (*own_parts, near, near_below, record, tables)
    return pl.pallas_call(
        flow_kernel,
        out_shape=jax.ShapeDtypeStruct((copies, PATCH), f32),
        in_specs=[pl.BlockSpec(memory_space=pltpu.VMEM)] * len(operands),
        out_specs=pl.BlockSpec(memory_space=pltpu.VMEM),
        scratch_shapes=[
            pltpu.VMEM((PAIRS + 1, 2 * PATCH, PATCH), bf16),
            pltpu.VMEM(((PAIRS + 1) * SHIFTS, 2 * PATCH), f32),
        ],
        compiler_params=pltpu.CompilerParams(vmem_limit_bytes=VMEM_LIMIT),
    )(*operands)


def relax_kernel(springs, ring, other, flow_out, moving_out):
    sec = lax.axis_index("sec")
    row = lax.axis_index("row")
    last_row = lax.axis_size("row") - 1
    place = lax.rem(row, RING)
    base = row - place
    count = SECS * RING
    node = lax.broadcasted_iota(jnp.int32, (count, PATCH), 0)
    lane = lax.broadcasted_iota(jnp.int32, (count, PATCH), 1)
    in_ring = node % RING
    section = node // RING
    other_first = jnp.broadcast_to(place, (count, PATCH)) < RING // 2
    valid = (section < SECS - 1) & (lane < 2 * COLS)
    valid_up = valid.astype(f32)
    has_left = (lane % COLS > 0).astype(f32)
    has_right = (lane % COLS < COLS - 1).astype(f32)
    row_here = base + in_ring
    row_other = row_here + jnp.where(other_first, -RING, RING)
    at_rows = (row_here, row_other)
    has_up = [(r > 0).astype(f32) for r in at_rows]
    has_down = [(r < last_row).astype(f32) for r in at_rows]
    first = in_ring == 0
    final = in_ring == RING - 1
    here = ring[...]
    beyond = other[...]
    moving = [pltpu.roll(b, PATCH - 2 * COLS, 1) for b in (here, beyond)]
    third = pltpu.roll(here, PATCH - 4 * COLS, 1)

    def moved(x, by):
        by = by % count
        return jnp.concatenate([x[by:], x[:by]], axis=0)

    flows = [jnp.where(valid, moved(b, RING), 0.0) for b in (here, beyond)]

    for sweep in range(SWEEPS):
        spring = springs[pl.ds(2 * sweep, 1), :]
        tether = springs[pl.ds(2 * sweep + 1, 1), :]
        near_x, far_x = moving
        edge_above = jnp.where(other_first, moved(far_x, RING - 1), moved(third, RING - 1))
        edge_below = jnp.where(other_first, moved(third, 1 - RING), moved(far_x, 1 - RING))
        above = (jnp.where(first, edge_above, moved(near_x, -1)), jnp.where(first, moved(near_x, RING - 1), moved(far_x, -1)))
        below = (jnp.where(final, edge_below, moved(near_x, 1)), jnp.where(final, moved(near_x, 1 - RING), moved(far_x, 1)))
        fresh = []
        for k, x in enumerate(moving):
            col_left = pltpu.roll(x, 1, 1)
            col_right = pltpu.roll(x, PATCH - 1, 1)
            laplace = (
                (above[k] - x) * has_up[k]
                + (below[k] - x) * has_down[k]
                + (col_left - x) * has_left
                + (col_right - x) * has_right
            )
            residual = (moved(x, RING) - x - flows[k]) * valid_up
            below_res = jnp.where(section == 0, 0.0, moved(residual, -RING))
            fresh.append(x + step_size * (spring * laplace + tether * (residual - below_res)))
        moving = fresh

    mine = (section == sec) & (in_ring == place)
    for x, ref in ((flows[0], flow_out), (moving[0], moving_out)):
        line = jnp.sum(jnp.where(mine, x, 0.0), axis=0, keepdims=True)
        ref[0, 0] = line[:, :COLS]
        ref[0, 1] = line[:, COLS : 2 * COLS]


def relax(springs, ring, other, shape):
    in_vmem = pl.BlockSpec(memory_space=pltpu.VMEM)
    return pl.pallas_call(
        relax_kernel,
        out_shape=[jax.ShapeDtypeStruct(shape, f32)] * 2,
        in_specs=[in_vmem] * 3,
        out_specs=[in_vmem] * 2,
        compiler_params=pltpu.CompilerParams(vmem_limit_bytes=VMEM_LIMIT),
    )(springs, ring, other)


def shifted(block, axis, distance):
    devices = range(lax.axis_size(axis))
    route = [(i - distance, i) for i in devices if i - distance in devices]
    return lax.ppermute(block, axis, route)


def ring_route(rows, outward):
    route = []
    for r in range(rows):
        step = RING if (r % RING < RING // 2) == outward else -RING
        if 0 <= r - step < rows:
            route.append((r - step, r))
    return route


def per_device(images, initial, offsets, stiffness, plan):
    rows = lax.axis_size("row")
    below = shifted(images, "row", -1)
    remote_initial = lax.ppermute(initial, "row", ring_route(rows, False))
    sent, record, springs = prepare(plan, images, offsets, initial, stiffness, remote_initial)
    near = shifted(sent, "sec", 1)
    below, record, springs = lax.optimization_barrier((below, record, springs))
    near_below = shifted(below, "sec", 1)
    count = SECS * RING
    tables = jnp.asarray(constant_tables())
    own_parts = own_spectra(sent, below, tables)
    mine = pair_flow(own_parts, near, near_below, record, tables, count)
    groups = [
        [s * rows + RING * g + j for s in range(SECS) for j in range(RING)] for g in range(rows // RING)
    ]
    ring = lax.all_to_all(mine.reshape(count, 1, PATCH), ("sec", "row"), 0, 0, axis_index_groups=groups)
    other = lax.ppermute(ring, "row", ring_route(rows, True))
    return tuple(
        relax(springs, ring.reshape(count, PATCH), other.reshape(count, PATCH), initial.shape)
    )


def solution(mesh):
    return jax.shard_map(
        per_device,
        mesh=mesh,
        in_specs=(
            P("sec", "row", None),
            P("sec", None, "row", None),
            P("sec", None, "row", None),
            P(),
            P(),
        ),
        out_specs=(P("sec", None, "row", None), P("sec", None, "row", None)),
        check_vma=False,
    )
```

```python
import math

import numpy as np
import jax
import jax.numpy as jnp
from jax import lax
from jax.experimental import pallas as pl
from jax.experimental.pallas import tpu as pltpu
from jax.sharding import PartitionSpec as P
import ml_dtypes

PATCH = 128
STRIDE = 64
HALF = 64
SWEEPS = 3
COLS = 16
PAIRS = 8
SECS = 4
RING = 4
SHIFTS = 16
REACH = 5
WIDTH = 1088

step_size = 0.2
floor_ratio = 0.2

VMEM_LIMIT = 24 * 1024 * 1024
PREPARE_FLOPS = 1_000_000_000

f32 = jnp.float32
bf16 = jnp.bfloat16


def dft_halves():
    freq = np.arange(PATCH)
    phase = freq[:, None] * freq[None, :] % PATCH
    folded = np.minimum(phase, PATCH - phase)
    angle = folded * (2.0 * math.pi / PATCH)
    sine = np.sin(angle) * np.where(2 * phase > PATCH, -1.0, 1.0)
    sine = np.where(2 * folded == PATCH, 0.0, sine)
    cosine = np.cos(angle)
    cosine = np.where(4 * folded == PATCH, np.cos(np.float32(math.pi / 2)), cosine)
    return cosine.astype(ml_dtypes.bfloat16), (-sine).astype(ml_dtypes.bfloat16)


def two_parts(table):
    high = table.astype(ml_dtypes.bfloat16)
    low = (table - high.astype(np.float64)).astype(ml_dtypes.bfloat16)
    return high, low


def constant_tables():
    cos_t, sin_t = dft_halves()
    cos_f = cos_t.astype(np.float32)
    sin_f = sin_t.astype(np.float32)
    rows = np.zeros((2 * PATCH, 2 * PATCH), np.float32)
    rows[0:PATCH, 0:HALF] = cos_f[:HALF].T
    rows[0:PATCH, PATCH : PATCH + HALF] = sin_f[:HALF].T
    rows[HALF : HALF + PATCH, HALF:PATCH] = cos_f[:HALF].T
    rows[HALF : HALF + PATCH, PATCH + HALF :] = sin_f[:HALF].T
    nyquist = np.zeros((2 * PATCH, PATCH), np.float32)
    nyquist[0:PATCH, 0::2] = cos_f[HALF][:, None]
    nyquist[HALF : HALF + PATCH, 1::2] = cos_f[HALF][:, None]
    columns = np.block([[cos_f, -sin_f], [sin_f, cos_f]])
    lags = np.arange(SHIFTS) - REACH
    used = (np.arange(SHIFTS) <= 2 * REACH).astype(np.float64)
    freq = np.arange(PATCH)
    turn = (freq[None, :] * lags[:, None] % PATCH) * (2.0 * math.pi / PATCH)
    cos_y = np.cos(turn) * used[:, None]
    sin_y = np.sin(turn) * used[:, None]
    high, low = two_parts(np.block([[cos_y, -sin_y], [sin_y, cos_y]]))
    lag_y = np.concatenate([high, low], axis=0)
    weight = np.where(freq[:HALF] == 0, 1.0, 2.0)
    across = np.zeros((3 * PATCH, PATCH))
    for p in range(2):
        cols = slice(p * HALF, p * HALF + SHIFTS)
        block = slice(p * HALF, (p + 1) * HALF)
        across[:PATCH][block, cols] = (cos_y[:, :HALF] * weight).T
        across[PATCH : 2 * PATCH][block, cols] = (-sin_y[:, :HALF] * weight).T
        for c in range(p, COLS, 2):
            across[2 * PATCH + c, cols] = np.where(lags % 2 == 0, 1.0, -1.0) * used
    high, low = two_parts(across)
    lag_x = np.concatenate([high, low], axis=1)
    lane = np.arange(PATCH)
    patch = (lane % COLS % 2)[None, :] == (lane // HALF)[:, None]
    gather = (patch & (lane < 2 * COLS)[None, :]).astype(np.float32)
    single = (patch & (lane < COLS)[None, :]).astype(np.float32)
    same = ((lane // HALF)[:, None] == (lane // HALF)[None, :]).astype(np.float32)
    blank = np.zeros((PATCH, PATCH), np.float32)
    spread = np.block([[same, gather], [single.T, blank]])
    packed = [rows, np.concatenate([nyquist[:PATCH], nyquist[PATCH:]], axis=1), columns, spread, lag_y, lag_x]
    return np.concatenate([np.asarray(t).astype(ml_dtypes.bfloat16) for t in packed], axis=0)


TABLE_ROWS = {"rows": (0, 256), "nyquist": (256, 128), "columns": (384, 256), "spread": (640, 256)}
TABLE_ROWS |= {"lag_y": (896, 64), "lag_x": (960, 384)}


def table(ref, name):
    start, length = TABLE_ROWS[name]
    return ref[pl.ds(start, length), :]


def three_parts(x):
    high = x.astype(bf16)
    rest = x - high.astype(f32)
    mid = rest.astype(bf16)
    low = (rest - mid.astype(f32)).astype(bf16)
    return jnp.concatenate([high, mid, low], axis=0)


def dot(a, b):
    return jnp.dot(a, b, preferred_element_type=f32)


def prepare_kernel(plan, offsets, initial, stiffness, remote, record, springs):
    record[...] = jnp.zeros((1, PATCH), f32)
    for i in range(2):
        record[:, pl.ds(i * COLS, COLS)] = offsets[0, i].astype(f32)
        record[:, pl.ds((2 + i) * COLS, COLS)] = initial[0, i]
        record[:, pl.ds((4 + i) * COLS, COLS)] = remote[0, i]
    level_id = lax.broadcasted_iota(jnp.int32, stiffness.shape, 1)
    for sweep in range(SWEEPS):
        picked = jnp.sum(jnp.where(level_id == plan[sweep], stiffness[...], 0.0), axis=1, keepdims=True)
        springs[pl.ds(2 * sweep, 2), :] = jnp.broadcast_to(picked, (2, PATCH))


def prepare(plan, offsets, initial, stiffness, remote_initial):
    in_vmem = pl.BlockSpec(memory_space=pltpu.VMEM)
    return pl.pallas_call(
        prepare_kernel,
        out_shape=[jax.ShapeDtypeStruct((1, PATCH), f32), jax.ShapeDtypeStruct((8, PATCH), f32)],
        in_specs=[pl.BlockSpec(memory_space=pltpu.SMEM)] + [in_vmem] * 4,
        out_specs=[in_vmem] * 2,
        compiler_params=pltpu.CompilerParams(vmem_limit_bytes=VMEM_LIMIT),
        cost_estimate=pl.CostEstimate(flops=PREPARE_FLOPS, bytes_accessed=10_000, transcendentals=0),
    )(plan, offsets, initial, stiffness.T, remote_initial)


def section_spectra(upper, lower, tables):
    nyq_t = table(tables, "nyquist")
    nyq_t = jnp.concatenate([nyq_t[:, :PATCH], nyq_t[:, PATCH:]], axis=0)
    rows_t = jnp.concatenate([table(tables, "rows"), nyq_t], axis=1)
    columns = table(tables, "columns")
    lane = lax.broadcasted_iota(jnp.int32, (PATCH, PATCH), 1)
    nyquist = jnp.zeros((PATCH, PATCH), f32)
    stacked = []
    for m in range(PAIRS):
        span = 2 * PATCH if m < PAIRS - 1 else WIDTH - m * PATCH
        tile = jnp.concatenate([upper(m * PATCH, span), lower(m * PATCH, span)], axis=0)
        seg = dot(tile, rows_t[:span])
        nyquist = jnp.where(lane // 2 == m, seg[:, 2 * PATCH :], nyquist)
        seg = seg[:, : 2 * PATCH].astype(bf16)
        stacked.append(jnp.concatenate([seg[:, :PATCH], seg[:, PATCH:]], axis=0))
    spectra = []
    for m in range(0, PAIRS, 2):
        product = dot(columns, jnp.concatenate(stacked[m : m + 2], axis=1)).astype(bf16)
        spectra += [product[:, :PATCH], product[:, PATCH:]]
    spectra.append(dot(columns[:, :PATCH], nyquist.astype(bf16)).astype(bf16))
    return spectra


def energy(spectrum):
    wide = spectrum.astype(f32)
    return jnp.sum(wide * wide, axis=0, keepdims=True)


def block_tile(ref):
    return lambda start, span: ref[0, :, pl.ds(start, span)]


def own_kernel(own, below, tables, spec, energies):
    for m, spectrum in enumerate(section_spectra(block_tile(own), block_tile(below), tables)):
        spec[m] = spectrum
        energies[pl.ds(m, 1), :] = energy(spectrum)


def own_spectra(own, below, tables):
    in_vmem = pl.BlockSpec(memory_space=pltpu.VMEM)
    return pl.pallas_call(
        own_kernel,
        out_shape=[
            jax.ShapeDtypeStruct((PAIRS + 1, 2 * PATCH, PATCH), bf16),
            jax.ShapeDtypeStruct((2 * PAIRS, PATCH), f32),
        ],
        in_specs=[in_vmem] * 3,
        out_specs=[in_vmem] * 2,
        compiler_params=pltpu.CompilerParams(vmem_limit_bytes=VMEM_LIMIT),
        cost_estimate=pl.CostEstimate(flops=600_000_000, bytes_accessed=2_000_000, transcendentals=0),
    )(own, below, tables)


def flow_kernel(own_spec, own_energies, near, near_below, record, tables, out, spec, lagged):
    spread = table(tables, "spread")
    energies = []
    for m, spectrum in enumerate(section_spectra(block_tile(near), block_tile(near_below), tables)):
        spec[m] = spectrum
        energies.append(energy(spectrum))

    lane = lax.broadcasted_iota(jnp.int32, (PAIRS, PATCH), 1)
    pair = lax.broadcasted_iota(jnp.int32, (PAIRS, PATCH), 0)
    own_pair = (lane % COLS) // 2 == pair
    first_16 = own_pair & (lane < COLS)
    weight = jnp.where(lane % HALF == 0, 1.0, 2.0)

    def halves(x):
        return x[:, :PATCH], x[:, PATCH:]

    def totals(main, extra):
        left = jnp.concatenate([main * weight, jnp.where(first_16, extra, 0.0)], axis=1)
        found = dot(three_parts(left), spread)
        found = found[:PAIRS] + found[PAIRS : 2 * PAIRS] + found[2 * PAIRS :]
        by_pair, by_patch = halves(found)
        by_patch = jnp.sum(jnp.where(first_16, by_patch, 0.0), axis=0, keepdims=True) + extra
        scale = 1.0 / (PATCH * PATCH)
        return jnp.sqrt(by_pair * scale + 1e-06), jnp.sqrt(by_patch * scale + 1e-06)

    low_pair, low_patch = totals(own_energies[pl.ds(0, PAIRS), :], own_energies[pl.ds(PAIRS, 1), :])
    up_pair, up_patch = totals(jnp.concatenate(energies[:PAIRS], axis=0), energies[PAIRS])
    floor_pair = floor_ratio * low_pair * up_pair
    floor_patch = floor_ratio * low_patch * up_patch

    for m in range(PAIRS + 1):
        floor = floor_pair[m : m + 1] if m < PAIRS else floor_patch
        low_re = own_spec[m, pl.ds(0, PATCH)].astype(f32)
        low_im = own_spec[m, pl.ds(PATCH, PATCH)].astype(f32)
        up_re = spec[m, pl.ds(0, PATCH)].astype(f32)
        up_im = spec[m, pl.ds(PATCH, PATCH)].astype(f32)
        cross_re = low_re * up_re + low_im * up_im
        cross_im = low_re * up_im - low_im * up_re
        square = cross_re * cross_re + cross_im * cross_im
        modulus = square * lax.rsqrt(jnp.maximum(square, 1e-36))
        inverse = 1.0 / (modulus + floor)
        white = jnp.concatenate([cross_re * inverse, cross_im * inverse], axis=0)
        high = white.astype(bf16)
        low = (white - high.astype(f32)).astype(bf16)
        found = dot(table(tables, "lag_y"), jnp.concatenate([high, low], axis=1))
        part = found[: 2 * SHIFTS, :PATCH] + found[: 2 * SHIFTS, PATCH:] + found[2 * SHIFTS :, :PATCH]
        lagged[pl.ds(m * SHIFTS, SHIFTS), pl.ds(0, PATCH)] = part[:SHIFTS]
        lagged[pl.ds(m * SHIFTS, SHIFTS), pl.ds(PATCH, PATCH)] = part[SHIFTS:]

    extra = lagged[pl.ds(PAIRS * SHIFTS, SHIFTS), pl.ds(0, PATCH)]
    extra = jnp.where(first_16[:, None, :], extra[None], 0.0).reshape(PAIRS * SHIFTS, PATCH)
    left = jnp.concatenate([lagged[pl.ds(0, PAIRS * SHIFTS), :], extra], axis=1)
    high = left.astype(bf16)
    low = (left - high.astype(f32)).astype(bf16)
    rows_all = PAIRS * SHIFTS
    found = dot(jnp.concatenate([high, low], axis=0), table(tables, "lag_x"))
    surface = found[:rows_all, :PATCH] + found[:rows_all, PATCH:] + found[rows_all:, :PATCH]
    surface = surface.reshape(PAIRS, SHIFTS, PATCH)

    rec = record[...]
    at_y = jnp.where(first_16, rec, 0.0)
    at_x = jnp.where(own_pair & (lane >= COLS) & (lane < 2 * COLS), rec, 0.0)
    gather = spread[:PATCH, PATCH:]
    shifts = lax.dot_general(
        jnp.concatenate([at_y, at_x], axis=0).astype(bf16),
        gather,
        (((1,), (1,)), ((), ())),
        preferred_element_type=f32,
    )
    lag_row = lax.broadcasted_iota(jnp.int32, (PAIRS, SHIFTS, PATCH), 1).astype(f32) - REACH
    lag_col = (lax.broadcasted_iota(jnp.int32, (PAIRS, SHIFTS, PATCH), 2) % HALF).astype(f32) - REACH
    dy = lag_row - shifts[:PAIRS][:, None, :]
    dx = lag_col - shifts[PAIRS:][:, None, :]
    mid_y, up_y, down_y = ((dy == k).astype(f32) for k in (0.0, 1.0, -1.0))
    mid_x, up_x, down_x = ((dx == k).astype(f32) for k in (0.0, 1.0, -1.0))
    at_mid_x = surface * mid_x
    at_mid_y = surface * mid_y
    picks = [
        jnp.sum(at_mid_x * (up_y - down_y), axis=1),
        jnp.sum(at_mid_x * (2.0 * mid_y - up_y - down_y), axis=1),
        jnp.sum(at_mid_y * (up_x - down_x), axis=1),
        jnp.sum(at_mid_y * (2.0 * mid_x - up_x - down_x), axis=1),
    ]
    found = dot(three_parts(jnp.concatenate(picks, axis=0)), gather)
    found = found[: 4 * PAIRS] + found[4 * PAIRS : 8 * PAIRS] + found[8 * PAIRS :]
    found = found.reshape(4, PAIRS, PATCH)
    found = jnp.sum(jnp.where(own_pair[None], found, 0.0), axis=1) * (1.0 / (PATCH * PATCH))
    lane_1 = lax.broadcasted_iota(jnp.int32, (1, PATCH), 1)
    slope = jnp.where(lane_1 < COLS, found[0:1], found[2:3])
    bend = jnp.where(lane_1 < COLS, found[1:2], found[3:4])
    flow = rec + 0.5 * slope / (1.0 + jnp.abs(bend))
    result = jnp.where(lane_1 < 2 * COLS, flow, rec)
    out[...] = jnp.broadcast_to(result, out.shape)


def pair_flow(own_parts, near, near_below, record, tables, copies):
    operands = (*own_parts, near, near_below, record, tables)
    return pl.pallas_call(
        flow_kernel,
        out_shape=jax.ShapeDtypeStruct((copies, PATCH), f32),
        in_specs=[pl.BlockSpec(memory_space=pltpu.VMEM)] * len(operands),
        out_specs=pl.BlockSpec(memory_space=pltpu.VMEM),
        scratch_shapes=[
            pltpu.VMEM((PAIRS + 1, 2 * PATCH, PATCH), bf16),
            pltpu.VMEM(((PAIRS + 1) * SHIFTS, 2 * PATCH), f32),
        ],
        compiler_params=pltpu.CompilerParams(vmem_limit_bytes=VMEM_LIMIT),
    )(*operands)


def relax_kernel(springs, ring, other, flow_out, moving_out):
    sec = lax.axis_index("sec")
    row = lax.axis_index("row")
    last_row = lax.axis_size("row") - 1
    place = lax.rem(row, RING)
    base = row - place
    count = SECS * RING
    node = lax.broadcasted_iota(jnp.int32, (count, PATCH), 0)
    lane = lax.broadcasted_iota(jnp.int32, (count, PATCH), 1)
    in_ring = node % RING
    section = node // RING
    other_first = jnp.broadcast_to(place, (count, PATCH)) < RING // 2
    valid = (section < SECS - 1) & (lane < 2 * COLS)
    valid_up = valid.astype(f32)
    has_left = (lane % COLS > 0).astype(f32)
    has_right = (lane % COLS < COLS - 1).astype(f32)
    row_here = base + in_ring
    row_other = row_here + jnp.where(other_first, -RING, RING)
    at_rows = (row_here, row_other)
    has_up = [(r > 0).astype(f32) for r in at_rows]
    has_down = [(r < last_row).astype(f32) for r in at_rows]
    first = in_ring == 0
    final = in_ring == RING - 1
    here = ring[...]
    beyond = other[...]
    flows = [jnp.where(valid, b, 0.0) for b in (here, beyond)]
    moving = [pltpu.roll(b, PATCH - 2 * COLS, 1) for b in (here, beyond)]
    third = pltpu.roll(here, PATCH - 4 * COLS, 1)

    def moved(x, by):
        by = by % count
        return jnp.concatenate([x[by:], x[:by]], axis=0)

    for sweep in range(SWEEPS):
        spring = springs[pl.ds(2 * sweep, 1), :]
        tether = springs[pl.ds(2 * sweep + 1, 1), :]
        near_x, far_x = moving
        edge_above = jnp.where(other_first, moved(far_x, RING - 1), moved(third, RING - 1))
        edge_below = jnp.where(other_first, moved(third, 1 - RING), moved(far_x, 1 - RING))
        above = (jnp.where(first, edge_above, moved(near_x, -1)), jnp.where(first, moved(near_x, RING - 1), moved(far_x, -1)))
        below = (jnp.where(final, edge_below, moved(near_x, 1)), jnp.where(final, moved(near_x, 1 - RING), moved(far_x, 1)))
        fresh = []
        for k, x in enumerate(moving):
            col_left = pltpu.roll(x, 1, 1)
            col_right = pltpu.roll(x, PATCH - 1, 1)
            laplace = (
                (above[k] - x) * has_up[k]
                + (below[k] - x) * has_down[k]
                + (col_left - x) * has_left
                + (col_right - x) * has_right
            )
            residual = (moved(x, RING) - x - flows[k]) * valid_up
            below_res = jnp.where(section == 0, 0.0, moved(residual, -RING))
            fresh.append(x + step_size * (spring * laplace + tether * (residual - below_res)))
        moving = fresh

    mine = (section == sec) & (in_ring == place)
    for x, ref in ((flows[0], flow_out), (moving[0], moving_out)):
        line = jnp.sum(jnp.where(mine, x, 0.0), axis=0, keepdims=True)
        ref[0, 0] = line[:, :COLS]
        ref[0, 1] = line[:, COLS : 2 * COLS]


def relax(springs, ring, other, shape):
    in_vmem = pl.BlockSpec(memory_space=pltpu.VMEM)
    return pl.pallas_call(
        relax_kernel,
        out_shape=[jax.ShapeDtypeStruct(shape, f32)] * 2,
        in_specs=[in_vmem] * 3,
        out_specs=[in_vmem] * 2,
        compiler_params=pltpu.CompilerParams(vmem_limit_bytes=VMEM_LIMIT),
    )(springs, ring, other)


def shifted(block, axis, distance):
    devices = range(lax.axis_size(axis))
    route = [(i - distance, i) for i in devices if i - distance in devices]
    return lax.ppermute(block, axis, route)


def ring_route(rows, outward):
    route = []
    for r in range(rows):
        step = RING if (r % RING < RING // 2) == outward else -RING
        if 0 <= r - step < rows:
            route.append((r - step, r))
    return route


def per_device(images, initial, offsets, stiffness, plan):
    rows = lax.axis_size("row")
    below = shifted(images, "row", -1)
    remote_initial = lax.ppermute(initial, "row", ring_route(rows, False))
    near = shifted(images, "sec", -1)
    below, remote_initial = lax.optimization_barrier((below, remote_initial))
    near_below = shifted(below, "sec", -1)
    record, springs = prepare(plan, offsets, initial, stiffness, remote_initial)
    count = SECS * RING
    tables = jnp.asarray(constant_tables())
    own_parts = own_spectra(images, below, tables)
    mine = pair_flow(own_parts, near, near_below, record, tables, count)
    groups = [
        [s * rows + RING * g + j for s in range(SECS) for j in range(RING)] for g in range(rows // RING)
    ]
    ring = lax.all_to_all(mine.reshape(count, 1, PATCH), ("sec", "row"), 0, 0, axis_index_groups=groups)
    other = lax.ppermute(ring, "row", ring_route(rows, True))
    return tuple(
        relax(springs, ring.reshape(count, PATCH), other.reshape(count, PATCH), initial.shape)
    )


def solution(mesh):
    return jax.shard_map(
        per_device,
        mesh=mesh,
        in_specs=(
            P("sec", "row", None),
            P("sec", None, "row", None),
            P("sec", None, "row", None),
            P(),
            P(),
        ),
        out_specs=(P("sec", None, "row", None), P("sec", None, "row", None)),
        check_vma=False,
    )
```

```python
import math

import numpy as np
import jax
import jax.numpy as jnp
from jax import lax
from jax.experimental import pallas as pl
from jax.experimental.pallas import tpu as pltpu
from jax.sharding import PartitionSpec as P
import ml_dtypes

PATCH = 128
STRIDE = 64
HALF = 64
SWEEPS = 3
COLS = 16
PAIRS = 8
SECS = 4
RING = 4
SHIFTS = 16
REACH = 5
WIDTH = 1088

step_size = 0.2
floor_ratio = 0.2

VMEM_LIMIT = 24 * 1024 * 1024
PREPARE_FLOPS = 1_000_000_000

f32 = jnp.float32
bf16 = jnp.bfloat16


def dft_halves():
    freq = np.arange(PATCH)
    phase = freq[:, None] * freq[None, :] % PATCH
    folded = np.minimum(phase, PATCH - phase)
    angle = folded * (2.0 * math.pi / PATCH)
    sine = np.sin(angle) * np.where(2 * phase > PATCH, -1.0, 1.0)
    sine = np.where(2 * folded == PATCH, 0.0, sine)
    cosine = np.cos(angle)
    cosine = np.where(4 * folded == PATCH, np.cos(np.float32(math.pi / 2)), cosine)
    return cosine.astype(ml_dtypes.bfloat16), (-sine).astype(ml_dtypes.bfloat16)


def two_parts(table):
    high = table.astype(ml_dtypes.bfloat16)
    low = (table - high.astype(np.float64)).astype(ml_dtypes.bfloat16)
    return high, low


def constant_tables():
    cos_t, sin_t = dft_halves()
    cos_f = cos_t.astype(np.float32)
    sin_f = sin_t.astype(np.float32)
    rows = np.zeros((2 * PATCH, 2 * PATCH), np.float32)
    rows[0:PATCH, 0:HALF] = cos_f[:HALF].T
    rows[0:PATCH, PATCH : PATCH + HALF] = sin_f[:HALF].T
    rows[HALF : HALF + PATCH, HALF:PATCH] = cos_f[:HALF].T
    rows[HALF : HALF + PATCH, PATCH + HALF :] = sin_f[:HALF].T
    nyquist = np.zeros((2 * PATCH, PATCH), np.float32)
    nyquist[0:PATCH, 0::2] = cos_f[HALF][:, None]
    nyquist[HALF : HALF + PATCH, 1::2] = cos_f[HALF][:, None]
    columns = np.block([[cos_f, -sin_f], [sin_f, cos_f]])
    lags = np.arange(SHIFTS) - REACH
    used = (np.arange(SHIFTS) <= 2 * REACH).astype(np.float64)
    freq = np.arange(PATCH)
    turn = (freq[None, :] * lags[:, None] % PATCH) * (2.0 * math.pi / PATCH)
    cos_y = np.cos(turn) * used[:, None]
    sin_y = np.sin(turn) * used[:, None]
    high, low = two_parts(np.block([[cos_y, -sin_y], [sin_y, cos_y]]))
    lag_y = np.concatenate([high, low], axis=0)
    weight = np.where(freq[:HALF] == 0, 1.0, 2.0)
    across = np.zeros((3 * PATCH, PATCH))
    for p in range(2):
        cols = slice(p * HALF, p * HALF + SHIFTS)
        block = slice(p * HALF, (p + 1) * HALF)
        across[:PATCH][block, cols] = (cos_y[:, :HALF] * weight).T
        across[PATCH : 2 * PATCH][block, cols] = (-sin_y[:, :HALF] * weight).T
        for c in range(p, COLS, 2):
            across[2 * PATCH + c, cols] = np.where(lags % 2 == 0, 1.0, -1.0) * used
    high, low = two_parts(across)
    lag_x = np.concatenate([high, low], axis=1)
    lane = np.arange(PATCH)
    patch = (lane % COLS % 2)[None, :] == (lane // HALF)[:, None]
    gather = (patch & (lane < 2 * COLS)[None, :]).astype(np.float32)
    single = (patch & (lane < COLS)[None, :]).astype(np.float32)
    same = ((lane // HALF)[:, None] == (lane // HALF)[None, :]).astype(np.float32)
    blank = np.zeros((PATCH, PATCH), np.float32)
    spread = np.block([[same, gather], [single.T, blank]])
    packed = [rows, np.concatenate([nyquist[:PATCH], nyquist[PATCH:]], axis=1), columns, spread, lag_y, lag_x]
    return np.concatenate([np.asarray(t).astype(ml_dtypes.bfloat16) for t in packed], axis=0)


TABLE_ROWS = {"rows": (0, 256), "nyquist": (256, 128), "columns": (384, 256), "spread": (640, 256)}
TABLE_ROWS |= {"lag_y": (896, 64), "lag_x": (960, 384)}


def table(ref, name):
    start, length = TABLE_ROWS[name]
    return ref[pl.ds(start, length), :]


def three_parts(x):
    high = x.astype(bf16)
    rest = x - high.astype(f32)
    mid = rest.astype(bf16)
    low = (rest - mid.astype(f32)).astype(bf16)
    return jnp.concatenate([high, mid, low], axis=0)


def dot(a, b):
    return jnp.dot(a, b, preferred_element_type=f32)


def prepare_kernel(plan, initial, stiffness, record, springs):
    record[...] = jnp.zeros((1, PATCH), f32)
    for i in range(2):
        record[:, pl.ds((2 + i) * COLS, COLS)] = initial[0, i]
    level_id = lax.broadcasted_iota(jnp.int32, stiffness.shape, 1)
    for sweep in range(SWEEPS):
        picked = jnp.sum(jnp.where(level_id == plan[sweep], stiffness[...], 0.0), axis=1, keepdims=True)
        springs[pl.ds(2 * sweep, 2), :] = jnp.broadcast_to(picked, (2, PATCH))


def prepare(plan, initial, stiffness):
    in_vmem = pl.BlockSpec(memory_space=pltpu.VMEM)
    return pl.pallas_call(
        prepare_kernel,
        out_shape=[jax.ShapeDtypeStruct((1, PATCH), f32), jax.ShapeDtypeStruct((8, PATCH), f32)],
        in_specs=[pl.BlockSpec(memory_space=pltpu.SMEM), in_vmem, in_vmem],
        out_specs=[in_vmem] * 2,
        compiler_params=pltpu.CompilerParams(vmem_limit_bytes=VMEM_LIMIT),
        cost_estimate=pl.CostEstimate(flops=PREPARE_FLOPS, bytes_accessed=10_000, transcendentals=0),
    )(plan, initial, stiffness.T)


def section_spectra(upper, lower, tables):
    nyq_t = table(tables, "nyquist")
    nyq_t = jnp.concatenate([nyq_t[:, :PATCH], nyq_t[:, PATCH:]], axis=0)
    rows_t = jnp.concatenate([table(tables, "rows"), nyq_t], axis=1)
    columns = table(tables, "columns")
    lane = lax.broadcasted_iota(jnp.int32, (PATCH, PATCH), 1)
    nyquist = jnp.zeros((PATCH, PATCH), f32)
    stacked = []
    for m in range(PAIRS):
        span = 2 * PATCH if m < PAIRS - 1 else WIDTH - m * PATCH
        tile = jnp.concatenate([upper(m * PATCH, span), lower(m * PATCH, span)], axis=0)
        seg = dot(tile, rows_t[:span])
        nyquist = jnp.where(lane // 2 == m, seg[:, 2 * PATCH :], nyquist)
        seg = seg[:, : 2 * PATCH].astype(bf16)
        stacked.append(jnp.concatenate([seg[:, :PATCH], seg[:, PATCH:]], axis=0))
    spectra = []
    for m in range(0, PAIRS, 2):
        product = dot(columns, jnp.concatenate(stacked[m : m + 2], axis=1)).astype(bf16)
        spectra += [product[:, :PATCH], product[:, PATCH:]]
    spectra.append(dot(columns[:, :PATCH], nyquist.astype(bf16)).astype(bf16))
    return spectra


def energy(spectrum):
    wide = spectrum.astype(f32)
    return jnp.sum(wide * wide, axis=0, keepdims=True)


def block_tile(ref):
    return lambda start, span: ref[0, :, pl.ds(start, span)]


def own_kernel(own, below, tables, spec, energies):
    for m, spectrum in enumerate(section_spectra(block_tile(own), block_tile(below), tables)):
        spec[m] = spectrum
        energies[pl.ds(m, 1), :] = energy(spectrum)


def own_spectra(own, below, tables):
    in_vmem = pl.BlockSpec(memory_space=pltpu.VMEM)
    return pl.pallas_call(
        own_kernel,
        out_shape=[
            jax.ShapeDtypeStruct((PAIRS + 1, 2 * PATCH, PATCH), bf16),
            jax.ShapeDtypeStruct((2 * PAIRS, PATCH), f32),
        ],
        in_specs=[in_vmem] * 3,
        out_specs=[in_vmem] * 2,
        compiler_params=pltpu.CompilerParams(vmem_limit_bytes=VMEM_LIMIT),
        cost_estimate=pl.CostEstimate(flops=600_000_000, bytes_accessed=2_000_000, transcendentals=0),
    )(own, below, tables)


def flow_kernel(own_spec, own_energies, near, near_below, record, remote, shifts_in, tables, out, spec, lagged, shift_row):
    spread = table(tables, "spread")
    energies = []
    for m, spectrum in enumerate(section_spectra(block_tile(near), block_tile(near_below), tables)):
        spec[m] = spectrum
        energies.append(energy(spectrum))

    lane = lax.broadcasted_iota(jnp.int32, (PAIRS, PATCH), 1)
    pair = lax.broadcasted_iota(jnp.int32, (PAIRS, PATCH), 0)
    own_pair = (lane % COLS) // 2 == pair
    first_16 = own_pair & (lane < COLS)
    weight = jnp.where(lane % HALF == 0, 1.0, 2.0)

    def halves(x):
        return x[:, :PATCH], x[:, PATCH:]

    def totals(main, extra):
        left = jnp.concatenate([main * weight, jnp.where(first_16, extra, 0.0)], axis=1)
        found = dot(three_parts(left), spread)
        found = found[:PAIRS] + found[PAIRS : 2 * PAIRS] + found[2 * PAIRS :]
        by_pair, by_patch = halves(found)
        by_patch = jnp.sum(jnp.where(first_16, by_patch, 0.0), axis=0, keepdims=True) + extra
        scale = 1.0 / (PATCH * PATCH)
        return jnp.sqrt(by_pair * scale + 1e-06), jnp.sqrt(by_patch * scale + 1e-06)

    low_pair, low_patch = totals(jnp.concatenate(energies[:PAIRS], axis=0), energies[PAIRS])
    up_pair, up_patch = totals(own_energies[pl.ds(0, PAIRS), :], own_energies[pl.ds(PAIRS, 1), :])
    floor_pair = floor_ratio * low_pair * up_pair
    floor_patch = floor_ratio * low_patch * up_patch

    for m in range(PAIRS + 1):
        floor = floor_pair[m : m + 1] if m < PAIRS else floor_patch
        low_re = spec[m, pl.ds(0, PATCH)].astype(f32)
        low_im = spec[m, pl.ds(PATCH, PATCH)].astype(f32)
        up_re = own_spec[m, pl.ds(0, PATCH)].astype(f32)
        up_im = own_spec[m, pl.ds(PATCH, PATCH)].astype(f32)
        cross_re = low_re * up_re + low_im * up_im
        cross_im = low_re * up_im - low_im * up_re
        square = cross_re * cross_re + cross_im * cross_im
        modulus = square * lax.rsqrt(jnp.maximum(square, 1e-36))
        inverse = 1.0 / (modulus + floor)
        white = jnp.concatenate([cross_re * inverse, cross_im * inverse], axis=0)
        high = white.astype(bf16)
        low = (white - high.astype(f32)).astype(bf16)
        found = dot(table(tables, "lag_y"), jnp.concatenate([high, low], axis=1))
        part = found[: 2 * SHIFTS, :PATCH] + found[: 2 * SHIFTS, PATCH:] + found[2 * SHIFTS :, :PATCH]
        lagged[pl.ds(m * SHIFTS, SHIFTS), pl.ds(0, PATCH)] = part[:SHIFTS]
        lagged[pl.ds(m * SHIFTS, SHIFTS), pl.ds(PATCH, PATCH)] = part[SHIFTS:]

    extra = lagged[pl.ds(PAIRS * SHIFTS, SHIFTS), pl.ds(0, PATCH)]
    extra = jnp.where(first_16[:, None, :], extra[None], 0.0).reshape(PAIRS * SHIFTS, PATCH)
    left = jnp.concatenate([lagged[pl.ds(0, PAIRS * SHIFTS), :], extra], axis=1)
    high = left.astype(bf16)
    low = (left - high.astype(f32)).astype(bf16)
    rows_all = PAIRS * SHIFTS
    found = dot(jnp.concatenate([high, low], axis=0), table(tables, "lag_x"))
    surface = found[:rows_all, :PATCH] + found[:rows_all, PATCH:] + found[rows_all:, :PATCH]
    surface = surface.reshape(PAIRS, SHIFTS, PATCH)

    shift_row[...] = record[...]
    for i in range(2):
        shift_row[:, pl.ds(i * COLS, COLS)] = shifts_in[0, i].astype(f32)
    rec = shift_row[...]
    at_y = jnp.where(first_16, rec, 0.0)
    at_x = jnp.where(own_pair & (lane >= COLS) & (lane < 2 * COLS), rec, 0.0)
    gather = spread[:PATCH, PATCH:]
    shifts = lax.dot_general(
        jnp.concatenate([at_y, at_x], axis=0).astype(bf16),
        gather,
        (((1,), (1,)), ((), ())),
        preferred_element_type=f32,
    )
    lag_row = lax.broadcasted_iota(jnp.int32, (PAIRS, SHIFTS, PATCH), 1).astype(f32) - REACH
    lag_col = (lax.broadcasted_iota(jnp.int32, (PAIRS, SHIFTS, PATCH), 2) % HALF).astype(f32) - REACH
    dy = lag_row - shifts[:PAIRS][:, None, :]
    dx = lag_col - shifts[PAIRS:][:, None, :]
    mid_y, up_y, down_y = ((dy == k).astype(f32) for k in (0.0, 1.0, -1.0))
    mid_x, up_x, down_x = ((dx == k).astype(f32) for k in (0.0, 1.0, -1.0))
    at_mid_x = surface * mid_x
    at_mid_y = surface * mid_y
    picks = [
        jnp.sum(at_mid_x * (up_y - down_y), axis=1),
        jnp.sum(at_mid_x * (2.0 * mid_y - up_y - down_y), axis=1),
        jnp.sum(at_mid_y * (up_x - down_x), axis=1),
        jnp.sum(at_mid_y * (2.0 * mid_x - up_x - down_x), axis=1),
    ]
    found = dot(three_parts(jnp.concatenate(picks, axis=0)), gather)
    found = found[: 4 * PAIRS] + found[4 * PAIRS : 8 * PAIRS] + found[8 * PAIRS :]
    found = found.reshape(4, PAIRS, PATCH)
    found = jnp.sum(jnp.where(own_pair[None], found, 0.0), axis=1) * (1.0 / (PATCH * PATCH))
    lane_1 = lax.broadcasted_iota(jnp.int32, (1, PATCH), 1)
    slope = jnp.where(lane_1 < COLS, found[0:1], found[2:3])
    bend = jnp.where(lane_1 < COLS, found[1:2], found[3:4])
    flow = rec + 0.5 * slope / (1.0 + jnp.abs(bend))
    result = jnp.where(lane_1 < 2 * COLS, flow, rec)
    out[...] = jnp.broadcast_to(result, out.shape)
    for i in range(2):
        out[:, pl.ds((4 + i) * COLS, COLS)] = jnp.broadcast_to(remote[0, i], (out.shape[0], COLS))


def pair_flow(own_parts, near, near_below, record, remote_initial, offsets, tables, copies):
    operands = (*own_parts, near, near_below, record, remote_initial, offsets, tables)
    return pl.pallas_call(
        flow_kernel,
        out_shape=jax.ShapeDtypeStruct((copies, PATCH), f32),
        in_specs=[pl.BlockSpec(memory_space=pltpu.VMEM)] * len(operands),
        out_specs=pl.BlockSpec(memory_space=pltpu.VMEM),
        scratch_shapes=[
            pltpu.VMEM((PAIRS + 1, 2 * PATCH, PATCH), bf16),
            pltpu.VMEM(((PAIRS + 1) * SHIFTS, 2 * PATCH), f32),
            pltpu.VMEM((1, PATCH), f32),
        ],
        compiler_params=pltpu.CompilerParams(vmem_limit_bytes=VMEM_LIMIT),
    )(*operands)


def relax_kernel(springs, ring, other, flow_out, moving_out):
    sec = lax.axis_index("sec")
    row = lax.axis_index("row")
    last_row = lax.axis_size("row") - 1
    place = lax.rem(row, RING)
    base = row - place
    count = SECS * RING
    node = lax.broadcasted_iota(jnp.int32, (count, PATCH), 0)
    lane = lax.broadcasted_iota(jnp.int32, (count, PATCH), 1)
    in_ring = node % RING
    section = node // RING
    other_first = jnp.broadcast_to(place, (count, PATCH)) < RING // 2
    valid = (section < SECS - 1) & (lane < 2 * COLS)
    valid_up = valid.astype(f32)
    has_left = (lane % COLS > 0).astype(f32)
    has_right = (lane % COLS < COLS - 1).astype(f32)
    row_here = base + in_ring
    row_other = row_here + jnp.where(other_first, -RING, RING)
    at_rows = (row_here, row_other)
    has_up = [(r > 0).astype(f32) for r in at_rows]
    has_down = [(r < last_row).astype(f32) for r in at_rows]
    first = in_ring == 0
    final = in_ring == RING - 1
    here = ring[...]
    beyond = other[...]
    moving = [pltpu.roll(b, PATCH - 2 * COLS, 1) for b in (here, beyond)]
    third = pltpu.roll(here, PATCH - 4 * COLS, 1)

    def moved(x, by):
        by = by % count
        return jnp.concatenate([x[by:], x[:by]], axis=0)

    flows = [jnp.where(valid, moved(b, RING), 0.0) for b in (here, beyond)]

    for sweep in range(SWEEPS):
        spring = springs[pl.ds(2 * sweep, 1), :]
        tether = springs[pl.ds(2 * sweep + 1, 1), :]
        near_x, far_x = moving
        edge_above = jnp.where(other_first, moved(far_x, RING - 1), moved(third, RING - 1))
        edge_below = jnp.where(other_first, moved(third, 1 - RING), moved(far_x, 1 - RING))
        above = (jnp.where(first, edge_above, moved(near_x, -1)), jnp.where(first, moved(near_x, RING - 1), moved(far_x, -1)))
        below = (jnp.where(final, edge_below, moved(near_x, 1)), jnp.where(final, moved(near_x, 1 - RING), moved(far_x, 1)))
        fresh = []
        for k, x in enumerate(moving):
            col_left = pltpu.roll(x, 1, 1)
            col_right = pltpu.roll(x, PATCH - 1, 1)
            laplace = (
                (above[k] - x) * has_up[k]
                + (below[k] - x) * has_down[k]
                + (col_left - x) * has_left
                + (col_right - x) * has_right
            )
            residual = (moved(x, RING) - x - flows[k]) * valid_up
            below_res = jnp.where(section == 0, 0.0, moved(residual, -RING))
            fresh.append(x + step_size * (spring * laplace + tether * (residual - below_res)))
        moving = fresh

    mine = (section == sec) & (in_ring == place)
    for x, ref in ((flows[0], flow_out), (moving[0], moving_out)):
        line = jnp.sum(jnp.where(mine, x, 0.0), axis=0, keepdims=True)
        ref[0, 0] = line[:, :COLS]
        ref[0, 1] = line[:, COLS : 2 * COLS]


def relax(springs, ring, other, shape):
    in_vmem = pl.BlockSpec(memory_space=pltpu.VMEM)
    return pl.pallas_call(
        relax_kernel,
        out_shape=[jax.ShapeDtypeStruct(shape, f32)] * 2,
        in_specs=[in_vmem] * 3,
        out_specs=[in_vmem] * 2,
        compiler_params=pltpu.CompilerParams(vmem_limit_bytes=VMEM_LIMIT),
    )(springs, ring, other)


def shifted(block, axis, distance):
    devices = range(lax.axis_size(axis))
    route = [(i - distance, i) for i in devices if i - distance in devices]
    return lax.ppermute(block, axis, route)


def ring_route(rows, outward):
    route = []
    for r in range(rows):
        step = RING if (r % RING < RING // 2) == outward else -RING
        if 0 <= r - step < rows:
            route.append((r - step, r))
    return route


def per_device(images, initial, offsets, stiffness, plan):
    rows = lax.axis_size("row")
    below = shifted(images, "row", -1)
    remote_initial = lax.ppermute(initial, "row", ring_route(rows, False))
    near_offsets = shifted(offsets, "sec", 1)
    record, springs = prepare(plan, initial, stiffness)
    later_images, record, springs = lax.optimization_barrier((images, record, springs))
    near = shifted(later_images, "sec", 1)
    below, near_offsets, remote_initial, record, springs = lax.optimization_barrier(
        (below, near_offsets, remote_initial, record, springs)
    )
    near_below = shifted(below, "sec", 1)
    count = SECS * RING
    tables = jnp.asarray(constant_tables())
    own_parts = own_spectra(images, below, tables)
    mine = pair_flow(own_parts, near, near_below, record, remote_initial, near_offsets, tables, count)
    groups = [
        [s * rows + RING * g + j for s in range(SECS) for j in range(RING)] for g in range(rows // RING)
    ]
    ring = lax.all_to_all(mine.reshape(count, 1, PATCH), ("sec", "row"), 0, 0, axis_index_groups=groups)
    other = lax.ppermute(ring, "row", ring_route(rows, True))
    return tuple(
        relax(springs, ring.reshape(count, PATCH), other.reshape(count, PATCH), initial.shape)
    )


def solution(mesh):
    return jax.shard_map(
        per_device,
        mesh=mesh,
        in_specs=(
            P("sec", "row", None),
            P("sec", None, "row", None),
            P("sec", None, "row", None),
            P(),
            P(),
        ),
        out_specs=(P("sec", None, "row", None), P("sec", None, "row", None)),
        check_vma=False,
    )
```

```python
import math

import numpy as np
import jax
import jax.numpy as jnp
from jax import lax
from jax.experimental import pallas as pl
from jax.experimental.pallas import tpu as pltpu
from jax.sharding import PartitionSpec as P
import ml_dtypes

PATCH = 128
STRIDE = 64
HALF = 64
SWEEPS = 3
COLS = 16
PAIRS = 8
SECS = 4
RING = 4
SHIFTS = 16
REACH = 5
WIDTH = 1088

step_size = 0.2
floor_ratio = 0.2

VMEM_LIMIT = 24 * 1024 * 1024
PREPARE_FLOPS = 1_000_000_000

f32 = jnp.float32
bf16 = jnp.bfloat16


def dft_halves():
    freq = np.arange(PATCH)
    phase = freq[:, None] * freq[None, :] % PATCH
    folded = np.minimum(phase, PATCH - phase)
    angle = folded * (2.0 * math.pi / PATCH)
    sine = np.sin(angle) * np.where(2 * phase > PATCH, -1.0, 1.0)
    sine = np.where(2 * folded == PATCH, 0.0, sine)
    cosine = np.cos(angle)
    cosine = np.where(4 * folded == PATCH, np.cos(np.float32(math.pi / 2)), cosine)
    return cosine.astype(ml_dtypes.bfloat16), (-sine).astype(ml_dtypes.bfloat16)


def two_parts(table):
    high = table.astype(ml_dtypes.bfloat16)
    low = (table - high.astype(np.float64)).astype(ml_dtypes.bfloat16)
    return high, low


def constant_tables():
    cos_t, sin_t = dft_halves()
    cos_f = cos_t.astype(np.float32)
    sin_f = sin_t.astype(np.float32)
    rows = np.zeros((2 * PATCH, 2 * PATCH), np.float32)
    rows[0:PATCH, 0:HALF] = cos_f[:HALF].T
    rows[0:PATCH, PATCH : PATCH + HALF] = sin_f[:HALF].T
    rows[HALF : HALF + PATCH, HALF:PATCH] = cos_f[:HALF].T
    rows[HALF : HALF + PATCH, PATCH + HALF :] = sin_f[:HALF].T
    nyquist = np.zeros((2 * PATCH, PATCH), np.float32)
    nyquist[0:PATCH, 0::2] = cos_f[HALF][:, None]
    nyquist[HALF : HALF + PATCH, 1::2] = cos_f[HALF][:, None]
    columns = np.block([[cos_f, -sin_f], [sin_f, cos_f]])
    lags = np.arange(SHIFTS) - REACH
    used = (np.arange(SHIFTS) <= 2 * REACH).astype(np.float64)
    freq = np.arange(PATCH)
    turn = (freq[None, :] * lags[:, None] % PATCH) * (2.0 * math.pi / PATCH)
    cos_y = np.cos(turn) * used[:, None]
    sin_y = np.sin(turn) * used[:, None]
    high, low = two_parts(np.block([[cos_y, -sin_y], [sin_y, cos_y]]))
    lag_y = np.concatenate([high, low], axis=0)
    weight = np.where(freq[:HALF] == 0, 1.0, 2.0)
    across = np.zeros((3 * PATCH, PATCH))
    for p in range(2):
        cols = slice(p * HALF, p * HALF + SHIFTS)
        block = slice(p * HALF, (p + 1) * HALF)
        across[:PATCH][block, cols] = (cos_y[:, :HALF] * weight).T
        across[PATCH : 2 * PATCH][block, cols] = (-sin_y[:, :HALF] * weight).T
        for c in range(p, COLS, 2):
            across[2 * PATCH + c, cols] = np.where(lags % 2 == 0, 1.0, -1.0) * used
    high, low = two_parts(across)
    lag_x = np.concatenate([high, low], axis=1)
    lane = np.arange(PATCH)
    patch = (lane % COLS % 2)[None, :] == (lane // HALF)[:, None]
    gather = (patch & (lane < 2 * COLS)[None, :]).astype(np.float32)
    single = (patch & (lane < COLS)[None, :]).astype(np.float32)
    same = ((lane // HALF)[:, None] == (lane // HALF)[None, :]).astype(np.float32)
    blank = np.zeros((PATCH, PATCH), np.float32)
    spread = np.block([[same, gather], [single.T, blank]])
    packed = [rows, np.concatenate([nyquist[:PATCH], nyquist[PATCH:]], axis=1), columns, spread, lag_y, lag_x]
    return np.concatenate([np.asarray(t).astype(ml_dtypes.bfloat16) for t in packed], axis=0)


TABLE_ROWS = {"rows": (0, 256), "nyquist": (256, 128), "columns": (384, 256), "spread": (640, 256)}
TABLE_ROWS |= {"lag_y": (896, 64), "lag_x": (960, 384)}


def table(ref, name):
    start, length = TABLE_ROWS[name]
    return ref[pl.ds(start, length), :]


def three_parts(x):
    high = x.astype(bf16)
    rest = x - high.astype(f32)
    mid = rest.astype(bf16)
    low = (rest - mid.astype(f32)).astype(bf16)
    return jnp.concatenate([high, mid, low], axis=0)


def dot(a, b):
    return jnp.dot(a, b, preferred_element_type=f32)


def prepare_kernel(plan, initial, stiffness, record, springs):
    record[...] = jnp.zeros((1, PATCH), f32)
    for i in range(2):
        record[:, pl.ds((2 + i) * COLS, COLS)] = initial[0, i]
    level_id = lax.broadcasted_iota(jnp.int32, stiffness.shape, 1)
    for sweep in range(SWEEPS):
        picked = jnp.sum(jnp.where(level_id == plan[sweep], stiffness[...], 0.0), axis=1, keepdims=True)
        springs[pl.ds(2 * sweep, 2), :] = jnp.broadcast_to(picked, (2, PATCH))


def prepare(plan, initial, stiffness):
    in_vmem = pl.BlockSpec(memory_space=pltpu.VMEM)
    return pl.pallas_call(
        prepare_kernel,
        out_shape=[jax.ShapeDtypeStruct((1, PATCH), f32), jax.ShapeDtypeStruct((8, PATCH), f32)],
        in_specs=[pl.BlockSpec(memory_space=pltpu.SMEM), in_vmem, in_vmem],
        out_specs=[in_vmem] * 2,
        compiler_params=pltpu.CompilerParams(vmem_limit_bytes=VMEM_LIMIT),
        cost_estimate=pl.CostEstimate(flops=PREPARE_FLOPS, bytes_accessed=10_000, transcendentals=0),
    )(plan, initial, stiffness.T)


def section_spectra(upper, lower, tables):
    nyq_t = table(tables, "nyquist")
    nyq_t = jnp.concatenate([nyq_t[:, :PATCH], nyq_t[:, PATCH:]], axis=0)
    rows_t = jnp.concatenate([table(tables, "rows"), nyq_t], axis=1)
    columns = table(tables, "columns")
    lane = lax.broadcasted_iota(jnp.int32, (PATCH, PATCH), 1)
    nyquist = jnp.zeros((PATCH, PATCH), f32)
    stacked = []
    for m in range(PAIRS):
        span = 2 * PATCH if m < PAIRS - 1 else WIDTH - m * PATCH
        tile = jnp.concatenate([upper(m * PATCH, span), lower(m * PATCH, span)], axis=0)
        seg = dot(tile, rows_t[:span])
        nyquist = jnp.where(lane // 2 == m, seg[:, 2 * PATCH :], nyquist)
        seg = seg[:, : 2 * PATCH].astype(bf16)
        stacked.append(jnp.concatenate([seg[:, :PATCH], seg[:, PATCH:]], axis=0))
    spectra = []
    for m in range(0, PAIRS, 2):
        product = dot(columns, jnp.concatenate(stacked[m : m + 2], axis=1)).astype(bf16)
        spectra += [product[:, :PATCH], product[:, PATCH:]]
    spectra.append(dot(columns[:, :PATCH], nyquist.astype(bf16)).astype(bf16))
    return spectra


def energy(spectrum):
    wide = spectrum.astype(f32)
    return jnp.sum(wide * wide, axis=0, keepdims=True)


def block_tile(ref):
    return lambda start, span: ref[0, :, pl.ds(start, span)]


def own_kernel(own, below, tables, spec, energies):
    for m, spectrum in enumerate(section_spectra(block_tile(own), block_tile(below), tables)):
        spec[m] = spectrum
        energies[pl.ds(m, 1), :] = energy(spectrum)


def own_spectra(own, below, tables):
    in_vmem = pl.BlockSpec(memory_space=pltpu.VMEM)
    return pl.pallas_call(
        own_kernel,
        out_shape=[
            jax.ShapeDtypeStruct((PAIRS + 1, 2 * PATCH, PATCH), bf16),
            jax.ShapeDtypeStruct((2 * PAIRS, PATCH), f32),
        ],
        in_specs=[in_vmem] * 3,
        out_specs=[in_vmem] * 2,
        compiler_params=pltpu.CompilerParams(vmem_limit_bytes=VMEM_LIMIT),
        cost_estimate=pl.CostEstimate(flops=600_000_000, bytes_accessed=2_000_000, transcendentals=0),
    )(own, below, tables)


def flow_kernel(
    own_spec, own_energies, near, near_below, lower, record, remote, shifts_in, tables, out, spec, lagged, shift_row
):
    spread = table(tables, "spread")
    energies = []

    def second(start, span):
        return near_below[0, :, pl.ds(start, span)] + lower[0, :, pl.ds(start, span)]

    for m, spectrum in enumerate(section_spectra(block_tile(near), second, tables)):
        spec[m] = spectrum
        energies.append(energy(spectrum))

    lane = lax.broadcasted_iota(jnp.int32, (PAIRS, PATCH), 1)
    pair = lax.broadcasted_iota(jnp.int32, (PAIRS, PATCH), 0)
    own_pair = (lane % COLS) // 2 == pair
    first_16 = own_pair & (lane < COLS)
    weight = jnp.where(lane % HALF == 0, 1.0, 2.0)

    def halves(x):
        return x[:, :PATCH], x[:, PATCH:]

    def totals(main, extra):
        left = jnp.concatenate([main * weight, jnp.where(first_16, extra, 0.0)], axis=1)
        found = dot(three_parts(left), spread)
        found = found[:PAIRS] + found[PAIRS : 2 * PAIRS] + found[2 * PAIRS :]
        by_pair, by_patch = halves(found)
        by_patch = jnp.sum(jnp.where(first_16, by_patch, 0.0), axis=0, keepdims=True) + extra
        scale = 1.0 / (PATCH * PATCH)
        return jnp.sqrt(by_pair * scale + 1e-06), jnp.sqrt(by_patch * scale + 1e-06)

    low_pair, low_patch = totals(jnp.concatenate(energies[:PAIRS], axis=0), energies[PAIRS])
    up_pair, up_patch = totals(own_energies[pl.ds(0, PAIRS), :], own_energies[pl.ds(PAIRS, 1), :])
    floor_pair = floor_ratio * low_pair * up_pair
    floor_patch = floor_ratio * low_patch * up_patch

    for m in range(PAIRS + 1):
        floor = floor_pair[m : m + 1] if m < PAIRS else floor_patch
        low_re = spec[m, pl.ds(0, PATCH)].astype(f32)
        low_im = spec[m, pl.ds(PATCH, PATCH)].astype(f32)
        up_re = own_spec[m, pl.ds(0, PATCH)].astype(f32)
        up_im = own_spec[m, pl.ds(PATCH, PATCH)].astype(f32)
        cross_re = low_re * up_re + low_im * up_im
        cross_im = low_re * up_im - low_im * up_re
        square = cross_re * cross_re + cross_im * cross_im
        modulus = square * lax.rsqrt(jnp.maximum(square, 1e-36))
        inverse = 1.0 / (modulus + floor)
        white = jnp.concatenate([cross_re * inverse, cross_im * inverse], axis=0)
        high = white.astype(bf16)
        low = (white - high.astype(f32)).astype(bf16)
        found = dot(table(tables, "lag_y"), jnp.concatenate([high, low], axis=1))
        part = found[: 2 * SHIFTS, :PATCH] + found[: 2 * SHIFTS, PATCH:] + found[2 * SHIFTS :, :PATCH]
        lagged[pl.ds(m * SHIFTS, SHIFTS), pl.ds(0, PATCH)] = part[:SHIFTS]
        lagged[pl.ds(m * SHIFTS, SHIFTS), pl.ds(PATCH, PATCH)] = part[SHIFTS:]

    extra = lagged[pl.ds(PAIRS * SHIFTS, SHIFTS), pl.ds(0, PATCH)]
    extra = jnp.where(first_16[:, None, :], extra[None], 0.0).reshape(PAIRS * SHIFTS, PATCH)
    left = jnp.concatenate([lagged[pl.ds(0, PAIRS * SHIFTS), :], extra], axis=1)
    high = left.astype(bf16)
    low = (left - high.astype(f32)).astype(bf16)
    rows_all = PAIRS * SHIFTS
    found = dot(jnp.concatenate([high, low], axis=0), table(tables, "lag_x"))
    surface = found[:rows_all, :PATCH] + found[:rows_all, PATCH:] + found[rows_all:, :PATCH]
    surface = surface.reshape(PAIRS, SHIFTS, PATCH)

    shift_row[...] = record[...]
    for i in range(2):
        shift_row[:, pl.ds(i * COLS, COLS)] = shifts_in[0, i].astype(f32)
    rec = shift_row[...]
    at_y = jnp.where(first_16, rec, 0.0)
    at_x = jnp.where(own_pair & (lane >= COLS) & (lane < 2 * COLS), rec, 0.0)
    gather = spread[:PATCH, PATCH:]
    shifts = lax.dot_general(
        jnp.concatenate([at_y, at_x], axis=0).astype(bf16),
        gather,
        (((1,), (1,)), ((), ())),
        preferred_element_type=f32,
    )
    lag_row = lax.broadcasted_iota(jnp.int32, (PAIRS, SHIFTS, PATCH), 1).astype(f32) - REACH
    lag_col = (lax.broadcasted_iota(jnp.int32, (PAIRS, SHIFTS, PATCH), 2) % HALF).astype(f32) - REACH
    dy = lag_row - shifts[:PAIRS][:, None, :]
    dx = lag_col - shifts[PAIRS:][:, None, :]
    mid_y, up_y, down_y = ((dy == k).astype(f32) for k in (0.0, 1.0, -1.0))
    mid_x, up_x, down_x = ((dx == k).astype(f32) for k in (0.0, 1.0, -1.0))
    at_mid_x = surface * mid_x
    at_mid_y = surface * mid_y
    picks = [
        jnp.sum(at_mid_x * (up_y - down_y), axis=1),
        jnp.sum(at_mid_x * (2.0 * mid_y - up_y - down_y), axis=1),
        jnp.sum(at_mid_y * (up_x - down_x), axis=1),
        jnp.sum(at_mid_y * (2.0 * mid_x - up_x - down_x), axis=1),
    ]
    found = dot(three_parts(jnp.concatenate(picks, axis=0)), gather)
    found = found[: 4 * PAIRS] + found[4 * PAIRS : 8 * PAIRS] + found[8 * PAIRS :]
    found = found.reshape(4, PAIRS, PATCH)
    found = jnp.sum(jnp.where(own_pair[None], found, 0.0), axis=1) * (1.0 / (PATCH * PATCH))
    lane_1 = lax.broadcasted_iota(jnp.int32, (1, PATCH), 1)
    slope = jnp.where(lane_1 < COLS, found[0:1], found[2:3])
    bend = jnp.where(lane_1 < COLS, found[1:2], found[3:4])
    flow = rec + 0.5 * slope / (1.0 + jnp.abs(bend))
    result = jnp.where(lane_1 < 2 * COLS, flow, rec)
    out[...] = jnp.broadcast_to(result, out.shape)
    for i in range(2):
        out[:, pl.ds((4 + i) * COLS, COLS)] = jnp.broadcast_to(remote[0, i], (out.shape[0], COLS))


def pair_flow(own_parts, near, near_below, lower, record, remote_initial, offsets, tables, copies):
    operands = (*own_parts, near, near_below, lower, record, remote_initial, offsets, tables)
    return pl.pallas_call(
        flow_kernel,
        out_shape=jax.ShapeDtypeStruct((copies, PATCH), f32),
        in_specs=[pl.BlockSpec(memory_space=pltpu.VMEM)] * len(operands),
        out_specs=pl.BlockSpec(memory_space=pltpu.VMEM),
        scratch_shapes=[
            pltpu.VMEM((PAIRS + 1, 2 * PATCH, PATCH), bf16),
            pltpu.VMEM(((PAIRS + 1) * SHIFTS, 2 * PATCH), f32),
            pltpu.VMEM((1, PATCH), f32),
        ],
        compiler_params=pltpu.CompilerParams(vmem_limit_bytes=VMEM_LIMIT),
    )(*operands)


def relax_kernel(springs, ring, other, flow_out, moving_out):
    sec = lax.axis_index("sec")
    row = lax.axis_index("row")
    last_row = lax.axis_size("row") - 1
    place = lax.rem(row, RING)
    base = row - place
    count = SECS * RING
    node = lax.broadcasted_iota(jnp.int32, (count, PATCH), 0)
    lane = lax.broadcasted_iota(jnp.int32, (count, PATCH), 1)
    in_ring = node % RING
    section = node // RING
    other_first = jnp.broadcast_to(place, (count, PATCH)) < RING // 2
    valid = (section < SECS - 1) & (lane < 2 * COLS)
    valid_up = valid.astype(f32)
    has_left = (lane % COLS > 0).astype(f32)
    has_right = (lane % COLS < COLS - 1).astype(f32)
    row_here = base + in_ring
    row_other = row_here + jnp.where(other_first, -RING, RING)
    at_rows = (row_here, row_other)
    has_up = [(r > 0).astype(f32) for r in at_rows]
    has_down = [(r < last_row).astype(f32) for r in at_rows]
    first = in_ring == 0
    final = in_ring == RING - 1
    here = ring[...]
    beyond = other[...]
    moving = [pltpu.roll(b, PATCH - 2 * COLS, 1) for b in (here, beyond)]
    third = pltpu.roll(here, PATCH - 4 * COLS, 1)

    def moved(x, by):
        by = by % count
        return jnp.concatenate([x[by:], x[:by]], axis=0)

    flows = [jnp.where(valid, moved(b, RING), 0.0) for b in (here, beyond)]

    for sweep in range(SWEEPS):
        spring = springs[pl.ds(2 * sweep, 1), :]
        tether = springs[pl.ds(2 * sweep + 1, 1), :]
        near_x, far_x = moving
        edge_above = jnp.where(other_first, moved(far_x, RING - 1), moved(third, RING - 1))
        edge_below = jnp.where(other_first, moved(third, 1 - RING), moved(far_x, 1 - RING))
        above = (jnp.where(first, edge_above, moved(near_x, -1)), jnp.where(first, moved(near_x, RING - 1), moved(far_x, -1)))
        below = (jnp.where(final, edge_below, moved(near_x, 1)), jnp.where(final, moved(near_x, 1 - RING), moved(far_x, 1)))
        fresh = []
        for k, x in enumerate(moving):
            col_left = pltpu.roll(x, 1, 1)
            col_right = pltpu.roll(x, PATCH - 1, 1)
            laplace = (
                (above[k] - x) * has_up[k]
                + (below[k] - x) * has_down[k]
                + (col_left - x) * has_left
                + (col_right - x) * has_right
            )
            residual = (moved(x, RING) - x - flows[k]) * valid_up
            below_res = jnp.where(section == 0, 0.0, moved(residual, -RING))
            fresh.append(x + step_size * (spring * laplace + tether * (residual - below_res)))
        moving = fresh

    mine = (section == sec) & (in_ring == place)
    for x, ref in ((flows[0], flow_out), (moving[0], moving_out)):
        line = jnp.sum(jnp.where(mine, x, 0.0), axis=0, keepdims=True)
        ref[0, 0] = line[:, :COLS]
        ref[0, 1] = line[:, COLS : 2 * COLS]


def relax(springs, ring, other, shape):
    in_vmem = pl.BlockSpec(memory_space=pltpu.VMEM)
    return pl.pallas_call(
        relax_kernel,
        out_shape=[jax.ShapeDtypeStruct(shape, f32)] * 2,
        in_specs=[in_vmem] * 3,
        out_specs=[in_vmem] * 2,
        compiler_params=pltpu.CompilerParams(vmem_limit_bytes=VMEM_LIMIT),
    )(springs, ring, other)


def shifted(block, axis, distance):
    devices = range(lax.axis_size(axis))
    route = [(i - distance, i) for i in devices if i - distance in devices]
    return lax.ppermute(block, axis, route)


def ring_route(rows, outward):
    route = []
    for r in range(rows):
        step = RING if (r % RING < RING // 2) == outward else -RING
        if 0 <= r - step < rows:
            route.append((r - step, r))
    return route


def edge_route(rows):
    route = []
    for r in range(rows):
        target = {0: r - RING, RING - 1: r + RING}.get(r % RING, -1)
        if 0 <= target < rows:
            route.append((r, target))
    return route


def per_device(images, initial, offsets, stiffness, plan):
    rows = lax.axis_size("row")
    below = shifted(images, "row", -1)
    lower = lax.ppermute(images, ("sec", "row"), [(rows + r + 1, 2 * rows + r) for r in range(rows - 1)])
    remote_initial = lax.ppermute(initial, "row", edge_route(rows))
    near_offsets = shifted(offsets, "sec", 1)
    record, springs = prepare(plan, initial, stiffness)
    later_images, record, springs = lax.optimization_barrier((images, record, springs))
    near = shifted(later_images, "sec", 1)
    below, near_offsets, remote_initial, record, springs = lax.optimization_barrier(
        (below, near_offsets, remote_initial, record, springs)
    )
    near_below = lax.ppermute(below, "sec", [(0, 1), (2, 3)])
    count = SECS * RING
    tables = jnp.asarray(constant_tables())
    own_parts = own_spectra(images, below, tables)
    mine = pair_flow(own_parts, near, near_below, lower, record, remote_initial, near_offsets, tables, count)
    groups = [
        [s * rows + RING * g + j for s in range(SECS) for j in range(RING)] for g in range(rows // RING)
    ]
    ring = lax.all_to_all(mine.reshape(count, 1, PATCH), ("sec", "row"), 0, 0, axis_index_groups=groups)
    other = lax.ppermute(ring, "row", ring_route(rows, True))
    return tuple(
        relax(springs, ring.reshape(count, PATCH), other.reshape(count, PATCH), initial.shape)
    )


def solution(mesh):
    return jax.shard_map(
        per_device,
        mesh=mesh,
        in_specs=(
            P("sec", "row", None),
            P("sec", None, "row", None),
            P("sec", None, "row", None),
            P(),
            P(),
        ),
        out_specs=(P("sec", None, "row", None), P("sec", None, "row", None)),
        check_vma=False,
    )
```

```python
import math

import numpy as np
import jax
import jax.numpy as jnp
from jax import lax
from jax.experimental import pallas as pl
from jax.experimental.pallas import tpu as pltpu
from jax.sharding import PartitionSpec as P
import ml_dtypes

PATCH = 128
STRIDE = 64
HALF = 64
SWEEPS = 3
COLS = 16
PAIRS = 8
SECS = 4
RING = 4
SHIFTS = 16
REACH = 5
WIDTH = 1088

step_size = 0.2
floor_ratio = 0.2

VMEM_LIMIT = 24 * 1024 * 1024
PREPARE_FLOPS = 1_000_000_000

f32 = jnp.float32
bf16 = jnp.bfloat16


def dft_halves():
    freq = np.arange(PATCH)
    phase = freq[:, None] * freq[None, :] % PATCH
    folded = np.minimum(phase, PATCH - phase)
    angle = folded * (2.0 * math.pi / PATCH)
    sine = np.sin(angle) * np.where(2 * phase > PATCH, -1.0, 1.0)
    sine = np.where(2 * folded == PATCH, 0.0, sine)
    cosine = np.cos(angle)
    cosine = np.where(4 * folded == PATCH, np.cos(np.float32(math.pi / 2)), cosine)
    return cosine.astype(ml_dtypes.bfloat16), (-sine).astype(ml_dtypes.bfloat16)


def two_parts(table):
    high = table.astype(ml_dtypes.bfloat16)
    low = (table - high.astype(np.float64)).astype(ml_dtypes.bfloat16)
    return high, low


def constant_tables():
    cos_t, sin_t = dft_halves()
    cos_f = cos_t.astype(np.float32)
    sin_f = sin_t.astype(np.float32)
    rows = np.zeros((2 * PATCH, 2 * PATCH), np.float32)
    rows[0:PATCH, 0:HALF] = cos_f[:HALF].T
    rows[0:PATCH, PATCH : PATCH + HALF] = sin_f[:HALF].T
    rows[HALF : HALF + PATCH, HALF:PATCH] = cos_f[:HALF].T
    rows[HALF : HALF + PATCH, PATCH + HALF :] = sin_f[:HALF].T
    nyquist = np.zeros((2 * PATCH, PATCH), np.float32)
    nyquist[0:PATCH, 0::2] = cos_f[HALF][:, None]
    nyquist[HALF : HALF + PATCH, 1::2] = cos_f[HALF][:, None]
    columns = np.block([[cos_f, -sin_f], [sin_f, cos_f]])
    lags = np.arange(SHIFTS) - REACH
    used = (np.arange(SHIFTS) <= 2 * REACH).astype(np.float64)
    freq = np.arange(PATCH)
    turn = (freq[None, :] * lags[:, None] % PATCH) * (2.0 * math.pi / PATCH)
    cos_y = np.cos(turn) * used[:, None]
    sin_y = np.sin(turn) * used[:, None]
    high, low = two_parts(np.block([[cos_y, -sin_y], [sin_y, cos_y]]))
    lag_y = np.concatenate([high, low], axis=0)
    weight = np.where(freq[:HALF] == 0, 1.0, 2.0)
    across = np.zeros((3 * PATCH, PATCH))
    for p in range(2):
        cols = slice(p * HALF, p * HALF + SHIFTS)
        block = slice(p * HALF, (p + 1) * HALF)
        across[:PATCH][block, cols] = (cos_y[:, :HALF] * weight).T
        across[PATCH : 2 * PATCH][block, cols] = (-sin_y[:, :HALF] * weight).T
        for c in range(p, COLS, 2):
            across[2 * PATCH + c, cols] = np.where(lags % 2 == 0, 1.0, -1.0) * used
    high, low = two_parts(across)
    lag_x = np.concatenate([high, low], axis=1)
    lane = np.arange(PATCH)
    patch = (lane % COLS % 2)[None, :] == (lane // HALF)[:, None]
    gather = (patch & (lane < 2 * COLS)[None, :]).astype(np.float32)
    single = (patch & (lane < COLS)[None, :]).astype(np.float32)
    same = ((lane // HALF)[:, None] == (lane // HALF)[None, :]).astype(np.float32)
    blank = np.zeros((PATCH, PATCH), np.float32)
    spread = np.block([[same, gather], [single.T, blank]])
    packed = [rows, np.concatenate([nyquist[:PATCH], nyquist[PATCH:]], axis=1), columns, spread, lag_y, lag_x]
    return np.concatenate([np.asarray(t).astype(ml_dtypes.bfloat16) for t in packed], axis=0)


TABLE_ROWS = {"rows": (0, 256), "nyquist": (256, 128), "columns": (384, 256), "spread": (640, 256)}
TABLE_ROWS |= {"lag_y": (896, 64), "lag_x": (960, 384)}


def table(ref, name):
    start, length = TABLE_ROWS[name]
    return ref[pl.ds(start, length), :]


def three_parts(x):
    high = x.astype(bf16)
    rest = x - high.astype(f32)
    mid = rest.astype(bf16)
    low = (rest - mid.astype(f32)).astype(bf16)
    return jnp.concatenate([high, mid, low], axis=0)


def dot(a, b):
    return jnp.dot(a, b, preferred_element_type=f32)


def prepare_kernel(plan, initial, stiffness, record, springs):
    record[...] = jnp.zeros((1, PATCH), f32)
    for i in range(2):
        record[:, pl.ds((2 + i) * COLS, COLS)] = initial[0, i]
    level_id = lax.broadcasted_iota(jnp.int32, stiffness.shape, 1)
    for sweep in range(SWEEPS):
        picked = jnp.sum(jnp.where(level_id == plan[sweep], stiffness[...], 0.0), axis=1, keepdims=True)
        springs[pl.ds(2 * sweep, 2), :] = jnp.broadcast_to(picked, (2, PATCH))


def prepare(plan, initial, stiffness):
    in_vmem = pl.BlockSpec(memory_space=pltpu.VMEM)
    return pl.pallas_call(
        prepare_kernel,
        out_shape=[jax.ShapeDtypeStruct((1, PATCH), f32), jax.ShapeDtypeStruct((8, PATCH), f32)],
        in_specs=[pl.BlockSpec(memory_space=pltpu.SMEM), in_vmem, in_vmem],
        out_specs=[in_vmem] * 2,
        compiler_params=pltpu.CompilerParams(vmem_limit_bytes=VMEM_LIMIT),
        cost_estimate=pl.CostEstimate(flops=PREPARE_FLOPS, bytes_accessed=10_000, transcendentals=0),
    )(plan, initial, stiffness.T)


def section_spectra(upper, lower, tables):
    nyq_t = table(tables, "nyquist")
    nyq_t = jnp.concatenate([nyq_t[:, :PATCH], nyq_t[:, PATCH:]], axis=0)
    rows_t = jnp.concatenate([table(tables, "rows"), nyq_t], axis=1)
    columns = table(tables, "columns")
    lane = lax.broadcasted_iota(jnp.int32, (PATCH, PATCH), 1)
    nyquist = jnp.zeros((PATCH, PATCH), f32)
    stacked = []
    for m in range(PAIRS):
        span = 2 * PATCH if m < PAIRS - 1 else WIDTH - m * PATCH
        tile = jnp.concatenate([upper(m * PATCH, span), lower(m * PATCH, span)], axis=0)
        seg = dot(tile, rows_t[:span])
        nyquist = jnp.where(lane // 2 == m, seg[:, 2 * PATCH :], nyquist)
        seg = seg[:, : 2 * PATCH].astype(bf16)
        stacked.append(jnp.concatenate([seg[:, :PATCH], seg[:, PATCH:]], axis=0))
    spectra = []
    for m in range(0, PAIRS, 2):
        product = dot(columns, jnp.concatenate(stacked[m : m + 2], axis=1)).astype(bf16)
        spectra += [product[:, :PATCH], product[:, PATCH:]]
    spectra.append(dot(columns[:, :PATCH], nyquist.astype(bf16)).astype(bf16))
    return spectra


def energy(spectrum):
    wide = spectrum.astype(f32)
    return jnp.sum(wide * wide, axis=0, keepdims=True)


def block_tile(ref):
    return lambda start, span: ref[0, :, pl.ds(start, span)]


def own_kernel(own, below, tables, spec, energies):
    for m, spectrum in enumerate(section_spectra(block_tile(own), block_tile(below), tables)):
        spec[m] = spectrum
        energies[pl.ds(m, 1), :] = energy(spectrum)


def own_spectra(own, below, tables):
    in_vmem = pl.BlockSpec(memory_space=pltpu.VMEM)
    return pl.pallas_call(
        own_kernel,
        out_shape=[
            jax.ShapeDtypeStruct((PAIRS + 1, 2 * PATCH, PATCH), bf16),
            jax.ShapeDtypeStruct((2 * PAIRS, PATCH), f32),
        ],
        in_specs=[in_vmem] * 3,
        out_specs=[in_vmem] * 2,
        compiler_params=pltpu.CompilerParams(vmem_limit_bytes=VMEM_LIMIT),
        cost_estimate=pl.CostEstimate(flops=600_000_000, bytes_accessed=2_000_000, transcendentals=0),
    )(own, below, tables)


def flow_kernel(
    own_spec, own_energies, near, near_below, lower, record, shifts_in, tables, out, spec, lagged, shift_row
):
    spread = table(tables, "spread")
    energies = []

    def second(start, span):
        return near_below[0, :, pl.ds(start, span)] + lower[0, :, pl.ds(start, span)]

    for m, spectrum in enumerate(section_spectra(block_tile(near), second, tables)):
        spec[m] = spectrum
        energies.append(energy(spectrum))

    lane = lax.broadcasted_iota(jnp.int32, (PAIRS, PATCH), 1)
    pair = lax.broadcasted_iota(jnp.int32, (PAIRS, PATCH), 0)
    own_pair = (lane % COLS) // 2 == pair
    first_16 = own_pair & (lane < COLS)
    weight = jnp.where(lane % HALF == 0, 1.0, 2.0)

    def halves(x):
        return x[:, :PATCH], x[:, PATCH:]

    def totals(main, extra):
        left = jnp.concatenate([main * weight, jnp.where(first_16, extra, 0.0)], axis=1)
        found = dot(three_parts(left), spread)
        found = found[:PAIRS] + found[PAIRS : 2 * PAIRS] + found[2 * PAIRS :]
        by_pair, by_patch = halves(found)
        by_patch = jnp.sum(jnp.where(first_16, by_patch, 0.0), axis=0, keepdims=True) + extra
        scale = 1.0 / (PATCH * PATCH)
        return jnp.sqrt(by_pair * scale + 1e-06), jnp.sqrt(by_patch * scale + 1e-06)

    low_pair, low_patch = totals(jnp.concatenate(energies[:PAIRS], axis=0), energies[PAIRS])
    up_pair, up_patch = totals(own_energies[pl.ds(0, PAIRS), :], own_energies[pl.ds(PAIRS, 1), :])
    floor_pair = floor_ratio * low_pair * up_pair
    floor_patch = floor_ratio * low_patch * up_patch

    for m in range(PAIRS + 1):
        floor = floor_pair[m : m + 1] if m < PAIRS else floor_patch
        low_re = spec[m, pl.ds(0, PATCH)].astype(f32)
        low_im = spec[m, pl.ds(PATCH, PATCH)].astype(f32)
        up_re = own_spec[m, pl.ds(0, PATCH)].astype(f32)
        up_im = own_spec[m, pl.ds(PATCH, PATCH)].astype(f32)
        cross_re = low_re * up_re + low_im * up_im
        cross_im = low_re * up_im - low_im * up_re
        square = cross_re * cross_re + cross_im * cross_im
        modulus = square * lax.rsqrt(jnp.maximum(square, 1e-36))
        inverse = 1.0 / (modulus + floor)
        white = jnp.concatenate([cross_re * inverse, cross_im * inverse], axis=0)
        high = white.astype(bf16)
        low = (white - high.astype(f32)).astype(bf16)
        found = dot(table(tables, "lag_y"), jnp.concatenate([high, low], axis=1))
        part = found[: 2 * SHIFTS, :PATCH] + found[: 2 * SHIFTS, PATCH:] + found[2 * SHIFTS :, :PATCH]
        lagged[pl.ds(m * SHIFTS, SHIFTS), pl.ds(0, PATCH)] = part[:SHIFTS]
        lagged[pl.ds(m * SHIFTS, SHIFTS), pl.ds(PATCH, PATCH)] = part[SHIFTS:]

    extra = lagged[pl.ds(PAIRS * SHIFTS, SHIFTS), pl.ds(0, PATCH)]
    extra = jnp.where(first_16[:, None, :], extra[None], 0.0).reshape(PAIRS * SHIFTS, PATCH)
    left = jnp.concatenate([lagged[pl.ds(0, PAIRS * SHIFTS), :], extra], axis=1)
    high = left.astype(bf16)
    low = (left - high.astype(f32)).astype(bf16)
    rows_all = PAIRS * SHIFTS
    found = dot(jnp.concatenate([high, low], axis=0), table(tables, "lag_x"))
    surface = found[:rows_all, :PATCH] + found[:rows_all, PATCH:] + found[rows_all:, :PATCH]
    surface = surface.reshape(PAIRS, SHIFTS, PATCH)

    shift_row[...] = record[...]
    for i in range(2):
        shift_row[:, pl.ds(i * COLS, COLS)] = shifts_in[0, i].astype(f32)
    rec = shift_row[...]
    at_y = jnp.where(first_16, rec, 0.0)
    at_x = jnp.where(own_pair & (lane >= COLS) & (lane < 2 * COLS), rec, 0.0)
    gather = spread[:PATCH, PATCH:]
    shifts = lax.dot_general(
        jnp.concatenate([at_y, at_x], axis=0).astype(bf16),
        gather,
        (((1,), (1,)), ((), ())),
        preferred_element_type=f32,
    )
    lag_row = lax.broadcasted_iota(jnp.int32, (PAIRS, SHIFTS, PATCH), 1).astype(f32) - REACH
    lag_col = (lax.broadcasted_iota(jnp.int32, (PAIRS, SHIFTS, PATCH), 2) % HALF).astype(f32) - REACH
    dy = lag_row - shifts[:PAIRS][:, None, :]
    dx = lag_col - shifts[PAIRS:][:, None, :]
    mid_y, up_y, down_y = ((dy == k).astype(f32) for k in (0.0, 1.0, -1.0))
    mid_x, up_x, down_x = ((dx == k).astype(f32) for k in (0.0, 1.0, -1.0))
    at_mid_x = surface * mid_x
    at_mid_y = surface * mid_y
    picks = [
        jnp.sum(at_mid_x * (up_y - down_y), axis=1),
        jnp.sum(at_mid_x * (2.0 * mid_y - up_y - down_y), axis=1),
        jnp.sum(at_mid_y * (up_x - down_x), axis=1),
        jnp.sum(at_mid_y * (2.0 * mid_x - up_x - down_x), axis=1),
    ]
    found = dot(three_parts(jnp.concatenate(picks, axis=0)), gather)
    found = found[: 4 * PAIRS] + found[4 * PAIRS : 8 * PAIRS] + found[8 * PAIRS :]
    found = found.reshape(4, PAIRS, PATCH)
    found = jnp.sum(jnp.where(own_pair[None], found, 0.0), axis=1) * (1.0 / (PATCH * PATCH))
    lane_1 = lax.broadcasted_iota(jnp.int32, (1, PATCH), 1)
    slope = jnp.where(lane_1 < COLS, found[0:1], found[2:3])
    bend = jnp.where(lane_1 < COLS, found[1:2], found[3:4])
    flow = rec + 0.5 * slope / (1.0 + jnp.abs(bend))
    result = jnp.where(lane_1 < 2 * COLS, flow, rec)
    out[...] = jnp.broadcast_to(result, out.shape)


def pair_flow(own_parts, near, near_below, lower, record, offsets, tables, copies):
    operands = (*own_parts, near, near_below, lower, record, offsets, tables)
    return pl.pallas_call(
        flow_kernel,
        out_shape=jax.ShapeDtypeStruct((copies, PATCH), f32),
        in_specs=[pl.BlockSpec(memory_space=pltpu.VMEM)] * len(operands),
        out_specs=pl.BlockSpec(memory_space=pltpu.VMEM),
        scratch_shapes=[
            pltpu.VMEM((PAIRS + 1, 2 * PATCH, PATCH), bf16),
            pltpu.VMEM(((PAIRS + 1) * SHIFTS, 2 * PATCH), f32),
            pltpu.VMEM((1, PATCH), f32),
        ],
        compiler_params=pltpu.CompilerParams(vmem_limit_bytes=VMEM_LIMIT),
    )(*operands)


def relax_kernel(springs, ring, first_ring, second_ring, flow_out, moving_out):
    sec = lax.axis_index("sec")
    row = lax.axis_index("row")
    last_row = lax.axis_size("row") - 1
    place = lax.rem(row, RING)
    base = row - place
    count = SECS * RING
    node = lax.broadcasted_iota(jnp.int32, (count, PATCH), 0)
    lane = lax.broadcasted_iota(jnp.int32, (count, PATCH), 1)
    in_ring = node % RING
    section = node // RING
    other_first = jnp.broadcast_to(place, (count, PATCH)) < RING // 2
    valid = (section < SECS - 1) & (lane < 2 * COLS)
    valid_up = valid.astype(f32)
    has_left = (lane % COLS > 0).astype(f32)
    has_right = (lane % COLS < COLS - 1).astype(f32)
    row_here = base + in_ring
    row_other = row_here + jnp.where(other_first, -RING, RING)
    at_rows = (row_here, row_other)
    has_up = [(r > 0).astype(f32) for r in at_rows]
    has_down = [(r < last_row).astype(f32) for r in at_rows]
    first = in_ring == 0
    final = in_ring == RING - 1
    here = ring[...]
    odd = jnp.broadcast_to(lax.rem(row // RING, 2), (count, PATCH)) == 1
    beyond = jnp.where(other_first == odd, second_ring[...], first_ring[...])
    far_side = jnp.where(other_first == odd, first_ring[...], second_ring[...])
    moving = [pltpu.roll(b, PATCH - 2 * COLS, 1) for b in (here, beyond)]
    third = pltpu.roll(far_side, PATCH - 2 * COLS, 1)

    def moved(x, by):
        by = by % count
        return jnp.concatenate([x[by:], x[:by]], axis=0)

    flows = [jnp.where(valid, moved(b, RING), 0.0) for b in (here, beyond)]

    for sweep in range(SWEEPS):
        spring = springs[pl.ds(2 * sweep, 1), :]
        tether = springs[pl.ds(2 * sweep + 1, 1), :]
        near_x, far_x = moving
        edge_above = jnp.where(other_first, moved(far_x, RING - 1), moved(third, RING - 1))
        edge_below = jnp.where(other_first, moved(third, 1 - RING), moved(far_x, 1 - RING))
        above = (jnp.where(first, edge_above, moved(near_x, -1)), jnp.where(first, moved(near_x, RING - 1), moved(far_x, -1)))
        below = (jnp.where(final, edge_below, moved(near_x, 1)), jnp.where(final, moved(near_x, 1 - RING), moved(far_x, 1)))
        fresh = []
        for k, x in enumerate(moving):
            col_left = pltpu.roll(x, 1, 1)
            col_right = pltpu.roll(x, PATCH - 1, 1)
            laplace = (
                (above[k] - x) * has_up[k]
                + (below[k] - x) * has_down[k]
                + (col_left - x) * has_left
                + (col_right - x) * has_right
            )
            residual = (moved(x, RING) - x - flows[k]) * valid_up
            below_res = jnp.where(section == 0, 0.0, moved(residual, -RING))
            fresh.append(x + step_size * (spring * laplace + tether * (residual - below_res)))
        moving = fresh

    mine = (section == sec) & (in_ring == place)
    for x, ref in ((flows[0], flow_out), (moving[0], moving_out)):
        line = jnp.sum(jnp.where(mine, x, 0.0), axis=0, keepdims=True)
        ref[0, 0] = line[:, :COLS]
        ref[0, 1] = line[:, COLS : 2 * COLS]


def relax(springs, ring, first_ring, second_ring, shape):
    in_vmem = pl.BlockSpec(memory_space=pltpu.VMEM)
    return pl.pallas_call(
        relax_kernel,
        out_shape=[jax.ShapeDtypeStruct(shape, f32)] * 2,
        in_specs=[in_vmem] * 4,
        out_specs=[in_vmem] * 2,
        compiler_params=pltpu.CompilerParams(vmem_limit_bytes=VMEM_LIMIT),
    )(springs, ring, first_ring, second_ring)


def shifted(block, axis, distance):
    devices = range(lax.axis_size(axis))
    route = [(i - distance, i) for i in devices if i - distance in devices]
    return lax.ppermute(block, axis, route)


def ring_routes(rows):
    routes = ([], [])
    for r in range(rows):
        ring = r // RING
        if r % RING < RING - 1 and r >= RING:
            routes[ring % 2].append((r - RING, r))
        if r % RING > 0 and r + RING < rows:
            routes[1 - ring % 2].append((r + RING, r))
    return routes


def per_device(images, initial, offsets, stiffness, plan):
    rows = lax.axis_size("row")
    at = lambda s, r: s * rows + r
    below = lax.ppermute(
        images, ("sec", "row"), [(at(s, r + 1), at(s, r)) for s in range(1, SECS) for r in range(rows - 1)]
    )
    lower = lax.ppermute(
        images, ("sec", "row"), [(at(s, r + 1), at(s + 1, r)) for s in range(2) for r in range(rows - 1)]
    )
    near_offsets = shifted(offsets, "sec", 1)
    record, springs = prepare(plan, initial, stiffness)
    later_images, record, springs = lax.optimization_barrier((images, record, springs))
    near = shifted(later_images, "sec", 1)
    below, near_offsets, record, springs = lax.optimization_barrier((below, near_offsets, record, springs))
    near_below = lax.ppermute(below, "sec", [(2, 3)])
    count = SECS * RING
    tables = jnp.asarray(constant_tables())
    own_parts = own_spectra(images, below, tables)
    mine = pair_flow(own_parts, near, near_below, lower, record, near_offsets, tables, count)
    groups = [
        [s * rows + RING * g + j for s in range(SECS) for j in range(RING)] for g in range(rows // RING)
    ]
    ring = lax.all_to_all(mine.reshape(count, 1, PATCH), ("sec", "row"), 0, 0, axis_index_groups=groups)
    blocks = [ring] + [lax.ppermute(ring, "row", route) for route in ring_routes(rows)]
    return tuple(relax(springs, *(block.reshape(count, PATCH) for block in blocks), initial.shape))


def solution(mesh):
    return jax.shard_map(
        per_device,
        mesh=mesh,
        in_specs=(
            P("sec", "row", None),
            P("sec", None, "row", None),
            P("sec", None, "row", None),
            P(),
            P(),
        ),
        out_specs=(P("sec", None, "row", None), P("sec", None, "row", None)),
        check_vma=False,
    )
```

```python
import math

import numpy as np
import jax
import jax.numpy as jnp
from jax import lax
from jax.experimental import pallas as pl
from jax.experimental.pallas import tpu as pltpu
from jax.sharding import PartitionSpec as P
import ml_dtypes

PATCH = 128
STRIDE = 64
HALF = 64
SWEEPS = 3
COLS = 16
PAIRS = 8
SECS = 4
RING = 4
SHIFTS = 16
REACH = 5
WIDTH = 1088

step_size = 0.2
floor_ratio = 0.2

VMEM_LIMIT = 24 * 1024 * 1024
PREPARE_FLOPS = 1_000_000_000

f32 = jnp.float32
bf16 = jnp.bfloat16


def dft_halves():
    freq = np.arange(PATCH)
    phase = freq[:, None] * freq[None, :] % PATCH
    folded = np.minimum(phase, PATCH - phase)
    angle = folded * (2.0 * math.pi / PATCH)
    sine = np.sin(angle) * np.where(2 * phase > PATCH, -1.0, 1.0)
    sine = np.where(2 * folded == PATCH, 0.0, sine)
    cosine = np.cos(angle)
    cosine = np.where(4 * folded == PATCH, np.cos(np.float32(math.pi / 2)), cosine)
    return cosine.astype(ml_dtypes.bfloat16), (-sine).astype(ml_dtypes.bfloat16)


def two_parts(table):
    high = table.astype(ml_dtypes.bfloat16)
    low = (table - high.astype(np.float64)).astype(ml_dtypes.bfloat16)
    return high, low


def constant_tables():
    cos_t, sin_t = dft_halves()
    cos_f = cos_t.astype(np.float32)
    sin_f = sin_t.astype(np.float32)
    rows = np.zeros((2 * PATCH, 2 * PATCH), np.float32)
    rows[0:PATCH, 0:HALF] = cos_f[:HALF].T
    rows[0:PATCH, PATCH : PATCH + HALF] = sin_f[:HALF].T
    rows[HALF : HALF + PATCH, HALF:PATCH] = cos_f[:HALF].T
    rows[HALF : HALF + PATCH, PATCH + HALF :] = sin_f[:HALF].T
    nyquist = np.zeros((2 * PATCH, PATCH), np.float32)
    nyquist[0:PATCH, 0::2] = cos_f[HALF][:, None]
    nyquist[HALF : HALF + PATCH, 1::2] = cos_f[HALF][:, None]
    columns = np.block([[cos_f, -sin_f], [sin_f, cos_f]])
    lags = np.arange(SHIFTS) - REACH
    used = (np.arange(SHIFTS) <= 2 * REACH).astype(np.float64)
    freq = np.arange(PATCH)
    turn = (freq[None, :] * lags[:, None] % PATCH) * (2.0 * math.pi / PATCH)
    cos_y = np.cos(turn) * used[:, None]
    sin_y = np.sin(turn) * used[:, None]
    high, low = two_parts(np.block([[cos_y, -sin_y], [sin_y, cos_y]]))
    lag_y = np.concatenate([high, low], axis=0)
    weight = np.where(freq[:HALF] == 0, 1.0, 2.0)
    across = np.zeros((3 * PATCH, PATCH))
    for p in range(2):
        cols = slice(p * HALF, p * HALF + SHIFTS)
        block = slice(p * HALF, (p + 1) * HALF)
        across[:PATCH][block, cols] = (cos_y[:, :HALF] * weight).T
        across[PATCH : 2 * PATCH][block, cols] = (-sin_y[:, :HALF] * weight).T
        for c in range(p, COLS, 2):
            across[2 * PATCH + c, cols] = np.where(lags % 2 == 0, 1.0, -1.0) * used
    high, low = two_parts(across)
    lag_x = np.concatenate([high, low], axis=1)
    lane = np.arange(PATCH)
    patch = (lane % COLS % 2)[None, :] == (lane // HALF)[:, None]
    gather = (patch & (lane < 2 * COLS)[None, :]).astype(np.float32)
    single = (patch & (lane < COLS)[None, :]).astype(np.float32)
    same = ((lane // HALF)[:, None] == (lane // HALF)[None, :]).astype(np.float32)
    blank = np.zeros((PATCH, PATCH), np.float32)
    spread = np.block([[same, gather], [single.T, blank]])
    packed = [rows, np.concatenate([nyquist[:PATCH], nyquist[PATCH:]], axis=1), columns, spread, lag_y, lag_x]
    return np.concatenate([np.asarray(t).astype(ml_dtypes.bfloat16) for t in packed], axis=0)


TABLE_ROWS = {"rows": (0, 256), "nyquist": (256, 128), "columns": (384, 256), "spread": (640, 256)}
TABLE_ROWS |= {"lag_y": (896, 64), "lag_x": (960, 384)}


def table(ref, name):
    start, length = TABLE_ROWS[name]
    return ref[pl.ds(start, length), :]


def three_parts(x):
    high = x.astype(bf16)
    rest = x - high.astype(f32)
    mid = rest.astype(bf16)
    low = (rest - mid.astype(f32)).astype(bf16)
    return jnp.concatenate([high, mid, low], axis=0)


def dot(a, b):
    return jnp.dot(a, b, preferred_element_type=f32)


def prepare_kernel(plan, initial, stiffness, record, springs):
    record[...] = jnp.zeros((1, PATCH), f32)
    for i in range(2):
        record[:, pl.ds((2 + i) * COLS, COLS)] = initial[0, i]
    level_id = lax.broadcasted_iota(jnp.int32, stiffness.shape, 1)
    for sweep in range(SWEEPS):
        picked = jnp.sum(jnp.where(level_id == plan[sweep], stiffness[...], 0.0), axis=1, keepdims=True)
        springs[pl.ds(2 * sweep, 2), :] = jnp.broadcast_to(picked, (2, PATCH))


def prepare(plan, initial, stiffness):
    in_vmem = pl.BlockSpec(memory_space=pltpu.VMEM)
    return pl.pallas_call(
        prepare_kernel,
        out_shape=[jax.ShapeDtypeStruct((1, PATCH), f32), jax.ShapeDtypeStruct((8, PATCH), f32)],
        in_specs=[pl.BlockSpec(memory_space=pltpu.SMEM), in_vmem, in_vmem],
        out_specs=[in_vmem] * 2,
        compiler_params=pltpu.CompilerParams(vmem_limit_bytes=VMEM_LIMIT),
        cost_estimate=pl.CostEstimate(flops=PREPARE_FLOPS, bytes_accessed=10_000, transcendentals=0),
    )(plan, initial, stiffness.T)


def section_spectra(upper, lower, tables):
    nyq_t = table(tables, "nyquist")
    nyq_t = jnp.concatenate([nyq_t[:, :PATCH], nyq_t[:, PATCH:]], axis=0)
    rows_t = jnp.concatenate([table(tables, "rows"), nyq_t], axis=1)
    columns = table(tables, "columns")
    lane = lax.broadcasted_iota(jnp.int32, (PATCH, PATCH), 1)
    nyquist = jnp.zeros((PATCH, PATCH), f32)
    stacked = []
    for m in range(PAIRS):
        span = 2 * PATCH if m < PAIRS - 1 else WIDTH - m * PATCH
        tile = jnp.concatenate([upper(m * PATCH, span), lower(m * PATCH, span)], axis=0)
        seg = dot(tile, rows_t[:span])
        nyquist = jnp.where(lane // 2 == m, seg[:, 2 * PATCH :], nyquist)
        seg = seg[:, : 2 * PATCH].astype(bf16)
        stacked.append(jnp.concatenate([seg[:, :PATCH], seg[:, PATCH:]], axis=0))
    spectra = []
    for m in range(0, PAIRS, 2):
        product = dot(columns, jnp.concatenate(stacked[m : m + 2], axis=1)).astype(bf16)
        spectra += [product[:, :PATCH], product[:, PATCH:]]
    spectra.append(dot(columns[:, :PATCH], nyquist.astype(bf16)).astype(bf16))
    return spectra


def energy(spectrum):
    wide = spectrum.astype(f32)
    return jnp.sum(wide * wide, axis=0, keepdims=True)


def block_tile(ref):
    return lambda start, span: ref[0, :, pl.ds(start, span)]


def own_kernel(own, below, tables, spec, energies):
    for m, spectrum in enumerate(section_spectra(block_tile(own), block_tile(below), tables)):
        spec[m] = spectrum
        energies[pl.ds(m, 1), :] = energy(spectrum)


def own_spectra(own, below, tables):
    in_vmem = pl.BlockSpec(memory_space=pltpu.VMEM)
    return pl.pallas_call(
        own_kernel,
        out_shape=[
            jax.ShapeDtypeStruct((PAIRS + 1, 2 * PATCH, PATCH), bf16),
            jax.ShapeDtypeStruct((2 * PAIRS, PATCH), f32),
        ],
        in_specs=[in_vmem] * 3,
        out_specs=[in_vmem] * 2,
        compiler_params=pltpu.CompilerParams(vmem_limit_bytes=VMEM_LIMIT),
        cost_estimate=pl.CostEstimate(flops=600_000_000, bytes_accessed=2_000_000, transcendentals=0),
    )(own, below, tables)


def flow_kernel(
    own_spec, own_energies, near, near_below, lower, record, shifts_in, tables, out, spec, lagged, shift_row
):
    spread = table(tables, "spread")
    energies = []

    def second(start, span):
        return near_below[0, :, pl.ds(start, span)] + lower[0, :, pl.ds(start, span)]

    for m, spectrum in enumerate(section_spectra(block_tile(near), second, tables)):
        spec[m] = spectrum
        energies.append(energy(spectrum))

    lane = lax.broadcasted_iota(jnp.int32, (PAIRS, PATCH), 1)
    pair = lax.broadcasted_iota(jnp.int32, (PAIRS, PATCH), 0)
    own_pair = (lane % COLS) // 2 == pair
    first_16 = own_pair & (lane < COLS)
    weight = jnp.where(lane % HALF == 0, 1.0, 2.0)

    def halves(x):
        return x[:, :PATCH], x[:, PATCH:]

    def totals(main, extra):
        left = jnp.concatenate([main * weight, jnp.where(first_16, extra, 0.0)], axis=1)
        found = dot(three_parts(left), spread)
        found = found[:PAIRS] + found[PAIRS : 2 * PAIRS] + found[2 * PAIRS :]
        by_pair, by_patch = halves(found)
        by_patch = jnp.sum(jnp.where(first_16, by_patch, 0.0), axis=0, keepdims=True) + extra
        scale = 1.0 / (PATCH * PATCH)
        return jnp.sqrt(by_pair * scale + 1e-06), jnp.sqrt(by_patch * scale + 1e-06)

    low_pair, low_patch = totals(jnp.concatenate(energies[:PAIRS], axis=0), energies[PAIRS])
    up_pair, up_patch = totals(own_energies[pl.ds(0, PAIRS), :], own_energies[pl.ds(PAIRS, 1), :])
    floor_pair = floor_ratio * low_pair * up_pair
    floor_patch = floor_ratio * low_patch * up_patch

    for m in range(PAIRS + 1):
        floor = floor_pair[m : m + 1] if m < PAIRS else floor_patch
        low_re = spec[m, pl.ds(0, PATCH)].astype(f32)
        low_im = spec[m, pl.ds(PATCH, PATCH)].astype(f32)
        up_re = own_spec[m, pl.ds(0, PATCH)].astype(f32)
        up_im = own_spec[m, pl.ds(PATCH, PATCH)].astype(f32)
        cross_re = low_re * up_re + low_im * up_im
        cross_im = low_re * up_im - low_im * up_re
        square = cross_re * cross_re + cross_im * cross_im
        modulus = square * lax.rsqrt(jnp.maximum(square, 1e-36))
        inverse = 1.0 / (modulus + floor)
        white = jnp.concatenate([cross_re * inverse, cross_im * inverse], axis=0)
        high = white.astype(bf16)
        low = (white - high.astype(f32)).astype(bf16)
        found = dot(table(tables, "lag_y"), jnp.concatenate([high, low], axis=1))
        part = found[: 2 * SHIFTS, :PATCH] + found[: 2 * SHIFTS, PATCH:] + found[2 * SHIFTS :, :PATCH]
        lagged[pl.ds(m * SHIFTS, SHIFTS), pl.ds(0, PATCH)] = part[:SHIFTS]
        lagged[pl.ds(m * SHIFTS, SHIFTS), pl.ds(PATCH, PATCH)] = part[SHIFTS:]

    extra = lagged[pl.ds(PAIRS * SHIFTS, SHIFTS), pl.ds(0, PATCH)]
    extra = jnp.where(first_16[:, None, :], extra[None], 0.0).reshape(PAIRS * SHIFTS, PATCH)
    left = jnp.concatenate([lagged[pl.ds(0, PAIRS * SHIFTS), :], extra], axis=1)
    high = left.astype(bf16)
    low = (left - high.astype(f32)).astype(bf16)
    rows_all = PAIRS * SHIFTS
    found = dot(jnp.concatenate([high, low], axis=0), table(tables, "lag_x"))
    surface = found[:rows_all, :PATCH] + found[:rows_all, PATCH:] + found[rows_all:, :PATCH]
    surface = surface.reshape(PAIRS, SHIFTS, PATCH)

    shift_row[...] = record[...]
    for i in range(2):
        shift_row[:, pl.ds(i * COLS, COLS)] = shifts_in[0, i].astype(f32)
    rec = shift_row[...]
    at_y = jnp.where(first_16, rec, 0.0)
    at_x = jnp.where(own_pair & (lane >= COLS) & (lane < 2 * COLS), rec, 0.0)
    gather = spread[:PATCH, PATCH:]
    shifts = lax.dot_general(
        jnp.concatenate([at_y, at_x], axis=0).astype(bf16),
        gather,
        (((1,), (1,)), ((), ())),
        preferred_element_type=f32,
    )
    lag_row = lax.broadcasted_iota(jnp.int32, (PAIRS, SHIFTS, PATCH), 1).astype(f32) - REACH
    lag_col = (lax.broadcasted_iota(jnp.int32, (PAIRS, SHIFTS, PATCH), 2) % HALF).astype(f32) - REACH
    dy = lag_row - shifts[:PAIRS][:, None, :]
    dx = lag_col - shifts[PAIRS:][:, None, :]
    mid_y, up_y, down_y = ((dy == k).astype(f32) for k in (0.0, 1.0, -1.0))
    mid_x, up_x, down_x = ((dx == k).astype(f32) for k in (0.0, 1.0, -1.0))
    at_mid_x = surface * mid_x
    at_mid_y = surface * mid_y
    picks = [
        jnp.sum(at_mid_x * (up_y - down_y), axis=1),
        jnp.sum(at_mid_x * (2.0 * mid_y - up_y - down_y), axis=1),
        jnp.sum(at_mid_y * (up_x - down_x), axis=1),
        jnp.sum(at_mid_y * (2.0 * mid_x - up_x - down_x), axis=1),
    ]
    found = dot(three_parts(jnp.concatenate(picks, axis=0)), gather)
    found = found[: 4 * PAIRS] + found[4 * PAIRS : 8 * PAIRS] + found[8 * PAIRS :]
    found = found.reshape(4, PAIRS, PATCH)
    found = jnp.sum(jnp.where(own_pair[None], found, 0.0), axis=1) * (1.0 / (PATCH * PATCH))
    lane_1 = lax.broadcasted_iota(jnp.int32, (1, PATCH), 1)
    slope = jnp.where(lane_1 < COLS, found[0:1], found[2:3])
    bend = jnp.where(lane_1 < COLS, found[1:2], found[3:4])
    flow = rec + 0.5 * slope / (1.0 + jnp.abs(bend))
    result = jnp.where(lane_1 < 2 * COLS, flow, rec)
    out[...] = jnp.broadcast_to(result, out.shape)


def pair_flow(own_parts, near, near_below, lower, record, offsets, tables, copies):
    operands = (*own_parts, near, near_below, lower, record, offsets, tables)
    return pl.pallas_call(
        flow_kernel,
        out_shape=jax.ShapeDtypeStruct((copies, PATCH), f32),
        in_specs=[pl.BlockSpec(memory_space=pltpu.VMEM)] * len(operands),
        out_specs=pl.BlockSpec(memory_space=pltpu.VMEM),
        scratch_shapes=[
            pltpu.VMEM((PAIRS + 1, 2 * PATCH, PATCH), bf16),
            pltpu.VMEM(((PAIRS + 1) * SHIFTS, 2 * PATCH), f32),
            pltpu.VMEM((1, PATCH), f32),
        ],
        compiler_params=pltpu.CompilerParams(vmem_limit_bytes=VMEM_LIMIT),
    )(*operands)


def relax_kernel(springs, ring, first_ring, second_ring, flow_out, moving_out):
    sec = lax.axis_index("sec")
    row = lax.axis_index("row")
    last_row = lax.axis_size("row") - 1
    place = lax.rem(row, RING)
    base = row - place
    count = SECS * RING
    node = lax.broadcasted_iota(jnp.int32, (count, PATCH), 0)
    lane = lax.broadcasted_iota(jnp.int32, (count, PATCH), 1)
    in_ring = node % RING
    section = node // RING
    other_first = jnp.broadcast_to(place, (count, PATCH)) < RING // 2
    valid = (section < SECS - 1) & (lane < 2 * COLS)
    valid_up = valid.astype(f32)
    has_left = (lane % COLS > 0).astype(f32)
    has_right = (lane % COLS < COLS - 1).astype(f32)
    row_here = base + in_ring
    row_other = row_here + jnp.where(other_first, -RING, RING)
    at_rows = (row_here, row_other)
    has_up = [(r > 0).astype(f32) for r in at_rows]
    has_down = [(r < last_row).astype(f32) for r in at_rows]
    first = in_ring == 0
    final = in_ring == RING - 1
    here = ring[...]
    odd = jnp.broadcast_to(lax.rem(row // RING, 2), (count, PATCH)) == 1
    inner = (jnp.broadcast_to(place, (count, PATCH)) > 0) & (jnp.broadcast_to(place, (count, PATCH)) < RING - 1)
    in_second = inner & (other_first == odd)
    beyond = jnp.where(in_second, second_ring[...], first_ring[...])
    far_side = jnp.where(in_second, first_ring[...], second_ring[...])
    moving = [pltpu.roll(b, PATCH - 2 * COLS, 1) for b in (here, beyond)]
    third = pltpu.roll(far_side, PATCH - 2 * COLS, 1)

    def moved(x, by):
        by = by % count
        return jnp.concatenate([x[by:], x[:by]], axis=0)

    flows = [jnp.where(valid, moved(b, RING), 0.0) for b in (here, beyond)]

    for sweep in range(SWEEPS):
        spring = springs[pl.ds(2 * sweep, 1), :]
        tether = springs[pl.ds(2 * sweep + 1, 1), :]
        near_x, far_x = moving
        edge_above = jnp.where(other_first, moved(far_x, RING - 1), moved(third, RING - 1))
        edge_below = jnp.where(other_first, moved(third, 1 - RING), moved(far_x, 1 - RING))
        above = (jnp.where(first, edge_above, moved(near_x, -1)), jnp.where(first, moved(near_x, RING - 1), moved(far_x, -1)))
        below = (jnp.where(final, edge_below, moved(near_x, 1)), jnp.where(final, moved(near_x, 1 - RING), moved(far_x, 1)))
        fresh = []
        for k, x in enumerate(moving):
            col_left = pltpu.roll(x, 1, 1)
            col_right = pltpu.roll(x, PATCH - 1, 1)
            laplace = (
                (above[k] - x) * has_up[k]
                + (below[k] - x) * has_down[k]
                + (col_left - x) * has_left
                + (col_right - x) * has_right
            )
            residual = (moved(x, RING) - x - flows[k]) * valid_up
            below_res = jnp.where(section == 0, 0.0, moved(residual, -RING))
            fresh.append(x + step_size * (spring * laplace + tether * (residual - below_res)))
        moving = fresh

    mine = (section == sec) & (in_ring == place)
    for x, ref in ((flows[0], flow_out), (moving[0], moving_out)):
        line = jnp.sum(jnp.where(mine, x, 0.0), axis=0, keepdims=True)
        ref[0, 0] = line[:, :COLS]
        ref[0, 1] = line[:, COLS : 2 * COLS]


def relax(springs, ring, first_ring, second_ring, shape):
    in_vmem = pl.BlockSpec(memory_space=pltpu.VMEM)
    return pl.pallas_call(
        relax_kernel,
        out_shape=[jax.ShapeDtypeStruct(shape, f32)] * 2,
        in_specs=[in_vmem] * 4,
        out_specs=[in_vmem] * 2,
        compiler_params=pltpu.CompilerParams(vmem_limit_bytes=VMEM_LIMIT),
    )(springs, ring, first_ring, second_ring)


def shifted(block, axis, distance):
    devices = range(lax.axis_size(axis))
    route = [(i - distance, i) for i in devices if i - distance in devices]
    return lax.ppermute(block, axis, route)


def ring_routes(rows):
    routes = ([], [])
    for r in range(rows):
        odd, place = r // RING % 2, r % RING
        inner = 0 < place < RING - 1
        if place < RING - 1 and r >= RING:
            routes[odd if inner else 0].append((r - RING, r))
        if place > 0 and r + RING < rows:
            routes[1 - odd if inner else 0].append((r + RING, r))
    return routes


def per_device(images, initial, offsets, stiffness, plan):
    rows = lax.axis_size("row")
    at = lambda s, r: s * rows + r
    below = lax.ppermute(
        images, ("sec", "row"), [(at(s, r + 1), at(s, r)) for s in range(1, SECS) for r in range(rows - 1)]
    )
    lower = lax.ppermute(
        images, ("sec", "row"), [(at(s, r + 1), at(s + 1, r)) for s in range(2) for r in range(rows - 1)]
    )
    near_offsets = shifted(offsets, "sec", 1)
    record, springs = prepare(plan, initial, stiffness)
    later_images, record, springs = lax.optimization_barrier((images, record, springs))
    near = shifted(later_images, "sec", 1)
    below, near_offsets, record, springs = lax.optimization_barrier((below, near_offsets, record, springs))
    near_below = lax.ppermute(below, "sec", [(2, 3)])
    count = SECS * RING
    tables = jnp.asarray(constant_tables())
    own_parts = own_spectra(images, below, tables)
    mine = pair_flow(own_parts, near, near_below, lower, record, near_offsets, tables, count)
    groups = [
        [s * rows + RING * g + j for s in range(SECS) for j in range(RING)] for g in range(rows // RING)
    ]
    ring = lax.all_to_all(mine.reshape(count, 1, PATCH), ("sec", "row"), 0, 0, axis_index_groups=groups)
    blocks = [ring] + [lax.ppermute(ring, "row", route) for route in ring_routes(rows)]
    return tuple(relax(springs, *(block.reshape(count, PATCH) for block in blocks), initial.shape))


def solution(mesh):
    return jax.shard_map(
        per_device,
        mesh=mesh,
        in_specs=(
            P("sec", "row", None),
            P("sec", None, "row", None),
            P("sec", None, "row", None),
            P(),
            P(),
        ),
        out_specs=(P("sec", None, "row", None), P("sec", None, "row", None)),
        check_vma=False,
    )
```

```python
import math

import numpy as np
import jax
import jax.numpy as jnp
from jax import lax
from jax.experimental import pallas as pl
from jax.experimental.pallas import tpu as pltpu
from jax.sharding import PartitionSpec as P
import ml_dtypes

PATCH = 128
STRIDE = 64
HALF = 64
SWEEPS = 3
COLS = 16
PAIRS = 8
SECS = 4
RING = 4
SHIFTS = 16
REACH = 5
WIDTH = 1088

step_size = 0.2
floor_ratio = 0.2

VMEM_LIMIT = 24 * 1024 * 1024
PREPARE_FLOPS = 1_000_000_000

f32 = jnp.float32
bf16 = jnp.bfloat16


def dft_halves():
    freq = np.arange(PATCH)
    phase = freq[:, None] * freq[None, :] % PATCH
    folded = np.minimum(phase, PATCH - phase)
    angle = folded * (2.0 * math.pi / PATCH)
    sine = np.sin(angle) * np.where(2 * phase > PATCH, -1.0, 1.0)
    sine = np.where(2 * folded == PATCH, 0.0, sine)
    cosine = np.cos(angle)
    cosine = np.where(4 * folded == PATCH, np.cos(np.float32(math.pi / 2)), cosine)
    return cosine.astype(ml_dtypes.bfloat16), (-sine).astype(ml_dtypes.bfloat16)


def two_parts(table):
    high = table.astype(ml_dtypes.bfloat16)
    low = (table - high.astype(np.float64)).astype(ml_dtypes.bfloat16)
    return high, low


def constant_tables():
    cos_t, sin_t = dft_halves()
    cos_f = cos_t.astype(np.float32)
    sin_f = sin_t.astype(np.float32)
    rows = np.zeros((2 * PATCH, 2 * PATCH), np.float32)
    rows[0:PATCH, 0:HALF] = cos_f[:HALF].T
    rows[0:PATCH, PATCH : PATCH + HALF] = sin_f[:HALF].T
    rows[HALF : HALF + PATCH, HALF:PATCH] = cos_f[:HALF].T
    rows[HALF : HALF + PATCH, PATCH + HALF :] = sin_f[:HALF].T
    nyquist = np.zeros((2 * PATCH, PATCH), np.float32)
    nyquist[0:PATCH, 0::2] = cos_f[HALF][:, None]
    nyquist[HALF : HALF + PATCH, 1::2] = cos_f[HALF][:, None]
    columns = np.block([[cos_f, -sin_f], [sin_f, cos_f]])
    lags = np.arange(SHIFTS) - REACH
    used = (np.arange(SHIFTS) <= 2 * REACH).astype(np.float64)
    freq = np.arange(PATCH)
    turn = (freq[None, :] * lags[:, None] % PATCH) * (2.0 * math.pi / PATCH)
    cos_y = np.cos(turn) * used[:, None]
    sin_y = np.sin(turn) * used[:, None]
    high, low = two_parts(np.block([[cos_y, -sin_y], [sin_y, cos_y]]))
    lag_y = np.concatenate([high, low], axis=0)
    weight = np.where(freq[:HALF] == 0, 1.0, 2.0)
    across = np.zeros((3 * PATCH, PATCH))
    for p in range(2):
        cols = slice(p * HALF, p * HALF + SHIFTS)
        block = slice(p * HALF, (p + 1) * HALF)
        across[:PATCH][block, cols] = (cos_y[:, :HALF] * weight).T
        across[PATCH : 2 * PATCH][block, cols] = (-sin_y[:, :HALF] * weight).T
        for c in range(p, COLS, 2):
            across[2 * PATCH + c, cols] = np.where(lags % 2 == 0, 1.0, -1.0) * used
    high, low = two_parts(across)
    lag_x = np.concatenate([high, low], axis=1)
    lane = np.arange(PATCH)
    patch = (lane % COLS % 2)[None, :] == (lane // HALF)[:, None]
    gather = (patch & (lane < 2 * COLS)[None, :]).astype(np.float32)
    single = (patch & (lane < COLS)[None, :]).astype(np.float32)
    same = ((lane // HALF)[:, None] == (lane // HALF)[None, :]).astype(np.float32)
    blank = np.zeros((PATCH, PATCH), np.float32)
    spread = np.block([[same, gather], [single.T, blank]])
    packed = [rows, np.concatenate([nyquist[:PATCH], nyquist[PATCH:]], axis=1), columns, spread, lag_y, lag_x]
    return np.concatenate([np.asarray(t).astype(ml_dtypes.bfloat16) for t in packed], axis=0)


TABLE_ROWS = {"rows": (0, 256), "nyquist": (256, 128), "columns": (384, 256), "spread": (640, 256)}
TABLE_ROWS |= {"lag_y": (896, 64), "lag_x": (960, 384)}


def table(ref, name):
    start, length = TABLE_ROWS[name]
    return ref[pl.ds(start, length), :]


def three_parts(x):
    high = x.astype(bf16)
    rest = x - high.astype(f32)
    mid = rest.astype(bf16)
    low = (rest - mid.astype(f32)).astype(bf16)
    return jnp.concatenate([high, mid, low], axis=0)


def dot(a, b):
    return jnp.dot(a, b, preferred_element_type=f32)


def prepare_kernel(plan, initial, stiffness, record, springs):
    record[...] = jnp.zeros((1, PATCH), f32)
    for i in range(2):
        record[:, pl.ds((2 + i) * COLS, COLS)] = initial[0, i]
    level_id = lax.broadcasted_iota(jnp.int32, stiffness.shape, 1)
    for sweep in range(SWEEPS):
        picked = jnp.sum(jnp.where(level_id == plan[sweep], stiffness[...], 0.0), axis=1, keepdims=True)
        springs[pl.ds(2 * sweep, 2), :] = jnp.broadcast_to(picked, (2, PATCH))


def prepare(plan, initial, stiffness):
    in_vmem = pl.BlockSpec(memory_space=pltpu.VMEM)
    return pl.pallas_call(
        prepare_kernel,
        out_shape=[jax.ShapeDtypeStruct((1, PATCH), f32), jax.ShapeDtypeStruct((8, PATCH), f32)],
        in_specs=[pl.BlockSpec(memory_space=pltpu.SMEM), in_vmem, in_vmem],
        out_specs=[in_vmem] * 2,
        compiler_params=pltpu.CompilerParams(vmem_limit_bytes=VMEM_LIMIT),
        cost_estimate=pl.CostEstimate(flops=PREPARE_FLOPS, bytes_accessed=10_000, transcendentals=0),
    )(plan, initial, stiffness.T)


def section_spectra(upper, lower, tables):
    nyq_t = table(tables, "nyquist")
    nyq_t = jnp.concatenate([nyq_t[:, :PATCH], nyq_t[:, PATCH:]], axis=0)
    rows_t = jnp.concatenate([table(tables, "rows"), nyq_t], axis=1)
    columns = table(tables, "columns")
    lane = lax.broadcasted_iota(jnp.int32, (PATCH, PATCH), 1)
    nyquist = jnp.zeros((PATCH, PATCH), f32)
    stacked = []
    for m in range(PAIRS):
        span = 2 * PATCH if m < PAIRS - 1 else WIDTH - m * PATCH
        tile = jnp.concatenate([upper(m * PATCH, span), lower(m * PATCH, span)], axis=0)
        seg = dot(tile, rows_t[:span])
        nyquist = jnp.where(lane // 2 == m, seg[:, 2 * PATCH :], nyquist)
        seg = seg[:, : 2 * PATCH].astype(bf16)
        stacked.append(jnp.concatenate([seg[:, :PATCH], seg[:, PATCH:]], axis=0))
    spectra = []
    for m in range(0, PAIRS, 2):
        product = dot(columns, jnp.concatenate(stacked[m : m + 2], axis=1)).astype(bf16)
        spectra += [product[:, :PATCH], product[:, PATCH:]]
    spectra.append(dot(columns[:, :PATCH], nyquist.astype(bf16)).astype(bf16))
    return spectra


def energy(spectrum):
    wide = spectrum.astype(f32)
    return jnp.sum(wide * wide, axis=0, keepdims=True)


def block_tile(ref):
    return lambda start, span: ref[0, :, pl.ds(start, span)]


def own_kernel(own, below, tables, spec, energies):
    for m, spectrum in enumerate(section_spectra(block_tile(own), block_tile(below), tables)):
        spec[m] = spectrum
        energies[pl.ds(m, 1), :] = energy(spectrum)


def own_spectra(own, below, tables):
    in_vmem = pl.BlockSpec(memory_space=pltpu.VMEM)
    return pl.pallas_call(
        own_kernel,
        out_shape=[
            jax.ShapeDtypeStruct((PAIRS + 1, 2 * PATCH, PATCH), bf16),
            jax.ShapeDtypeStruct((2 * PAIRS, PATCH), f32),
        ],
        in_specs=[in_vmem] * 3,
        out_specs=[in_vmem] * 2,
        compiler_params=pltpu.CompilerParams(vmem_limit_bytes=VMEM_LIMIT),
        cost_estimate=pl.CostEstimate(flops=600_000_000, bytes_accessed=2_000_000, transcendentals=0),
    )(own, below, tables)


def flow_kernel(
    own_spec, own_energies, lower, near, near_below, record, shifts_in, tables, out, spec, lagged, shift_row
):
    spread = table(tables, "spread")
    energies = []

    def second(start, span):
        return near_below[0, :, pl.ds(start, span)] + lower[0, :, pl.ds(start, span)]

    for m, spectrum in enumerate(section_spectra(block_tile(near), second, tables)):
        spec[m] = spectrum
        energies.append(energy(spectrum))

    lane = lax.broadcasted_iota(jnp.int32, (PAIRS, PATCH), 1)
    pair = lax.broadcasted_iota(jnp.int32, (PAIRS, PATCH), 0)
    own_pair = (lane % COLS) // 2 == pair
    first_16 = own_pair & (lane < COLS)
    weight = jnp.where(lane % HALF == 0, 1.0, 2.0)

    def halves(x):
        return x[:, :PATCH], x[:, PATCH:]

    def totals(main, extra):
        left = jnp.concatenate([main * weight, jnp.where(first_16, extra, 0.0)], axis=1)
        found = dot(three_parts(left), spread)
        found = found[:PAIRS] + found[PAIRS : 2 * PAIRS] + found[2 * PAIRS :]
        by_pair, by_patch = halves(found)
        by_patch = jnp.sum(jnp.where(first_16, by_patch, 0.0), axis=0, keepdims=True) + extra
        scale = 1.0 / (PATCH * PATCH)
        return jnp.sqrt(by_pair * scale + 1e-06), jnp.sqrt(by_patch * scale + 1e-06)

    low_pair, low_patch = totals(jnp.concatenate(energies[:PAIRS], axis=0), energies[PAIRS])
    up_pair, up_patch = totals(own_energies[pl.ds(0, PAIRS), :], own_energies[pl.ds(PAIRS, 1), :])
    floor_pair = floor_ratio * low_pair * up_pair
    floor_patch = floor_ratio * low_patch * up_patch

    for m in range(PAIRS + 1):
        floor = floor_pair[m : m + 1] if m < PAIRS else floor_patch
        low_re = spec[m, pl.ds(0, PATCH)].astype(f32)
        low_im = spec[m, pl.ds(PATCH, PATCH)].astype(f32)
        up_re = own_spec[m, pl.ds(0, PATCH)].astype(f32)
        up_im = own_spec[m, pl.ds(PATCH, PATCH)].astype(f32)
        cross_re = low_re * up_re + low_im * up_im
        cross_im = low_re * up_im - low_im * up_re
        square = cross_re * cross_re + cross_im * cross_im
        modulus = square * lax.rsqrt(jnp.maximum(square, 1e-36))
        inverse = 1.0 / (modulus + floor)
        white = jnp.concatenate([cross_re * inverse, cross_im * inverse], axis=0)
        high = white.astype(bf16)
        low = (white - high.astype(f32)).astype(bf16)
        found = dot(table(tables, "lag_y"), jnp.concatenate([high, low], axis=1))
        part = found[: 2 * SHIFTS, :PATCH] + found[: 2 * SHIFTS, PATCH:] + found[2 * SHIFTS :, :PATCH]
        lagged[pl.ds(m * SHIFTS, SHIFTS), pl.ds(0, PATCH)] = part[:SHIFTS]
        lagged[pl.ds(m * SHIFTS, SHIFTS), pl.ds(PATCH, PATCH)] = part[SHIFTS:]

    extra = lagged[pl.ds(PAIRS * SHIFTS, SHIFTS), pl.ds(0, PATCH)]
    extra = jnp.where(first_16[:, None, :], extra[None], 0.0).reshape(PAIRS * SHIFTS, PATCH)
    left = jnp.concatenate([lagged[pl.ds(0, PAIRS * SHIFTS), :], extra], axis=1)
    high = left.astype(bf16)
    low = (left - high.astype(f32)).astype(bf16)
    rows_all = PAIRS * SHIFTS
    found = dot(jnp.concatenate([high, low], axis=0), table(tables, "lag_x"))
    surface = found[:rows_all, :PATCH] + found[:rows_all, PATCH:] + found[rows_all:, :PATCH]
    surface = surface.reshape(PAIRS, SHIFTS, PATCH)

    shift_row[...] = record[...]
    for i in range(2):
        shift_row[:, pl.ds(i * COLS, COLS)] = shifts_in[0, i].astype(f32)
    rec = shift_row[...]
    at_y = jnp.where(first_16, rec, 0.0)
    at_x = jnp.where(own_pair & (lane >= COLS) & (lane < 2 * COLS), rec, 0.0)
    gather = spread[:PATCH, PATCH:]
    shifts = lax.dot_general(
        jnp.concatenate([at_y, at_x], axis=0).astype(bf16),
        gather,
        (((1,), (1,)), ((), ())),
        preferred_element_type=f32,
    )
    lag_row = lax.broadcasted_iota(jnp.int32, (PAIRS, SHIFTS, PATCH), 1).astype(f32) - REACH
    lag_col = (lax.broadcasted_iota(jnp.int32, (PAIRS, SHIFTS, PATCH), 2) % HALF).astype(f32) - REACH
    dy = lag_row - shifts[:PAIRS][:, None, :]
    dx = lag_col - shifts[PAIRS:][:, None, :]
    mid_y, up_y, down_y = ((dy == k).astype(f32) for k in (0.0, 1.0, -1.0))
    mid_x, up_x, down_x = ((dx == k).astype(f32) for k in (0.0, 1.0, -1.0))
    at_mid_x = surface * mid_x
    at_mid_y = surface * mid_y
    picks = [
        jnp.sum(at_mid_x * (up_y - down_y), axis=1),
        jnp.sum(at_mid_x * (2.0 * mid_y - up_y - down_y), axis=1),
        jnp.sum(at_mid_y * (up_x - down_x), axis=1),
        jnp.sum(at_mid_y * (2.0 * mid_x - up_x - down_x), axis=1),
    ]
    found = dot(three_parts(jnp.concatenate(picks, axis=0)), gather)
    found = found[: 4 * PAIRS] + found[4 * PAIRS : 8 * PAIRS] + found[8 * PAIRS :]
    found = found.reshape(4, PAIRS, PATCH)
    found = jnp.sum(jnp.where(own_pair[None], found, 0.0), axis=1) * (1.0 / (PATCH * PATCH))
    lane_1 = lax.broadcasted_iota(jnp.int32, (1, PATCH), 1)
    slope = jnp.where(lane_1 < COLS, found[0:1], found[2:3])
    bend = jnp.where(lane_1 < COLS, found[1:2], found[3:4])
    flow = rec + 0.5 * slope / (1.0 + jnp.abs(bend))
    result = jnp.where(lane_1 < 2 * COLS, flow, rec)
    out[...] = jnp.broadcast_to(result, out.shape)


def pair_flow(own_parts, near, near_below, lower, record, offsets, tables, copies):
    operands = (*own_parts, lower, near, near_below, record, offsets, tables)
    return pl.pallas_call(
        flow_kernel,
        out_shape=jax.ShapeDtypeStruct((copies, PATCH), f32),
        in_specs=[pl.BlockSpec(memory_space=pltpu.VMEM)] * len(operands),
        out_specs=pl.BlockSpec(memory_space=pltpu.VMEM),
        scratch_shapes=[
            pltpu.VMEM((PAIRS + 1, 2 * PATCH, PATCH), bf16),
            pltpu.VMEM(((PAIRS + 1) * SHIFTS, 2 * PATCH), f32),
            pltpu.VMEM((1, PATCH), f32),
        ],
        compiler_params=pltpu.CompilerParams(vmem_limit_bytes=VMEM_LIMIT),
    )(*operands)


def relax_kernel(springs, ring, first_ring, second_ring, flow_out, moving_out):
    sec = lax.axis_index("sec")
    row = lax.axis_index("row")
    last_row = lax.axis_size("row") - 1
    place = lax.rem(row, RING)
    base = row - place
    count = SECS * RING
    node = lax.broadcasted_iota(jnp.int32, (count, PATCH), 0)
    lane = lax.broadcasted_iota(jnp.int32, (count, PATCH), 1)
    in_ring = node % RING
    section = node // RING
    other_first = jnp.broadcast_to(place, (count, PATCH)) < RING // 2
    valid = (section < SECS - 1) & (lane < 2 * COLS)
    valid_up = valid.astype(f32)
    has_left = (lane % COLS > 0).astype(f32)
    has_right = (lane % COLS < COLS - 1).astype(f32)
    row_here = base + in_ring
    row_other = row_here + jnp.where(other_first, -RING, RING)
    at_rows = (row_here, row_other)
    has_up = [(r > 0).astype(f32) for r in at_rows]
    has_down = [(r < last_row).astype(f32) for r in at_rows]
    first = in_ring == 0
    final = in_ring == RING - 1
    here = ring[...]
    odd = jnp.broadcast_to(lax.rem(row // RING, 2), (count, PATCH)) == 1
    inner = (jnp.broadcast_to(place, (count, PATCH)) > 0) & (jnp.broadcast_to(place, (count, PATCH)) < RING - 1)
    in_second = inner & (other_first == odd)
    beyond = jnp.where(in_second, second_ring[...], first_ring[...])
    far_side = jnp.where(in_second, first_ring[...], second_ring[...])
    moving = [pltpu.roll(b, PATCH - 2 * COLS, 1) for b in (here, beyond)]
    third = pltpu.roll(far_side, PATCH - 2 * COLS, 1)

    def moved(x, by):
        by = by % count
        return jnp.concatenate([x[by:], x[:by]], axis=0)

    flows = [jnp.where(valid, moved(b, RING), 0.0) for b in (here, beyond)]

    for sweep in range(SWEEPS):
        spring = springs[pl.ds(2 * sweep, 1), :]
        tether = springs[pl.ds(2 * sweep + 1, 1), :]
        near_x, far_x = moving
        edge_above = jnp.where(other_first, moved(far_x, RING - 1), moved(third, RING - 1))
        edge_below = jnp.where(other_first, moved(third, 1 - RING), moved(far_x, 1 - RING))
        above = (jnp.where(first, edge_above, moved(near_x, -1)), jnp.where(first, moved(near_x, RING - 1), moved(far_x, -1)))
        below = (jnp.where(final, edge_below, moved(near_x, 1)), jnp.where(final, moved(near_x, 1 - RING), moved(far_x, 1)))
        fresh = []
        for k, x in enumerate(moving):
            col_left = pltpu.roll(x, 1, 1)
            col_right = pltpu.roll(x, PATCH - 1, 1)
            laplace = (
                (above[k] - x) * has_up[k]
                + (below[k] - x) * has_down[k]
                + (col_left - x) * has_left
                + (col_right - x) * has_right
            )
            residual = (moved(x, RING) - x - flows[k]) * valid_up
            below_res = jnp.where(section == 0, 0.0, moved(residual, -RING))
            fresh.append(x + step_size * (spring * laplace + tether * (residual - below_res)))
        moving = fresh

    mine = (section == sec) & (in_ring == place)
    for x, ref in ((flows[0], flow_out), (moving[0], moving_out)):
        line = jnp.sum(jnp.where(mine, x, 0.0), axis=0, keepdims=True)
        ref[0, 0] = line[:, :COLS]
        ref[0, 1] = line[:, COLS : 2 * COLS]


def relax(springs, ring, first_ring, second_ring, shape):
    in_vmem = pl.BlockSpec(memory_space=pltpu.VMEM)
    return pl.pallas_call(
        relax_kernel,
        out_shape=[jax.ShapeDtypeStruct(shape, f32)] * 2,
        in_specs=[in_vmem] * 4,
        out_specs=[in_vmem] * 2,
        compiler_params=pltpu.CompilerParams(vmem_limit_bytes=VMEM_LIMIT),
    )(springs, ring, first_ring, second_ring)


def shifted(block, axis, distance):
    devices = range(lax.axis_size(axis))
    route = [(i - distance, i) for i in devices if i - distance in devices]
    return lax.ppermute(block, axis, route)


def ring_routes(rows):
    routes = ([], [])
    for r in range(rows):
        odd, place = r // RING % 2, r % RING
        inner = 0 < place < RING - 1
        if place < RING - 1 and r >= RING:
            routes[odd if inner else 0].append((r - RING, r))
        if place > 0 and r + RING < rows:
            routes[1 - odd if inner else 0].append((r + RING, r))
    return routes


def per_device(images, initial, offsets, stiffness, plan):
    rows = lax.axis_size("row")
    near = shifted(images, "sec", 1)
    at = lambda s, r: s * rows + r
    below = lax.ppermute(
        images, ("sec", "row"), [(at(s, r + 1), at(s, r)) for s in range(1, SECS) for r in range(rows - 1)]
    )
    lower = lax.ppermute(
        images, ("sec", "row"), [(at(s, r + 1), at(s + 1, r)) for s in range(2) for r in range(rows - 1)]
    )
    near_offsets = shifted(offsets, "sec", 1)
    record, springs = prepare(plan, initial, stiffness)
    below, near_offsets, record, springs = lax.optimization_barrier((below, near_offsets, record, springs))
    near_below = lax.ppermute(below, "sec", [(2, 3)])
    count = SECS * RING
    tables = jnp.asarray(constant_tables())
    own_parts = own_spectra(images, below, tables)
    mine = pair_flow(own_parts, near, near_below, lower, record, near_offsets, tables, count)
    groups = [
        [s * rows + RING * g + j for s in range(SECS) for j in range(RING)] for g in range(rows // RING)
    ]
    ring = lax.all_to_all(mine.reshape(count, 1, PATCH), ("sec", "row"), 0, 0, axis_index_groups=groups)
    blocks = [ring] + [lax.ppermute(ring, "row", route) for route in ring_routes(rows)]
    return tuple(relax(springs, *(block.reshape(count, PATCH) for block in blocks), initial.shape))


def solution(mesh):
    return jax.shard_map(
        per_device,
        mesh=mesh,
        in_specs=(
            P("sec", "row", None),
            P("sec", None, "row", None),
            P("sec", None, "row", None),
            P(),
            P(),
        ),
        out_specs=(P("sec", None, "row", None), P("sec", None, "row", None)),
        check_vma=False,
    )
```

```python
import math

import numpy as np
import jax
import jax.numpy as jnp
from jax import lax
from jax.experimental import pallas as pl
from jax.experimental.pallas import tpu as pltpu
from jax.sharding import PartitionSpec as P
import ml_dtypes

PATCH = 128
STRIDE = 64
HALF = 64
SWEEPS = 3
COLS = 16
PAIRS = 8
SECS = 4
RING = 4
SHIFTS = 16
REACH = 5
WIDTH = 1088

step_size = 0.2
floor_ratio = 0.2

VMEM_LIMIT = 24 * 1024 * 1024
PREPARE_FLOPS = 1_000_000_000

f32 = jnp.float32
bf16 = jnp.bfloat16


def dft_halves():
    freq = np.arange(PATCH)
    phase = freq[:, None] * freq[None, :] % PATCH
    folded = np.minimum(phase, PATCH - phase)
    angle = folded * (2.0 * math.pi / PATCH)
    sine = np.sin(angle) * np.where(2 * phase > PATCH, -1.0, 1.0)
    sine = np.where(2 * folded == PATCH, 0.0, sine)
    cosine = np.cos(angle)
    cosine = np.where(4 * folded == PATCH, np.cos(np.float32(math.pi / 2)), cosine)
    return cosine.astype(ml_dtypes.bfloat16), (-sine).astype(ml_dtypes.bfloat16)


def two_parts(table):
    high = table.astype(ml_dtypes.bfloat16)
    low = (table - high.astype(np.float64)).astype(ml_dtypes.bfloat16)
    return high, low


def constant_tables():
    cos_t, sin_t = dft_halves()
    cos_f = cos_t.astype(np.float32)
    sin_f = sin_t.astype(np.float32)
    rows = np.zeros((2 * PATCH, 2 * PATCH), np.float32)
    rows[0:PATCH, 0:HALF] = cos_f[:HALF].T
    rows[0:PATCH, PATCH : PATCH + HALF] = sin_f[:HALF].T
    rows[HALF : HALF + PATCH, HALF:PATCH] = cos_f[:HALF].T
    rows[HALF : HALF + PATCH, PATCH + HALF :] = sin_f[:HALF].T
    nyquist = np.zeros((2 * PATCH, PATCH), np.float32)
    nyquist[0:PATCH, 0::2] = cos_f[HALF][:, None]
    nyquist[HALF : HALF + PATCH, 1::2] = cos_f[HALF][:, None]
    columns = np.block([[cos_f, -sin_f], [sin_f, cos_f]])
    lags = np.arange(SHIFTS) - REACH
    used = (np.arange(SHIFTS) <= 2 * REACH).astype(np.float64)
    freq = np.arange(PATCH)
    turn = (freq[None, :] * lags[:, None] % PATCH) * (2.0 * math.pi / PATCH)
    cos_y = np.cos(turn) * used[:, None]
    sin_y = np.sin(turn) * used[:, None]
    high, low = two_parts(np.block([[cos_y, -sin_y], [sin_y, cos_y]]))
    lag_y = np.concatenate([high, low], axis=0)
    weight = np.where(freq[:HALF] == 0, 1.0, 2.0)
    across = np.zeros((3 * PATCH, PATCH))
    for p in range(2):
        cols = slice(p * HALF, p * HALF + SHIFTS)
        block = slice(p * HALF, (p + 1) * HALF)
        across[:PATCH][block, cols] = (cos_y[:, :HALF] * weight).T
        across[PATCH : 2 * PATCH][block, cols] = (-sin_y[:, :HALF] * weight).T
        for c in range(p, COLS, 2):
            across[2 * PATCH + c, cols] = np.where(lags % 2 == 0, 1.0, -1.0) * used
    high, low = two_parts(across)
    lag_x = np.concatenate([high, low], axis=1)
    lane = np.arange(PATCH)
    patch = (lane % COLS % 2)[None, :] == (lane // HALF)[:, None]
    gather = (patch & (lane < 2 * COLS)[None, :]).astype(np.float32)
    single = (patch & (lane < COLS)[None, :]).astype(np.float32)
    same = ((lane // HALF)[:, None] == (lane // HALF)[None, :]).astype(np.float32)
    blank = np.zeros((PATCH, PATCH), np.float32)
    spread = np.block([[same, gather], [single.T, blank]])
    packed = [rows, np.concatenate([nyquist[:PATCH], nyquist[PATCH:]], axis=1), columns, spread, lag_y, lag_x]
    return np.concatenate([np.asarray(t).astype(ml_dtypes.bfloat16) for t in packed], axis=0)


TABLE_ROWS = {"rows": (0, 256), "nyquist": (256, 128), "columns": (384, 256), "spread": (640, 256)}
TABLE_ROWS |= {"lag_y": (896, 64), "lag_x": (960, 384)}


def table(ref, name):
    start, length = TABLE_ROWS[name]
    return ref[pl.ds(start, length), :]


def three_parts(x):
    high = x.astype(bf16)
    rest = x - high.astype(f32)
    mid = rest.astype(bf16)
    low = (rest - mid.astype(f32)).astype(bf16)
    return jnp.concatenate([high, mid, low], axis=0)


def dot(a, b):
    return jnp.dot(a, b, preferred_element_type=f32)


def spring_kernel(plan, stiffness, springs):
    level_id = lax.broadcasted_iota(jnp.int32, stiffness.shape, 1)
    for sweep in range(SWEEPS):
        picked = jnp.sum(jnp.where(level_id == plan[sweep], stiffness[...], 0.0), axis=1, keepdims=True)
        springs[pl.ds(2 * sweep, 2), :] = jnp.broadcast_to(picked, (2, PATCH))


def spring_rows(plan, stiffness):
    in_vmem = pl.BlockSpec(memory_space=pltpu.VMEM)
    return pl.pallas_call(
        spring_kernel,
        out_shape=jax.ShapeDtypeStruct((8, PATCH), f32),
        in_specs=[pl.BlockSpec(memory_space=pltpu.SMEM), in_vmem],
        out_specs=in_vmem,
        compiler_params=pltpu.CompilerParams(vmem_limit_bytes=VMEM_LIMIT),
        cost_estimate=pl.CostEstimate(flops=PREPARE_FLOPS, bytes_accessed=10_000, transcendentals=0),
    )(plan, stiffness.T)


def section_spectra(upper, lower, tables):
    nyq_t = table(tables, "nyquist")
    nyq_t = jnp.concatenate([nyq_t[:, :PATCH], nyq_t[:, PATCH:]], axis=0)
    rows_t = jnp.concatenate([table(tables, "rows"), nyq_t], axis=1)
    columns = table(tables, "columns")
    lane = lax.broadcasted_iota(jnp.int32, (PATCH, PATCH), 1)
    nyquist = jnp.zeros((PATCH, PATCH), f32)
    stacked = []
    for m in range(PAIRS):
        span = 2 * PATCH if m < PAIRS - 1 else WIDTH - m * PATCH
        tile = jnp.concatenate([upper(m * PATCH, span), lower(m * PATCH, span)], axis=0)
        seg = dot(tile, rows_t[:span])
        nyquist = jnp.where(lane // 2 == m, seg[:, 2 * PATCH :], nyquist)
        seg = seg[:, : 2 * PATCH].astype(bf16)
        stacked.append(jnp.concatenate([seg[:, :PATCH], seg[:, PATCH:]], axis=0))
    spectra = []
    for m in range(0, PAIRS, 2):
        product = dot(columns, jnp.concatenate(stacked[m : m + 2], axis=1)).astype(bf16)
        spectra += [product[:, :PATCH], product[:, PATCH:]]
    spectra.append(dot(columns[:, :PATCH], nyquist.astype(bf16)).astype(bf16))
    return spectra


def energy(spectrum):
    wide = spectrum.astype(f32)
    return jnp.sum(wide * wide, axis=0, keepdims=True)


def block_tile(ref):
    return lambda start, span: ref[0, :, pl.ds(start, span)]


def own_kernel(own, below, initial, tables, spec, energies, record):
    record[...] = jnp.zeros((1, PATCH), f32)
    for i in range(2):
        record[:, pl.ds((2 + i) * COLS, COLS)] = initial[0, i]
    for m, spectrum in enumerate(section_spectra(block_tile(own), block_tile(below), tables)):
        spec[m] = spectrum
        energies[pl.ds(m, 1), :] = energy(spectrum)


def own_spectra(own, below, initial, tables):
    in_vmem = pl.BlockSpec(memory_space=pltpu.VMEM)
    return pl.pallas_call(
        own_kernel,
        out_shape=[
            jax.ShapeDtypeStruct((PAIRS + 1, 2 * PATCH, PATCH), bf16),
            jax.ShapeDtypeStruct((2 * PAIRS, PATCH), f32),
            jax.ShapeDtypeStruct((1, PATCH), f32),
        ],
        in_specs=[in_vmem] * 4,
        out_specs=[in_vmem] * 3,
        compiler_params=pltpu.CompilerParams(vmem_limit_bytes=VMEM_LIMIT),
        cost_estimate=pl.CostEstimate(flops=600_000_000, bytes_accessed=2_000_000, transcendentals=0),
    )(own, below, initial, tables)


def flow_kernel(
    own_spec, own_energies, record, lower, near, near_below, shifts_in, tables, out, spec, lagged, shift_row
):
    spread = table(tables, "spread")
    energies = []

    def second(start, span):
        return near_below[0, :, pl.ds(start, span)] + lower[0, :, pl.ds(start, span)]

    for m, spectrum in enumerate(section_spectra(block_tile(near), second, tables)):
        spec[m] = spectrum
        energies.append(energy(spectrum))

    lane = lax.broadcasted_iota(jnp.int32, (PAIRS, PATCH), 1)
    pair = lax.broadcasted_iota(jnp.int32, (PAIRS, PATCH), 0)
    own_pair = (lane % COLS) // 2 == pair
    first_16 = own_pair & (lane < COLS)
    weight = jnp.where(lane % HALF == 0, 1.0, 2.0)

    def halves(x):
        return x[:, :PATCH], x[:, PATCH:]

    def totals(main, extra):
        left = jnp.concatenate([main * weight, jnp.where(first_16, extra, 0.0)], axis=1)
        found = dot(three_parts(left), spread)
        found = found[:PAIRS] + found[PAIRS : 2 * PAIRS] + found[2 * PAIRS :]
        by_pair, by_patch = halves(found)
        by_patch = jnp.sum(jnp.where(first_16, by_patch, 0.0), axis=0, keepdims=True) + extra
        scale = 1.0 / (PATCH * PATCH)
        return jnp.sqrt(by_pair * scale + 1e-06), jnp.sqrt(by_patch * scale + 1e-06)

    low_pair, low_patch = totals(jnp.concatenate(energies[:PAIRS], axis=0), energies[PAIRS])
    up_pair, up_patch = totals(own_energies[pl.ds(0, PAIRS), :], own_energies[pl.ds(PAIRS, 1), :])
    floor_pair = floor_ratio * low_pair * up_pair
    floor_patch = floor_ratio * low_patch * up_patch

    for m in range(PAIRS + 1):
        floor = floor_pair[m : m + 1] if m < PAIRS else floor_patch
        low_re = spec[m, pl.ds(0, PATCH)].astype(f32)
        low_im = spec[m, pl.ds(PATCH, PATCH)].astype(f32)
        up_re = own_spec[m, pl.ds(0, PATCH)].astype(f32)
        up_im = own_spec[m, pl.ds(PATCH, PATCH)].astype(f32)
        cross_re = low_re * up_re + low_im * up_im
        cross_im = low_re * up_im - low_im * up_re
        square = cross_re * cross_re + cross_im * cross_im
        modulus = square * lax.rsqrt(jnp.maximum(square, 1e-36))
        inverse = 1.0 / (modulus + floor)
        white = jnp.concatenate([cross_re * inverse, cross_im * inverse], axis=0)
        found = dot(table(tables, "lag_y"), white.astype(bf16))
        part = found[: 2 * SHIFTS] + found[2 * SHIFTS :]
        lagged[pl.ds(m * SHIFTS, SHIFTS), pl.ds(0, PATCH)] = part[:SHIFTS]
        lagged[pl.ds(m * SHIFTS, SHIFTS), pl.ds(PATCH, PATCH)] = part[SHIFTS:]

    extra = lagged[pl.ds(PAIRS * SHIFTS, SHIFTS), pl.ds(0, PATCH)]
    extra = jnp.where(first_16[:, None, :], extra[None], 0.0).reshape(PAIRS * SHIFTS, PATCH)
    left = jnp.concatenate([lagged[pl.ds(0, PAIRS * SHIFTS), :], extra], axis=1)
    high = left.astype(bf16)
    low = (left - high.astype(f32)).astype(bf16)
    rows_all = PAIRS * SHIFTS
    found = dot(jnp.concatenate([high, low], axis=0), table(tables, "lag_x"))
    surface = found[:rows_all, :PATCH] + found[:rows_all, PATCH:] + found[rows_all:, :PATCH]
    surface = surface.reshape(PAIRS, SHIFTS, PATCH)

    shift_row[...] = record[...]
    for i in range(2):
        shift_row[:, pl.ds(i * COLS, COLS)] = shifts_in[0, i].astype(f32)
    rec = shift_row[...]
    at_y = jnp.where(first_16, rec, 0.0)
    at_x = jnp.where(own_pair & (lane >= COLS) & (lane < 2 * COLS), rec, 0.0)
    gather = spread[:PATCH, PATCH:]
    shifts = lax.dot_general(
        jnp.concatenate([at_y, at_x], axis=0).astype(bf16),
        gather,
        (((1,), (1,)), ((), ())),
        preferred_element_type=f32,
    )
    lag_row = lax.broadcasted_iota(jnp.int32, (PAIRS, SHIFTS, PATCH), 1).astype(f32) - REACH
    lag_col = (lax.broadcasted_iota(jnp.int32, (PAIRS, SHIFTS, PATCH), 2) % HALF).astype(f32) - REACH
    dy = lag_row - shifts[:PAIRS][:, None, :]
    dx = lag_col - shifts[PAIRS:][:, None, :]
    mid_y, up_y, down_y = ((dy == k).astype(f32) for k in (0.0, 1.0, -1.0))
    mid_x, up_x, down_x = ((dx == k).astype(f32) for k in (0.0, 1.0, -1.0))
    at_mid_x = surface * mid_x
    at_mid_y = surface * mid_y
    picks = [
        jnp.sum(at_mid_x * (up_y - down_y), axis=1),
        jnp.sum(at_mid_x * (2.0 * mid_y - up_y - down_y), axis=1),
        jnp.sum(at_mid_y * (up_x - down_x), axis=1),
        jnp.sum(at_mid_y * (2.0 * mid_x - up_x - down_x), axis=1),
    ]
    found = dot(three_parts(jnp.concatenate(picks, axis=0)), gather)
    found = found[: 4 * PAIRS] + found[4 * PAIRS : 8 * PAIRS] + found[8 * PAIRS :]
    found = found.reshape(4, PAIRS, PATCH)
    found = jnp.sum(jnp.where(own_pair[None], found, 0.0), axis=1) * (1.0 / (PATCH * PATCH))
    lane_1 = lax.broadcasted_iota(jnp.int32, (1, PATCH), 1)
    slope = jnp.where(lane_1 < COLS, found[0:1], found[2:3])
    bend = jnp.where(lane_1 < COLS, found[1:2], found[3:4])
    flow = rec + 0.5 * slope / (1.0 + jnp.abs(bend))
    result = jnp.where(lane_1 < 2 * COLS, flow, rec)
    out[...] = jnp.broadcast_to(result, out.shape)


def pair_flow(own_parts, near, near_below, lower, offsets, tables, copies):
    operands = (*own_parts, lower, near, near_below, offsets, tables)
    return pl.pallas_call(
        flow_kernel,
        out_shape=jax.ShapeDtypeStruct((copies, PATCH), f32),
        in_specs=[pl.BlockSpec(memory_space=pltpu.VMEM)] * len(operands),
        out_specs=pl.BlockSpec(memory_space=pltpu.VMEM),
        scratch_shapes=[
            pltpu.VMEM((PAIRS + 1, 2 * PATCH, PATCH), bf16),
            pltpu.VMEM(((PAIRS + 1) * SHIFTS, 2 * PATCH), f32),
            pltpu.VMEM((1, PATCH), f32),
        ],
        compiler_params=pltpu.CompilerParams(vmem_limit_bytes=VMEM_LIMIT),
    )(*operands)


def relax_kernel(springs, ring, first_ring, second_ring, flow_out, moving_out):
    sec = lax.axis_index("sec")
    row = lax.axis_index("row")
    last_row = lax.axis_size("row") - 1
    place = lax.rem(row, RING)
    base = row - place
    count = SECS * RING
    node = lax.broadcasted_iota(jnp.int32, (count, PATCH), 0)
    lane = lax.broadcasted_iota(jnp.int32, (count, PATCH), 1)
    in_ring = node % RING
    section = node // RING
    other_first = jnp.broadcast_to(place, (count, PATCH)) < RING // 2
    valid = (section < SECS - 1) & (lane < 2 * COLS)
    valid_up = valid.astype(f32)
    has_left = (lane % COLS > 0).astype(f32)
    has_right = (lane % COLS < COLS - 1).astype(f32)
    row_here = base + in_ring
    row_other = row_here + jnp.where(other_first, -RING, RING)
    at_rows = (row_here, row_other)
    has_up = [(r > 0).astype(f32) for r in at_rows]
    has_down = [(r < last_row).astype(f32) for r in at_rows]
    first = in_ring == 0
    final = in_ring == RING - 1
    here = ring[...]
    odd = jnp.broadcast_to(lax.rem(row // RING, 2), (count, PATCH)) == 1
    inner = (jnp.broadcast_to(place, (count, PATCH)) > 0) & (jnp.broadcast_to(place, (count, PATCH)) < RING - 1)
    in_second = inner & (other_first == odd)
    beyond = jnp.where(in_second, second_ring[...], first_ring[...])
    far_side = jnp.where(in_second, first_ring[...], second_ring[...])
    moving = [pltpu.roll(b, PATCH - 2 * COLS, 1) for b in (here, beyond)]
    third = pltpu.roll(far_side, PATCH - 2 * COLS, 1)

    def moved(x, by):
        by = by % count
        return jnp.concatenate([x[by:], x[:by]], axis=0)

    flows = [jnp.where(valid, moved(b, RING), 0.0) for b in (here, beyond)]

    for sweep in range(SWEEPS):
        spring = springs[pl.ds(2 * sweep, 1), :]
        tether = springs[pl.ds(2 * sweep + 1, 1), :]
        near_x, far_x = moving
        edge_above = jnp.where(other_first, moved(far_x, RING - 1), moved(third, RING - 1))
        edge_below = jnp.where(other_first, moved(third, 1 - RING), moved(far_x, 1 - RING))
        above = (jnp.where(first, edge_above, moved(near_x, -1)), jnp.where(first, moved(near_x, RING - 1), moved(far_x, -1)))
        below = (jnp.where(final, edge_below, moved(near_x, 1)), jnp.where(final, moved(near_x, 1 - RING), moved(far_x, 1)))
        fresh = []
        for k, x in enumerate(moving):
            col_left = pltpu.roll(x, 1, 1)
            col_right = pltpu.roll(x, PATCH - 1, 1)
            laplace = (
                (above[k] - x) * has_up[k]
                + (below[k] - x) * has_down[k]
                + (col_left - x) * has_left
                + (col_right - x) * has_right
            )
            residual = (moved(x, RING) - x - flows[k]) * valid_up
            below_res = jnp.where(section == 0, 0.0, moved(residual, -RING))
            fresh.append(x + step_size * (spring * laplace + tether * (residual - below_res)))
        moving = fresh

    mine = (section == sec) & (in_ring == place)
    for x, ref in ((flows[0], flow_out), (moving[0], moving_out)):
        line = jnp.sum(jnp.where(mine, x, 0.0), axis=0, keepdims=True)
        ref[0, 0] = line[:, :COLS]
        ref[0, 1] = line[:, COLS : 2 * COLS]


def relax(springs, ring, first_ring, second_ring, shape):
    in_vmem = pl.BlockSpec(memory_space=pltpu.VMEM)
    return pl.pallas_call(
        relax_kernel,
        out_shape=[jax.ShapeDtypeStruct(shape, f32)] * 2,
        in_specs=[in_vmem] * 4,
        out_specs=[in_vmem] * 2,
        compiler_params=pltpu.CompilerParams(vmem_limit_bytes=VMEM_LIMIT),
    )(springs, ring, first_ring, second_ring)


def shifted(block, axis, distance):
    devices = range(lax.axis_size(axis))
    route = [(i - distance, i) for i in devices if i - distance in devices]
    return lax.ppermute(block, axis, route)


def ring_routes(rows):
    routes = ([], [])
    for r in range(rows):
        odd, place = r // RING % 2, r % RING
        inner = 0 < place < RING - 1
        if place < RING - 1 and r >= RING:
            routes[odd if inner else 0].append((r - RING, r))
        if place > 0 and r + RING < rows:
            routes[1 - odd if inner else 0].append((r + RING, r))
    return routes


def per_device(images, initial, offsets, stiffness, plan):
    rows = lax.axis_size("row")
    near = shifted(images, "sec", 1)
    at = lambda s, r: s * rows + r
    below = lax.ppermute(
        images, ("sec", "row"), [(at(s, r + 1), at(s, r)) for s in range(1, SECS) for r in range(rows - 1)]
    )
    lower = lax.ppermute(
        images, ("sec", "row"), [(at(s, r + 1), at(s + 1, r)) for s in range(2) for r in range(rows - 1)]
    )
    near_offsets = shifted(offsets, "sec", 1)
    springs = spring_rows(plan, stiffness)
    below, near_offsets, springs = lax.optimization_barrier((below, near_offsets, springs))
    near_below = lax.ppermute(below, "sec", [(2, 3)])
    count = SECS * RING
    tables = jnp.asarray(constant_tables())
    own_parts = own_spectra(images, below, initial, tables)
    mine = pair_flow(own_parts, near, near_below, lower, near_offsets, tables, count)
    groups = [
        [s * rows + RING * g + j for s in range(SECS) for j in range(RING)] for g in range(rows // RING)
    ]
    ring = lax.all_to_all(mine.reshape(count, 1, PATCH), ("sec", "row"), 0, 0, axis_index_groups=groups)
    blocks = [ring] + [lax.ppermute(ring, "row", route) for route in ring_routes(rows)]
    return tuple(relax(springs, *(block.reshape(count, PATCH) for block in blocks), initial.shape))


def solution(mesh):
    return jax.shard_map(
        per_device,
        mesh=mesh,
        in_specs=(
            P("sec", "row", None),
            P("sec", None, "row", None),
            P("sec", None, "row", None),
            P(),
            P(),
        ),
        out_specs=(P("sec", None, "row", None), P("sec", None, "row", None)),
        check_vma=False,
    )
```

```python
import math

import numpy as np
import jax
import jax.numpy as jnp
from jax import lax
from jax.experimental import pallas as pl
from jax.experimental.pallas import tpu as pltpu
from jax.sharding import PartitionSpec as P
import ml_dtypes

PATCH = 128
STRIDE = 64
HALF = 64
SWEEPS = 3
COLS = 16
PAIRS = 8
SECS = 4
RING = 4
SHIFTS = 16
REACH = 5
WIDTH = 1088

step_size = 0.2
floor_ratio = 0.2

VMEM_LIMIT = 24 * 1024 * 1024
PREPARE_FLOPS = 1_000_000_000

f32 = jnp.float32
bf16 = jnp.bfloat16


def dft_halves():
    freq = np.arange(PATCH)
    phase = freq[:, None] * freq[None, :] % PATCH
    folded = np.minimum(phase, PATCH - phase)
    angle = folded * (2.0 * math.pi / PATCH)
    sine = np.sin(angle) * np.where(2 * phase > PATCH, -1.0, 1.0)
    sine = np.where(2 * folded == PATCH, 0.0, sine)
    cosine = np.cos(angle)
    cosine = np.where(4 * folded == PATCH, np.cos(np.float32(math.pi / 2)), cosine)
    return cosine.astype(ml_dtypes.bfloat16), (-sine).astype(ml_dtypes.bfloat16)


def two_parts(table):
    high = table.astype(ml_dtypes.bfloat16)
    low = (table - high.astype(np.float64)).astype(ml_dtypes.bfloat16)
    return high, low


def constant_tables():
    cos_t, sin_t = dft_halves()
    cos_f = cos_t.astype(np.float32)
    sin_f = sin_t.astype(np.float32)
    rows = np.zeros((2 * PATCH, 2 * PATCH), np.float32)
    rows[0:PATCH, 0:HALF] = cos_f[:HALF].T
    rows[0:PATCH, PATCH : PATCH + HALF] = sin_f[:HALF].T
    rows[HALF : HALF + PATCH, HALF:PATCH] = cos_f[:HALF].T
    rows[HALF : HALF + PATCH, PATCH + HALF :] = sin_f[:HALF].T
    nyquist = np.zeros((2 * PATCH, PATCH), np.float32)
    nyquist[0:PATCH, 0::2] = cos_f[HALF][:, None]
    nyquist[HALF : HALF + PATCH, 1::2] = cos_f[HALF][:, None]
    columns = np.block([[cos_f, -sin_f], [sin_f, cos_f]])
    lags = np.arange(SHIFTS) - REACH
    used = (np.arange(SHIFTS) <= 2 * REACH).astype(np.float64)
    freq = np.arange(PATCH)
    turn = (freq[None, :] * lags[:, None] % PATCH) * (2.0 * math.pi / PATCH)
    cos_y = np.cos(turn) * used[:, None]
    sin_y = np.sin(turn) * used[:, None]
    high, low = two_parts(np.block([[cos_y, -sin_y], [sin_y, cos_y]]))
    lag_y = np.concatenate([high, low], axis=0)
    weight = np.where(freq[:HALF] == 0, 1.0, 2.0)
    across = np.zeros((3 * PATCH, PATCH))
    for p in range(2):
        cols = slice(p * HALF, p * HALF + SHIFTS)
        block = slice(p * HALF, (p + 1) * HALF)
        across[:PATCH][block, cols] = (cos_y[:, :HALF] * weight).T
        across[PATCH : 2 * PATCH][block, cols] = (-sin_y[:, :HALF] * weight).T
        for c in range(p, COLS, 2):
            across[2 * PATCH + c, cols] = np.where(lags % 2 == 0, 1.0, -1.0) * used
    high, low = two_parts(across)
    lag_x = np.concatenate([high, low], axis=1)
    lane = np.arange(PATCH)
    patch = (lane % COLS % 2)[None, :] == (lane // HALF)[:, None]
    gather = (patch & (lane < 2 * COLS)[None, :]).astype(np.float32)
    single = (patch & (lane < COLS)[None, :]).astype(np.float32)
    same = ((lane // HALF)[:, None] == (lane // HALF)[None, :]).astype(np.float32)
    blank = np.zeros((PATCH, PATCH), np.float32)
    spread = np.block([[same, gather], [single.T, blank]])
    packed = [rows, np.concatenate([nyquist[:PATCH], nyquist[PATCH:]], axis=1), columns, spread, lag_y, lag_x]
    return np.concatenate([np.asarray(t).astype(ml_dtypes.bfloat16) for t in packed], axis=0)


TABLE_ROWS = {"rows": (0, 256), "nyquist": (256, 128), "columns": (384, 256), "spread": (640, 256)}
TABLE_ROWS |= {"lag_y": (896, 64), "lag_x": (960, 384)}


def table(ref, name):
    start, length = TABLE_ROWS[name]
    return ref[pl.ds(start, length), :]


def three_parts(x):
    high = x.astype(bf16)
    rest = x - high.astype(f32)
    mid = rest.astype(bf16)
    low = (rest - mid.astype(f32)).astype(bf16)
    return jnp.concatenate([high, mid, low], axis=0)


def dot(a, b):
    return jnp.dot(a, b, preferred_element_type=f32)


def spring_kernel(plan, stiffness, springs):
    level_id = lax.broadcasted_iota(jnp.int32, stiffness.shape, 1)
    for sweep in range(SWEEPS):
        picked = jnp.sum(jnp.where(level_id == plan[sweep], stiffness[...], 0.0), axis=1, keepdims=True)
        springs[pl.ds(2 * sweep, 2), :] = jnp.broadcast_to(picked, (2, PATCH))


def spring_rows(plan, stiffness):
    in_vmem = pl.BlockSpec(memory_space=pltpu.VMEM)
    return pl.pallas_call(
        spring_kernel,
        out_shape=jax.ShapeDtypeStruct((8, PATCH), f32),
        in_specs=[pl.BlockSpec(memory_space=pltpu.SMEM), in_vmem],
        out_specs=in_vmem,
        compiler_params=pltpu.CompilerParams(vmem_limit_bytes=VMEM_LIMIT),
        cost_estimate=pl.CostEstimate(flops=PREPARE_FLOPS, bytes_accessed=10_000, transcendentals=0),
    )(plan, stiffness.T)


def section_spectra(upper, lower, tables):
    nyq_t = table(tables, "nyquist")
    nyq_t = jnp.concatenate([nyq_t[:, :PATCH], nyq_t[:, PATCH:]], axis=0)
    rows_t = jnp.concatenate([table(tables, "rows"), nyq_t], axis=1)
    columns = table(tables, "columns")
    lane = lax.broadcasted_iota(jnp.int32, (PATCH, PATCH), 1)
    nyquist = jnp.zeros((PATCH, PATCH), f32)
    stacked = []
    for m in range(PAIRS):
        span = 2 * PATCH if m < PAIRS - 1 else WIDTH - m * PATCH
        tile = jnp.concatenate([upper(m * PATCH, span), lower(m * PATCH, span)], axis=0)
        seg = dot(tile, rows_t[:span])
        nyquist = jnp.where(lane // 2 == m, seg[:, 2 * PATCH :], nyquist)
        seg = seg[:, : 2 * PATCH].astype(bf16)
        stacked.append(jnp.concatenate([seg[:, :PATCH], seg[:, PATCH:]], axis=0))
    spectra = []
    for m in range(0, PAIRS, 2):
        product = dot(columns, jnp.concatenate(stacked[m : m + 2], axis=1)).astype(bf16)
        spectra += [product[:, :PATCH], product[:, PATCH:]]
    spectra.append(dot(columns[:, :PATCH], nyquist.astype(bf16)).astype(bf16))
    return spectra


def energy(spectrum):
    wide = spectrum.astype(f32)
    return jnp.sum(wide * wide, axis=0, keepdims=True)


def block_tile(ref):
    return lambda start, span: ref[0, :, pl.ds(start, span)]


def own_kernel(own, below, initial, tables, spec, energies, record):
    record[...] = jnp.zeros((1, PATCH), f32)
    for i in range(2):
        record[:, pl.ds((2 + i) * COLS, COLS)] = initial[0, i]
    for m, spectrum in enumerate(section_spectra(block_tile(own), block_tile(below), tables)):
        spec[m] = spectrum
        energies[pl.ds(m, 1), :] = energy(spectrum)


def own_spectra(own, below, initial, tables):
    in_vmem = pl.BlockSpec(memory_space=pltpu.VMEM)
    return pl.pallas_call(
        own_kernel,
        out_shape=[
            jax.ShapeDtypeStruct((PAIRS + 1, 2 * PATCH, PATCH), bf16),
            jax.ShapeDtypeStruct((2 * PAIRS, PATCH), f32),
            jax.ShapeDtypeStruct((1, PATCH), f32),
        ],
        in_specs=[in_vmem] * 4,
        out_specs=[in_vmem] * 3,
        compiler_params=pltpu.CompilerParams(vmem_limit_bytes=VMEM_LIMIT),
        cost_estimate=pl.CostEstimate(flops=600_000_000, bytes_accessed=2_000_000, transcendentals=0),
    )(own, below, initial, tables)


def flow_kernel(
    own_spec, own_energies, record, lower, near, near_below, shifts_in, tables, out, spec, lagged, shift_row
):
    spread = table(tables, "spread")
    energies = []

    def second(start, span):
        return near_below[0, :, pl.ds(start, span)] + lower[0, :, pl.ds(start, span)]

    for m, spectrum in enumerate(section_spectra(block_tile(near), second, tables)):
        spec[m] = spectrum
        energies.append(energy(spectrum))

    lane = lax.broadcasted_iota(jnp.int32, (PAIRS, PATCH), 1)
    pair = lax.broadcasted_iota(jnp.int32, (PAIRS, PATCH), 0)
    own_pair = (lane % COLS) // 2 == pair
    first_16 = own_pair & (lane < COLS)
    weight = jnp.where(lane % HALF == 0, 1.0, 2.0)

    def halves(x):
        return x[:, :PATCH], x[:, PATCH:]

    def totals(main, extra):
        left = jnp.concatenate([main * weight, jnp.where(first_16, extra, 0.0)], axis=1)
        found = dot(three_parts(left), spread)
        found = found[:PAIRS] + found[PAIRS : 2 * PAIRS] + found[2 * PAIRS :]
        by_pair, by_patch = halves(found)
        by_patch = jnp.sum(jnp.where(first_16, by_patch, 0.0), axis=0, keepdims=True) + extra
        scale = 1.0 / (PATCH * PATCH)
        return jnp.sqrt(by_pair * scale + 1e-06), jnp.sqrt(by_patch * scale + 1e-06)

    low_pair, low_patch = totals(jnp.concatenate(energies[:PAIRS], axis=0), energies[PAIRS])
    up_pair, up_patch = totals(own_energies[pl.ds(0, PAIRS), :], own_energies[pl.ds(PAIRS, 1), :])
    floor_pair = floor_ratio * low_pair * up_pair
    floor_patch = floor_ratio * low_patch * up_patch

    for m in range(PAIRS + 1):
        floor = floor_pair[m : m + 1] if m < PAIRS else floor_patch
        low_re = spec[m, pl.ds(0, PATCH)].astype(f32)
        low_im = spec[m, pl.ds(PATCH, PATCH)].astype(f32)
        up_re = own_spec[m, pl.ds(0, PATCH)].astype(f32)
        up_im = own_spec[m, pl.ds(PATCH, PATCH)].astype(f32)
        cross_re = low_re * up_re + low_im * up_im
        cross_im = low_re * up_im - low_im * up_re
        square = cross_re * cross_re + cross_im * cross_im
        modulus = square * lax.rsqrt(jnp.maximum(square, 1e-36))
        inverse = 1.0 / (modulus + floor)
        white = jnp.concatenate([cross_re * inverse, cross_im * inverse], axis=0)
        found = dot(table(tables, "lag_y"), white.astype(bf16))
        part = found[: 2 * SHIFTS] + found[2 * SHIFTS :]
        lagged[pl.ds(m * SHIFTS, SHIFTS), pl.ds(0, PATCH)] = part[:SHIFTS]
        lagged[pl.ds(m * SHIFTS, SHIFTS), pl.ds(PATCH, PATCH)] = part[SHIFTS:]

    extra = lagged[pl.ds(PAIRS * SHIFTS, SHIFTS), pl.ds(0, PATCH)]
    extra = jnp.where(first_16[:, None, :], extra[None], 0.0).reshape(PAIRS * SHIFTS, PATCH)
    left = jnp.concatenate([lagged[pl.ds(0, PAIRS * SHIFTS), :], extra], axis=1)
    high = left.astype(bf16)
    low = (left - high.astype(f32)).astype(bf16)
    rows_all = PAIRS * SHIFTS
    found = dot(jnp.concatenate([high, low], axis=0), table(tables, "lag_x"))
    surface = found[:rows_all, :PATCH] + found[:rows_all, PATCH:] + found[rows_all:, :PATCH]
    surface = surface.reshape(PAIRS, SHIFTS, PATCH)

    shift_row[...] = record[...]
    for i in range(2):
        shift_row[:, pl.ds(i * COLS, COLS)] = shifts_in[0, i].astype(f32)
    rec = shift_row[...]
    at_y = jnp.where(first_16, rec, 0.0)
    at_x = jnp.where(own_pair & (lane >= COLS) & (lane < 2 * COLS), rec, 0.0)
    gather = spread[:PATCH, PATCH:]
    shifts = lax.dot_general(
        jnp.concatenate([at_y, at_x], axis=0).astype(bf16),
        gather,
        (((1,), (1,)), ((), ())),
        preferred_element_type=f32,
    )
    lag_row = lax.broadcasted_iota(jnp.int32, (PAIRS, SHIFTS, PATCH), 1).astype(f32) - REACH
    lag_col = (lax.broadcasted_iota(jnp.int32, (PAIRS, SHIFTS, PATCH), 2) % HALF).astype(f32) - REACH
    dy = lag_row - shifts[:PAIRS][:, None, :]
    dx = lag_col - shifts[PAIRS:][:, None, :]
    mid_y, up_y, down_y = ((dy == k).astype(f32) for k in (0.0, 1.0, -1.0))
    mid_x, up_x, down_x = ((dx == k).astype(f32) for k in (0.0, 1.0, -1.0))
    at_mid_x = surface * mid_x
    at_mid_y = surface * mid_y
    picks = [
        jnp.sum(at_mid_x * (up_y - down_y), axis=1),
        jnp.sum(at_mid_x * (2.0 * mid_y - up_y - down_y), axis=1),
        jnp.sum(at_mid_y * (up_x - down_x), axis=1),
        jnp.sum(at_mid_y * (2.0 * mid_x - up_x - down_x), axis=1),
    ]
    found = dot(three_parts(jnp.concatenate(picks, axis=0)), gather)
    found = found[: 4 * PAIRS] + found[4 * PAIRS : 8 * PAIRS] + found[8 * PAIRS :]
    found = found.reshape(4, PAIRS, PATCH)
    found = jnp.sum(jnp.where(own_pair[None], found, 0.0), axis=1) * (1.0 / (PATCH * PATCH))
    lane_1 = lax.broadcasted_iota(jnp.int32, (1, PATCH), 1)
    slope = jnp.where(lane_1 < COLS, found[0:1], found[2:3])
    bend = jnp.where(lane_1 < COLS, found[1:2], found[3:4])
    flow = rec + 0.5 * slope / (1.0 + jnp.abs(bend))
    result = jnp.where(lane_1 < 2 * COLS, flow, rec)
    out[...] = jnp.broadcast_to(result, out.shape)


def pair_flow(own_parts, near, near_below, lower, offsets, tables, copies):
    operands = (*own_parts, lower, near, near_below, offsets, tables)
    return pl.pallas_call(
        flow_kernel,
        out_shape=jax.ShapeDtypeStruct((copies, PATCH), f32),
        in_specs=[pl.BlockSpec(memory_space=pltpu.VMEM)] * len(operands),
        out_specs=pl.BlockSpec(memory_space=pltpu.VMEM),
        scratch_shapes=[
            pltpu.VMEM((PAIRS + 1, 2 * PATCH, PATCH), bf16),
            pltpu.VMEM(((PAIRS + 1) * SHIFTS, 2 * PATCH), f32),
            pltpu.VMEM((1, PATCH), f32),
        ],
        compiler_params=pltpu.CompilerParams(vmem_limit_bytes=VMEM_LIMIT),
    )(*operands)


def relax_kernel(springs, ring, first_ring, second_ring, flow_out, moving_out):
    sec = lax.axis_index("sec")
    row = lax.axis_index("row")
    last_row = lax.axis_size("row") - 1
    place = lax.rem(row, RING)
    base = row - place
    count = SECS * RING
    node = lax.broadcasted_iota(jnp.int32, (count, PATCH), 0)
    lane = lax.broadcasted_iota(jnp.int32, (count, PATCH), 1)
    in_ring = node % RING
    section = node // RING
    other_first = jnp.broadcast_to(place, (count, PATCH)) < RING // 2
    valid = (section < SECS - 1) & (lane < 2 * COLS)
    valid_up = valid.astype(f32)
    has_left = (lane % COLS > 0).astype(f32)
    has_right = (lane % COLS < COLS - 1).astype(f32)
    row_here = base + in_ring
    row_other = row_here + jnp.where(other_first, -RING, RING)
    at_rows = (row_here, row_other)
    has_up = [(r > 0).astype(f32) for r in at_rows]
    has_down = [(r < last_row).astype(f32) for r in at_rows]
    first = in_ring == 0
    final = in_ring == RING - 1
    here = ring[...]
    odd = jnp.broadcast_to(lax.rem(row // RING, 2), (count, PATCH)) == 1
    inner = (jnp.broadcast_to(place, (count, PATCH)) > 0) & (jnp.broadcast_to(place, (count, PATCH)) < RING - 1)
    in_second = inner & (other_first == odd)
    beyond = jnp.where(in_second, second_ring[...], first_ring[...])
    far_side = jnp.where(in_second, first_ring[...], second_ring[...])
    moving = [pltpu.roll(b, PATCH - 2 * COLS, 1) for b in (here, beyond)]
    third = pltpu.roll(far_side, PATCH - 2 * COLS, 1)

    def moved(x, by):
        by = by % count
        return jnp.concatenate([x[by:], x[:by]], axis=0)

    flows = [jnp.where(valid, moved(b, RING), 0.0) for b in (here, beyond)]

    for sweep in range(SWEEPS):
        spring = springs[pl.ds(2 * sweep, 1), :]
        tether = springs[pl.ds(2 * sweep + 1, 1), :]
        near_x, far_x = moving
        edge_above = jnp.where(other_first, moved(far_x, RING - 1), moved(third, RING - 1))
        edge_below = jnp.where(other_first, moved(third, 1 - RING), moved(far_x, 1 - RING))
        above = (jnp.where(first, edge_above, moved(near_x, -1)), jnp.where(first, moved(near_x, RING - 1), moved(far_x, -1)))
        below = (jnp.where(final, edge_below, moved(near_x, 1)), jnp.where(final, moved(near_x, 1 - RING), moved(far_x, 1)))
        fresh = []
        for k, x in enumerate(moving):
            col_left = pltpu.roll(x, 1, 1)
            col_right = pltpu.roll(x, PATCH - 1, 1)
            laplace = (
                (above[k] - x) * has_up[k]
                + (below[k] - x) * has_down[k]
                + (col_left - x) * has_left
                + (col_right - x) * has_right
            )
            residual = (moved(x, RING) - x - flows[k]) * valid_up
            below_res = jnp.where(section == 0, 0.0, moved(residual, -RING))
            fresh.append(x + step_size * (spring * laplace + tether * (residual - below_res)))
        moving = fresh

    mine = (section == sec) & (in_ring == place)
    for x, ref in ((flows[0], flow_out), (moving[0], moving_out)):
        line = jnp.sum(jnp.where(mine, x, 0.0), axis=0, keepdims=True)
        ref[0, 0] = line[:, :COLS]
        ref[0, 1] = line[:, COLS : 2 * COLS]


def relax(springs, ring, first_ring, second_ring, shape):
    in_vmem = pl.BlockSpec(memory_space=pltpu.VMEM)
    return pl.pallas_call(
        relax_kernel,
        out_shape=[jax.ShapeDtypeStruct(shape, f32)] * 2,
        in_specs=[in_vmem] * 4,
        out_specs=[in_vmem] * 2,
        compiler_params=pltpu.CompilerParams(vmem_limit_bytes=VMEM_LIMIT),
    )(springs, ring, first_ring, second_ring)


def shifted(block, axis, distance):
    devices = range(lax.axis_size(axis))
    route = [(i - distance, i) for i in devices if i - distance in devices]
    return lax.ppermute(block, axis, route)


def ring_routes(rows):
    routes = ([], [])
    for r in range(rows):
        odd, place = r // RING % 2, r % RING
        inner = 0 < place < RING - 1
        if place < RING - 1 and r >= RING:
            routes[odd if inner else 0].append((r - RING, r))
        if place > 0 and r + RING < rows:
            routes[1 - odd if inner else 0].append((r + RING, r))
    return routes


def per_device(images, initial, offsets, stiffness, plan):
    rows = lax.axis_size("row")
    near = shifted(images, "sec", 1)
    at = lambda s, r: s * rows + r
    below = lax.ppermute(
        images, ("sec", "row"), [(at(s, r + 1), at(s, r)) for s in range(1, SECS) for r in range(rows - 1)]
    )
    lower = lax.ppermute(
        images, ("sec", "row"), [(at(s, r + 1), at(s + 1, r)) for s in range(2) for r in range(rows - 1)]
    )
    near_offsets = shifted(offsets, "sec", 1)
    springs = spring_rows(plan, stiffness)
    count = SECS * RING
    tables = jnp.asarray(constant_tables())
    spec, energies, record = own_spectra(images, below, initial, tables)
    sent_on, near_offsets, springs, record = lax.optimization_barrier((below, near_offsets, springs, record))
    near_below = lax.ppermute(sent_on, "sec", [(2, 3)])
    mine = pair_flow((spec, energies, record), near, near_below, lower, near_offsets, tables, count)
    groups = [
        [s * rows + RING * g + j for s in range(SECS) for j in range(RING)] for g in range(rows // RING)
    ]
    ring = lax.all_to_all(mine.reshape(count, 1, PATCH), ("sec", "row"), 0, 0, axis_index_groups=groups)
    blocks = [ring] + [lax.ppermute(ring, "row", route) for route in ring_routes(rows)]
    return tuple(relax(springs, *(block.reshape(count, PATCH) for block in blocks), initial.shape))


def solution(mesh):
    return jax.shard_map(
        per_device,
        mesh=mesh,
        in_specs=(
            P("sec", "row", None),
            P("sec", None, "row", None),
            P("sec", None, "row", None),
            P(),
            P(),
        ),
        out_specs=(P("sec", None, "row", None), P("sec", None, "row", None)),
        check_vma=False,
    )
```
